128 devices in a mesh: expert: 16 (over z, y), fsdp: 8 (over x, core).
Axes of the slice: x: 4, y: 4, z: 4, core: 2. Of those that a mesh axis runs over, the one named last changes fastest.
Arguments:
- tokens: bfloat16 [2, 8, 2048, 1024], P(None, 'fsdp', 'expert'), may hold values from -6 to 6
- cotangent: bfloat16 [2, 8, 2048, 1024], P(None, 'fsdp', 'expert'), may hold values from -6 to 6
- doc_lengths: int32 [2, 8, 3], P(None, 'fsdp'), may hold values from 1 to 2046, as said below
- routes: int32 [2, 8, 2048, 2], P(None, 'fsdp', 'expert'), may hold values from 0 to 15, all different within a row
- order: int32 [2, 8, 16, 256], P(None, 'fsdp', 'expert'), may hold values from 0 to 255, each once within a row
- gain_attn: bfloat16 [1024], P(('expert', 'fsdp')), may hold values from 0.5 to 1.5
- w_query: bfloat16 [1024, 1024], P(('expert', 'fsdp')), may hold values from -0.1875 to 0.1875
- w_key: bfloat16 [1024, 1024], P(('expert', 'fsdp')), may hold values from -0.1875 to 0.1875
- w_value: bfloat16 [1024, 1024], P(('expert', 'fsdp')), may hold values from -0.1875 to 0.1875
- w_out: bfloat16 [1024, 1024], P(('expert', 'fsdp')), may hold values from -1 to 1
- rel_table: bfloat16 [512], P(('expert', 'fsdp')), may hold values from -3 to 3
- gain_moe: bfloat16 [1024], P(('expert', 'fsdp')), may hold values from 0.5 to 1.5
- w_router: bfloat16 [1024, 16], P(('expert', 'fsdp')), may hold values from -0.125 to 0.125
- w_gate: bfloat16 [16, 1024, 2816], P('expert', None, 'fsdp'), may hold values from -0.1875 to 0.1875
- w_up: bfloat16 [16, 1024, 2816], P('expert', None, 'fsdp'), may hold values from -0.1875 to 0.1875
- w_down: bfloat16 [16, 2816, 1024], P('expert', 'fsdp'), may hold values from -0.15625 to 0.15625
Outputs:
- output: bfloat16 [2, 8, 2048, 1024], P(None, 'fsdp', 'expert')
- input_grad: bfloat16 [2, 8, 2048, 1024], P(None, 'fsdp', 'expert')
- grad_gain_attn: float32 [1024], P(('expert', 'fsdp'))
- grad_query: float32 [1024, 1024], P(('expert', 'fsdp'))
- grad_key: float32 [1024, 1024], P(('expert', 'fsdp'))
- grad_value: float32 [1024, 1024], P(('expert', 'fsdp'))
- grad_out: float32 [1024, 1024], P(('expert', 'fsdp'))
- grad_table: float32 [512], P(('expert', 'fsdp'))
- grad_gain_moe: float32 [1024], P(('expert', 'fsdp'))
- grad_router: float32 [1024, 16], P(('expert', 'fsdp'))
- grad_gate: float32 [16, 1024, 2816], P('expert', None, 'fsdp')
- grad_up: float32 [16, 1024, 2816], P('expert', None, 'fsdp')
- grad_down: float32 [16, 2816, 1024], P('expert', 'fsdp')
The draws below stay inside these ranges and needn't reach their ends.
Inputs may be any that keep to these rules, and one draw needn't show every extreme that they name: `doc_lengths`: in each sequence the first and last documents are shorter than 128 tokens and the middle one holds the rest; in some sequence the first and last documents hold one token each. The two routes of a token differ. Each block's slots in an order of precedence, each number once.
All inputs are finite; a program needn't handle non-finite values.
Results may differ from the reference program's by a relative error of at most 0.035.
Values may be sent and summed in bfloat16 or wider, within the bound.
A program may use at most 256 MiB of HBM per device.

```python
import math
import jax
import jax.numpy as jnp
from jax import lax

D = 1024
H = 16
HD = 64
FF = 2816
NB = 32
WINDOW = 1024
MICRO = 2
SG = 1
EXPERTS = 16
SHARDS = 8
SPANS = 16
SEQ = 2048
SEQS = 8
TS = 128
ROWS = 128
SLOTS = 256
CAP = 20


def draw_doc_lengths(key, part):
    key = jax.random.fold_in(key, 7)
    lead_key, trailing_key_rows, pick_key = jax.random.split(key, 3)
    leading = jax.random.randint(lead_key, (MICRO, SEQS, 1), 1, TS)
    trailing = jax.random.randint(trailing_key_rows, (MICRO, SEQS, 1), 1, TS)
    chosen = jax.random.randint(pick_key, (), 0, MICRO * SEQS)
    flat_ids = jnp.arange(MICRO * SEQS, dtype=jnp.int32).reshape(MICRO, SEQS, 1)
    pinned = flat_ids == chosen
    leading = jnp.where(pinned, 1, leading)
    trailing = jnp.where(pinned, 1, trailing)
    middle = SEQ - leading - trailing
    return jnp.concatenate([leading, middle, trailing], axis=-1).astype(jnp.int32)


def level_of(key, shape, pieces, low, largest):
    gain = 1.0
    for axis_at, shards_of in pieces:
        draws = jax.random.uniform(jax.random.fold_in(jax.random.fold_in(key, 6), axis_at), (shards_of,), jnp.float32, low / len(pieces), largest / len(pieces))
        gain = gain * jnp.repeat(jnp.exp(draws), shape[axis_at] // shards_of).reshape((-1,) + (1,) * (len(shape) - 1 - axis_at))
    return gain


def choose_distinct(rng, rows, amount, top, lift):
    sequence = jax.random.permutation(jax.random.fold_in(rng, 1), amount)
    boost = sequence
    for power in range(3):
        boost = boost * boost // amount
    boost = boost * lift // amount
    tickets = jax.random.randint(jax.random.fold_in(rng, 2), (rows, amount), 0, 4096) + boost
    sure = jax.random.permutation(jax.random.fold_in(rng, 3), rows)[jnp.arange(amount) % rows]
    tickets = jnp.where(jnp.arange(rows)[:, None] == sure[None, :], 1 << 14, tickets)
    merit = tickets * amount + jnp.arange(amount)
    return lax.top_k(merit.astype(jnp.int32), top)[1].astype(jnp.int32)


def scatter_about(stream_key, dims, width, most, shards=(), held_as=jnp.bfloat16):
    drawn = width * jax.random.normal(stream_key, dims, jnp.float32)
    if shards:
        drawn = drawn * level_of(stream_key, dims, shards, -0.22, 0.18)
    return jnp.clip(drawn, -most, most).astype(held_as)


def setup_inputs(seed: int = 0) -> dict:
    keys = jax.random.split(jax.random.key(seed), 17)
    return {
        "tokens": scatter_about(keys[0], (MICRO, SEQS, SEQ, D), 1.0, 6.0, ((1, 8), (2, 16))),
        "cotangent": scatter_about(keys[1], (MICRO, SEQS, SEQ, D), 1.0, 6.0, ((1, 8), (2, 16))),
        "doc_lengths": draw_doc_lengths(jax.random.fold_in(keys[16], 71), 0),
        "routes": choose_distinct(keys[3], MICRO * SEQS * SEQ, EXPERTS, 2, 2048).reshape((MICRO, SEQS, SEQ, 2)),
        "order": jax.vmap(lambda own: jax.random.permutation(own, SLOTS))(jax.random.split(keys[4], MICRO * SHARDS * SPANS)).reshape((MICRO, SHARDS, SPANS, SLOTS)).astype(jnp.int32),
        "gain_attn": jnp.clip(1.0 + 0.1 * jax.random.normal(keys[5], (D,), jnp.float32), 0.5, 1.5).astype(jnp.bfloat16),
        "w_query": scatter_about(keys[6], (D, D), D ** -0.5, 0.1875, ((0, 128),)),
        "w_key": scatter_about(keys[7], (D, D), D ** -0.5, 0.1875, ((0, 128),)),
        "w_value": scatter_about(keys[8], (D, D), D ** -0.5, 0.1875, ((0, 128),)),
        "w_out": scatter_about(keys[9], (D, D), (D // 32) ** -0.5, 1.0, ((0, 128),)),
        "rel_table": scatter_about(keys[10], (H * NB,), 0.5, 3.0, ((0, 128),)),
        "gain_moe": jnp.clip(1.0 + 0.1 * jax.random.normal(keys[11], (D,), jnp.float32), 0.5, 1.5).astype(jnp.bfloat16),
        "w_router": scatter_about(keys[12], (D, EXPERTS), (2 * D) ** -0.5, 0.125, ((0, 128),)),
        "w_gate": scatter_about(keys[13], (EXPERTS, D, FF), D ** -0.5, 0.1875, ((0, 16), (2, 8))),
        "w_up": scatter_about(keys[14], (EXPERTS, D, FF), D ** -0.5, 0.1875, ((0, 16), (2, 8))),
        "w_down": scatter_about(keys[15], (EXPERTS, FF, D), (FF // 2) ** -0.5, 0.15625, ((0, 16), (1, 8))),
    }


EPS = 1e-06
MASKED = -1e+30
THRESHOLDS = (19, 21, 24, 27, 31, 35, 40, 46, 52, 59, 67, 77, 87, 99, 113)

@jax.custom_vjp
def low(v):
    return lax.optimization_barrier(v.astype(jnp.bfloat16)).astype(jnp.float32)

@jax.custom_vjp
def low_back(v):
    return v

def low_keep(v):
    return (low(v), None)

def low_pass(kept, grad):
    return (grad,)

def back_keep(v):
    return (v, None)

def back_low(kept, grad):
    return (low(grad),)
low.defvjp(low_keep, low_pass)
low_back.defvjp(back_keep, back_low)

def matmul(left, right):
    return jnp.dot(left, right, precision=lax.Precision.HIGHEST)

def rms_norm(values, gain_vec):
    factor = lax.rsqrt(lax.optimization_barrier(jnp.mean(values * values, axis=-1, keepdims=True)) + EPS)
    return values * factor * gain_vec

def buckets(distance):
    beyond = 16 + sum(((distance >= boundary).astype(jnp.int32) for boundary in THRESHOLDS))
    return jnp.where(distance < 16, distance, beyond).astype(jnp.int32)

def document_index(lengths, position):
    first_end = lengths[..., 0:1]
    second_end = first_end + lengths[..., 1:2]
    return (position >= first_end).astype(jnp.int32) + (position >= second_end).astype(jnp.int32)

def attend_block(block_item, key_rows, value_rows, lengths, position_bias_lookup):
    query_rows, block_start = block_item
    block_rows = query_rows.shape[0]
    seq_len = key_rows.shape[0]
    query_pos = block_start + jnp.arange(block_rows, dtype=jnp.int32)
    key_pos = jnp.arange(seq_len, dtype=jnp.int32)
    distance = query_pos[:, None] - key_pos[None, :]
    same_doc = document_index(lengths, query_pos)[:, None] == document_index(lengths, key_pos)[None, :]
    allowed = same_doc & (distance >= 0) & (distance < WINDOW)
    relative_offset_bias = position_bias_lookup[:, buckets(jnp.clip(distance, 0, seq_len))]
    head_q = query_rows.reshape(block_rows, H, HD)
    head_k = key_rows.reshape(seq_len, H, HD)
    head_v = value_rows.reshape(seq_len, H, HD)
    scores = jnp.einsum('qhd,khd->hqk', head_q, head_k, precision=lax.Precision.HIGHEST) * HD ** (-0.5) + relative_offset_bias
    scores = jnp.where(allowed[None], low_back(scores), MASKED)
    top_score = lax.optimization_barrier(jnp.max(scores, axis=-1, keepdims=True))
    exponent = jnp.exp(scores - top_score)
    attn_probs = exponent / lax.optimization_barrier(jnp.sum(exponent, axis=-1, keepdims=True))
    mixed_heads = jnp.einsum('hqk,khd->qhd', low(attn_probs), head_v, precision=lax.Precision.HIGHEST)
    return mixed_heads.reshape(block_rows, D)

def attend_sequence(queries, key_rows, value_rows, lengths, position_bias_lookup):
    block_rows = math.gcd(SEQ, 512)
    block_count = SEQ // block_rows
    starts = jnp.arange(block_count, dtype=jnp.int32) * block_rows

    def per_block(block_item):
        return attend_block(block_item, key_rows, value_rows, lengths, position_bias_lookup)
    mixed = lax.map(jax.checkpoint(per_block), (queries.reshape(block_count, block_rows, D), starts))
    return mixed.reshape(SEQ, D)

def run_expert(expert_item):
    rows_in, gate_w, up_w, down_w = expert_item
    gate_pre = low_back(matmul(rows_in, gate_w))
    up_pre = low_back(matmul(rows_in, up_w))
    activated = low(low_back(jax.nn.gelu(gate_pre, approximate=True) * up_pre))
    return low(low_back(matmul(activated, down_w)))

def device_order(values_in):
    trailing = values_in.shape[2:]
    shaped = values_in.reshape((SHARDS, SG, SPANS, TS) + trailing)
    return jnp.swapaxes(shaped, 1, 2).reshape((SHARDS, SPANS, ROWS) + trailing)

def forward(hidden_in, params, lengths, routes_now, order_now):
    gain_attn, w_query, w_key, w_value, w_out, rel_table, gain_moe, w_router, w_gate, w_up, w_down = params
    position_bias_lookup = rel_table.reshape(H, NB)
    flat_in = hidden_in.reshape(SEQS * SEQ, D)
    normed = low(rms_norm(flat_in, gain_attn))
    queries = low(low_back(matmul(normed, w_query))).reshape(SEQS, SEQ, D)
    key_rows = low(low_back(matmul(normed, w_key))).reshape(SEQS, SEQ, D)
    value_rows = low(low_back(matmul(normed, w_value))).reshape(SEQS, SEQ, D)

    def per_sequence(sequence_item):
        return attend_sequence(sequence_item[0], sequence_item[1], sequence_item[2], sequence_item[3], position_bias_lookup)
    attended = lax.map(jax.checkpoint(per_sequence), (queries, key_rows, value_rows, lengths))
    attended = low(low_back(attended.reshape(SEQS * SEQ, D)))
    branch = low_back(matmul(attended, w_out))
    hidden = flat_in + branch
    mixed_rows = low(rms_norm(hidden, gain_moe))
    chance = jax.nn.softmax(matmul(mixed_rows, w_router), axis=-1)
    mixed_dev = device_order(mixed_rows.reshape(SEQS, SEQ, D))
    chance_dev = device_order(chance.reshape(SEQS, SEQ, EXPERTS))
    routes_dev = device_order(routes_now)
    chosen = jnp.take_along_axis(chance_dev, routes_dev, axis=-1)
    gate_share = chosen / lax.optimization_barrier(jnp.sum(chosen, axis=-1, keepdims=True))
    slot_expert = routes_dev.reshape(SHARDS, SPANS, SLOTS)
    precedence = order_now.reshape(SHARDS, SPANS, SLOTS)
    same_expert = slot_expert[..., :, None] == slot_expert[..., None, :]
    earlier = precedence[..., None, :] < precedence[..., :, None]
    slot_rank = lax.optimization_barrier(jnp.sum((same_expert & earlier).astype(jnp.int32), axis=-1))
    kept_mask = slot_rank < CAP
    shard_pos = jnp.arange(SHARDS, dtype=jnp.int32)[:, None, None]
    span_pos = jnp.arange(SPANS, dtype=jnp.int32)[None, :, None]
    total_slots = EXPERTS * SHARDS * SPANS * CAP
    target = ((slot_expert * SHARDS + shard_pos) * SPANS + span_pos) * CAP + slot_rank
    target = jnp.where(kept_mask, target, total_slots).reshape(-1).astype(jnp.int32)
    slot_rows = low_back(jnp.repeat(mixed_dev, 2, axis=2).reshape(-1, D))
    buffer = jnp.zeros((total_slots + 1, D), jnp.float32).at[target].set(slot_rows)
    buffer = buffer[:total_slots].reshape(EXPERTS, SHARDS * SPANS * CAP, D)
    expert_out = lax.map(jax.checkpoint(run_expert), (buffer, w_gate, w_up, w_down))
    returned = expert_out.reshape(total_slots, D)[jnp.minimum(target, total_slots - 1)]
    returned = returned * kept_mask.reshape(-1, 1).astype(jnp.float32)
    combined = lax.optimization_barrier(jnp.sum(returned.reshape(SHARDS, SPANS, ROWS, 2, D) * gate_share[..., None], axis=3))
    moe_out = jnp.swapaxes(combined.reshape(SHARDS, SPANS, SG, TS, D), 1, 2).reshape(SEQS * SEQ, D)
    return (hidden + moe_out).reshape(SEQS, SEQ, D)

def reference(tokens, cotangent, doc_lengths, routes, order, gain_attn, w_query, w_key, w_value, w_out, rel_table, gain_moe, w_router, w_gate, w_up, w_down):
    weights = tuple((item.astype(jnp.float32) for item in (gain_attn, w_query, w_key, w_value, w_out, rel_table, gain_moe, w_router, w_gate, w_up, w_down)))
    totals = tuple((jnp.zeros_like(item) for item in weights))
    results = []
    inputs_grad = []
    for micro_step in range(MICRO):
        lengths = doc_lengths[micro_step]
        routes_now = routes[micro_step]
        order_now = order[micro_step]

        def layer(hidden_in, params):
            return forward(hidden_in, params, lengths, routes_now, order_now)
        result, pullback = jax.vjp(layer, tokens[micro_step].astype(jnp.float32), weights)
        grad_in, grad_params = pullback(cotangent[micro_step].astype(jnp.float32))
        results.append(result.astype(jnp.bfloat16))
        inputs_grad.append(grad_in.astype(jnp.bfloat16))
        totals = tuple((left_val + right_val for left_val, right_val in zip(totals, grad_params)))
    return (jnp.stack(results), jnp.stack(inputs_grad), totals[0], totals[1], totals[2], totals[3], totals[4], totals[5], totals[6], totals[7], totals[8], totals[9], totals[10])
```

```python
import jax
import jax.numpy as jnp
from jax import lax
from jax.experimental import pallas as pl
from jax.experimental.pallas import tpu as pltpu
from jax.sharding import PartitionSpec as P

H = 16
HD = 64
NB = 32
D = 1024
FF = 2816
WINDOW = 1024
EXPERTS = 16
CAP = 20
TS = 128
FSDP = 8
SHARD = FF // FSDP
TOK = 2 * TS
BUF = EXPERTS * 2 * CAP
SEQ = EXPERTS * TS
EPS = 1e-06
MASKED = -1e30
EDGES = tuple(range(1, 17)) + (19, 21, 24, 27, 31, 35, 40, 46, 52, 59, 67, 77, 87, 99, 113)
GELU_C = 0.7978845608028654
BF = jnp.bfloat16
F32 = jnp.float32
VMEM_LIMIT = 58 * 1024 * 1024


def nn(left, right):
    return lax.dot_general(left, right, (((1,), (0,)), ((), ())), preferred_element_type=F32)


def nt(left, right):
    return lax.dot_general(left, right, (((1,), (1,)), ((), ())), preferred_element_type=F32)


def tn(left, right):
    return lax.dot_general(left, right, (((0,), (0,)), ((), ())), preferred_element_type=F32)


def halves(value):
    high = value.astype(BF)
    return high, (value - high.astype(F32)).astype(BF)


def call(kernel, out_shape, *args, scratch=(), in_specs=None, **kw):
    return pl.pallas_call(
        kernel,
        out_shape=out_shape,
        in_specs=in_specs or [pl.BlockSpec(memory_space=pltpu.VMEM)] * len(args),
        out_specs=jax.tree.map(lambda _: pl.BlockSpec(memory_space=pltpu.VMEM), out_shape),
        scratch_shapes=list(scratch),
        compiler_params=pltpu.CompilerParams(vmem_limit_bytes=VMEM_LIMIT),
        **kw,
    )(*args)


def shape(dims, dtype):
    return jax.ShapeDtypeStruct(dims, dtype)


def lane_half(dims):
    return lax.broadcasted_iota(jnp.int32, dims, 1) % 128 < HD


def pack_pair(first, second):
    left = lane_half(first.shape)
    return (
        jnp.where(left, first, pltpu.roll(second, HD, 1)).astype(BF),
        jnp.where(left, pltpu.roll(first, HD, 1), second).astype(BF),
    )


def qkv_kernel(x_ref, gain_ref, wq_ref, wk_ref, wv_ref, normed_ref, out_ref):
    x = x_ref[...].astype(F32)
    factor = lax.rsqrt(jnp.mean(x * x, axis=-1, keepdims=True) + EPS)
    normed = (x * factor * gain_ref[...]).astype(BF)
    normed_ref[...] = normed
    for which, w_ref in enumerate((wq_ref, wk_ref, wv_ref)):
        for part in range(4):
            res = nn(normed, w_ref[:, part * 256 : (part + 1) * 256])
            for pair in range(2):
                head = part * 4 + pair * 2
                cols = slice(pair * 128, pair * 128 + 128)
                one, two = pack_pair(res[:TS, cols], res[TS:, cols])
                out_ref[head, which * TS : (which + 1) * TS, :] = one
                out_ref[head + 1, which * TS : (which + 1) * TS, :] = two


def attn_setup(len_ref, tab_ref, recv_ref, kext, qext, bias):
    rows = lax.broadcasted_iota(jnp.int32, (SEQ, 128), 0)
    lanes = lax.broadcasted_iota(jnp.int32, (SEQ, 128), 1)
    end1 = [len_ref[m, 0] for m in range(2)]
    end2 = [len_ref[m, 0] + len_ref[m, 1] for m in range(2)]
    kfeat = jnp.where(lanes == 4, 1.0, 0.0)
    for m in range(2):
        kfeat = jnp.where((lanes == 2 * m) & (rows < end1[m]), 1.0, kfeat)
        kfeat = jnp.where((lanes == 2 * m + 1) & (rows < end2[m]), 1.0, kfeat)
    kext[:, 128:] = kfeat.astype(BF)
    for i in range(EXPERTS):
        kext[i * TS : (i + 1) * TS, :128] = recv_ref[i, TS : 2 * TS, :]
    left = lane_half((TS, 128))
    row_in = lax.broadcasted_iota(jnp.int32, (TS, 128), 0)
    lane_in = lax.broadcasted_iota(jnp.int32, (TS, 128), 1)
    for i in range(EXPERTS):
        q2 = recv_ref[i, 0:TS, :].astype(F32) * (HD**-0.5)
        pos = row_in + i * TS
        for m in range(2):
            keep = left if m == 0 else jnp.logical_not(left)
            qext[i, m * TS : (m + 1) * TS, :128] = jnp.where(keep, q2, 0.0).astype(BF)
            feat = jnp.where((lane_in == 2 * m) & (pos >= end1[m]), MASKED, 0.0)
            feat = jnp.where((lane_in == 2 * m + 1) & (pos >= end2[m]), MASKED, feat)
            qext[i, m * TS : (m + 1) * TS, 128:] = feat.astype(BF)
    for block in range(12):
        dist = 1024 - block * TS + lane_in - row_in
        if block in (7, 8):
            value = jnp.full((TS, 128), tab_ref[0, 0], F32)
            for bucket, edge in enumerate(EDGES):
                value = jnp.where(dist >= edge, tab_ref[0, bucket + 1], value)
        else:
            value = jnp.full((TS, 128), tab_ref[0, NB - 1], F32)
        value = jnp.where((dist >= 0) & (dist < WINDOW), value, MASKED)
        bias[block * TS : (block + 1) * TS, :128] = value
        bias[block * TS : (block + 1) * TS, 128:] = value


def eye(size):
    return (
        lax.broadcasted_iota(jnp.int32, (size, size), 0)
        == lax.broadcasted_iota(jnp.int32, (size, size), 1)
    ).astype(BF)


def strip_loops(strip):
    def early(i, carry):
        strip(i, 4, 0)
        return carry

    def middle(i, carry):
        strip(i, 8, 0)
        return carry

    def late(i, carry):
        strip(i, 9, i - 8)
        return carry

    lax.fori_loop(0, 4, early, 0)
    lax.fori_loop(4, 8, middle, 0)
    lax.fori_loop(8, 16, late, 0)


def span(block, count):
    return pl.ds(pl.multiple_of(block * TS, TS), count * TS)


def attn_fwd_kernel(len_ref, tab_ref, recv_ref, out_ref, lse_ref, kext, qext, bias, vt):
    attn_setup(len_ref, tab_ref, recv_ref, kext, qext, bias)
    unit = eye(TS)
    for i in range(EXPERTS):
        vt[:, i * TS : (i + 1) * TS] = nt(unit, recv_ref[i, 2 * TS : 3 * TS, :]).astype(BF)

    def strip(i, count, first):
        s = nt(kext[span(first, count), :], qext[i]) + bias[span(first - i + 8, count), :]
        top = jnp.max(s, axis=0, keepdims=True)
        p = jnp.exp(s - top)
        total = jnp.sum(p, axis=0, keepdims=True)
        res = nn(vt[:, span(first, count)], p.astype(BF)) / total
        both = jnp.concatenate([res[:HD, :TS], res[HD:, TS:]], axis=0)
        out_ref[i] = both.T.astype(BF)
        lse_ref[i] = jnp.broadcast_to(top + jnp.log(total), (8, TOK))

    strip_loops(strip)


def attn_bwd_kernel(
    len_ref, tab_ref, recv_ref, dout_ref, lse_ref, out_ref, tab_out_ref, kext, qext, bias, ktext, dk, dv, near, far
):
    attn_setup(len_ref, tab_ref, recv_ref, kext, qext, bias)
    unit = eye(256)
    for i in range(EXPERTS):
        ktext[:, i * TS : (i + 1) * TS] = nt(unit, kext[i * TS : (i + 1) * TS, :])[:144].astype(BF)
    dk[...] = jnp.zeros_like(dk)
    dv[...] = jnp.zeros_like(dv)
    near[...] = jnp.zeros_like(near)
    far[...] = jnp.zeros_like(far)
    left = lane_half((TS, 128))

    def strip(i, count, first):
        q = qext[i]
        s = nt(kext[span(first, count), :], q) + bias[span(first - i + 8, count), :]
        p = jnp.exp(s - lse_ref[i][0:1])
        do2 = dout_ref[i]
        zero = jnp.zeros_like(do2)
        do = jnp.concatenate([jnp.where(left, do2, zero), jnp.where(left, zero, do2)], axis=0)
        if count == 9:
            v = recv_ref[pl.ds(first, count), 2 * TS : 3 * TS, :].reshape(count * TS, 128)
        else:
            v = recv_ref[0:count, 2 * TS : 3 * TS, :].reshape(count * TS, 128)
        dp = nt(v, do)
        inner = jnp.sum(p * dp, axis=0, keepdims=True)
        ds = (p * (dp - inner)).astype(BF)
        dv[span(first, count), :] += nn(p.astype(BF), do)
        dk[span(first, count), :] += nn(ds, q[:, :128])
        dqt = nn(ktext[:, span(first, count)], ds)
        both = jnp.concatenate([dqt[:HD, :TS], dqt[HD : 2 * HD, TS:]], axis=0) * (HD**-0.5)
        out_ref[i, 0:TS, :] = both.T.astype(BF)
        far[...] += dqt[128:136]
        if count == 9:
            near[...] += ds[7 * TS :].astype(F32)
        else:
            nearby.append(ds)

    nearby = []

    def loop(low, high, count):
        def body(i, carry):
            nearby.clear()
            first = i - 8 if count == 9 else 0
            strip(i, count, first)
            if count != 9:
                ds = nearby[0]
                for block in range(count):
                    value = ds[block * TS : (block + 1) * TS].astype(F32)

                    @pl.when(i == block)
                    def _(value=value):
                        near[TS:] += value

                    @pl.when(i == block + 1)
                    def _(value=value):
                        near[:TS] += value

            return carry

        lax.fori_loop(low, high, body, 0)

    loop(0, 4, 4)
    loop(4, 8, 8)
    loop(8, 16, 9)
    for i in range(EXPERTS):
        out_ref[i, TS : 2 * TS, :] = dk[i * TS : (i + 1) * TS, :].astype(BF)
        out_ref[i, 2 * TS :, :] = dv[i * TS : (i + 1) * TS, :].astype(BF)
    grads = near[:, :TS] + near[:, TS:]
    dist = (
        TS
        + lax.broadcasted_iota(jnp.int32, (TOK, TS), 1)
        - lax.broadcasted_iota(jnp.int32, (TOK, TS), 0)
    )
    total = jnp.sum(far[4:5, :])
    lane = lax.broadcasted_iota(jnp.int32, (8, 128), 1)
    res = jnp.zeros((8, 128), F32)
    lows = (0,) + EDGES
    seen = 0.0
    for b in range(NB - 1):
        part = jnp.sum(jnp.where((dist >= lows[b]) & (dist < lows[b + 1]), grads, 0.0))
        seen = seen + part
        res = jnp.where(lane == b, part, res)
    res = jnp.where(lane == NB - 1, total - seen, res)
    tab_out_ref[...] = res


def row_expert():
    row = lax.broadcasted_iota(jnp.int32, (BUF, 128), 0)
    lane = lax.broadcasted_iota(jnp.int32, (BUF, 128), 1) * (2 * CAP)
    return (row >= lane) & (row < lane + 2 * CAP)


def unpack_heads(recv_ref, lo, emit):
    for pair in range(H // 2):
        one = recv_ref[2 * pair, lo : lo + TS, :].astype(F32)
        two = recv_ref[2 * pair + 1, lo : lo + TS, :].astype(F32)
        first, second = pack_pair(one, two)
        emit(pair, first, second)


def slot_share(place, share_e, own):
    high, low = halves(share_e)
    return jnp.sum(jnp.where(own, nn(place, high) + nn(place, low), 0.0), axis=1, keepdims=True)


def mid_kernel(
    recv_ref, x_ref, wo_ref, gain_ref, wr_ref, mask_ref, place_ref, dy_ref,
    att_ref, hidden_ref, mixed_ref, share_ref, send_ref,
):
    def emit(pair, first, second):
        att_ref[0:TS, pair * 128 : pair * 128 + 128] = first
        att_ref[TS:, pair * 128 : pair * 128 + 128] = second

    unpack_heads(recv_ref, 0, emit)
    hidden = x_ref[...].astype(F32) + nn(att_ref[...], wo_ref[...])
    hidden_ref[...] = hidden
    factor = lax.rsqrt(jnp.mean(hidden * hidden, axis=-1, keepdims=True) + EPS)
    mixed = (hidden * factor * gain_ref[...]).astype(BF)
    mixed_ref[...] = mixed
    place = place_ref[...]
    send_ref[:, :D] = nn(place, mixed).astype(BF)
    picked = mask_ref[...] > 0
    logits = jnp.where(picked, nn(mixed, wr_ref[...]), MASKED)
    weight = jnp.exp(logits - jnp.max(logits, axis=1, keepdims=True))
    share = weight / jnp.sum(weight, axis=1, keepdims=True)
    share_ref[...] = share
    send_ref[:, D:] = (slot_share(place, share, row_expert()) * nn(place, dy_ref[...])).astype(BF)


def expert_kernel(rows_ref, w_ref, out_ref, grad_ref, acc_out, acc_row):
    step = pl.program_id(0)

    @pl.when(step == 0)
    def _():
        acc_out[...] = jnp.zeros_like(acc_out)
        acc_row[...] = jnp.zeros_like(acc_row)

    rows = rows_ref[:, :D]
    slot_grad = rows_ref[:, D:]
    gate_w = w_ref[:, 0:SHARD, :].reshape(2 * SHARD, D)
    up_w = w_ref[:, SHARD : 2 * SHARD, :].reshape(2 * SHARD, D)
    down_w = w_ref[:, 2 * SHARD :, :].reshape(2 * SHARD, D)
    gate = nt(rows, gate_w)
    up = nt(rows, up_w)
    act_grad = nt(slot_grad, down_w).astype(BF).astype(F32)
    square = gate * gate
    tanh = jnp.tanh(GELU_C * gate * (1.0 + 0.044715 * square))
    gelu = 0.5 * gate * (1.0 + tanh)
    slope = 0.5 * (1.0 + tanh) + 0.5 * gate * (1.0 - tanh * tanh) * (
        GELU_C * (1.0 + 3 * 0.044715 * square)
    )
    act = (gelu * up).astype(BF)
    gate_grad = (act_grad * up * slope).astype(BF)
    up_grad = (act_grad * gelu).astype(BF)
    acc_out[...] += nn(act, down_w)
    acc_row[...] += nn(gate_grad, gate_w) + nn(up_grad, up_w)
    grad_ref[:, 0:SHARD, :] = tn(gate_grad, rows).astype(BF).reshape(2, SHARD, D)
    grad_ref[:, SHARD : 2 * SHARD, :] = tn(up_grad, rows).astype(BF).reshape(2, SHARD, D)
    grad_ref[:, 2 * SHARD :, :] = tn(act, slot_grad).astype(BF).reshape(2, SHARD, D)

    @pl.when(step == pl.num_programs(0) - 1)
    def _():
        out_ref[:, :D] = acc_out[...].astype(BF)
        out_ref[:, D:] = acc_row[...].astype(BF)


def back_kernel(
    ret_ref, place_ref, place_t_ref, dy_ref, hidden_ref, mixed_ref, share_ref, wr_ref, gain_ref, wo_ref,
    result_ref, hgrad_ref, branch_ref, send_ref, router_ref, gain_out_ref,
):
    place = place_ref[...]
    place_t = place_t_ref[...]
    own = row_expert()
    dy = dy_ref[...]
    returned = ret_ref[:, :D]
    dots = jnp.sum(nn(place, dy) * returned.astype(F32), axis=1, keepdims=True)
    high, low = halves(jnp.where(own, dots, 0.0))
    share = share_ref[...]
    share_grad = nn(place_t, high) + nn(place_t, low)
    inner = jnp.sum(share * share_grad, axis=1, keepdims=True)
    lg_high, lg_low = halves(share * (share_grad - inner))
    wr = wr_ref[...]
    mixed_grad = nn(place_t, ret_ref[:, D:]) + (nt(lg_high, wr) + nt(lg_low, wr))
    hidden = hidden_ref[...]
    factor = lax.rsqrt(jnp.mean(hidden * hidden, axis=-1, keepdims=True) + EPS)
    unit = hidden * factor
    gain_out_ref[...] = jnp.broadcast_to(jnp.sum(mixed_grad * unit, axis=0, keepdims=True), (8, D))
    scaled = mixed_grad * gain_ref[...]
    hgrad = dy.astype(F32) + factor * (
        scaled - unit * jnp.mean(scaled * unit, axis=-1, keepdims=True)
    )
    hgrad_ref[...] = hgrad
    branch = hgrad.astype(BF)
    branch_ref[...] = branch
    for part in range(4):
        res = nt(branch, wo_ref[part * 256 : (part + 1) * 256, :])
        for pair in range(2):
            head = part * 4 + pair * 2
            cols = slice(pair * 128, pair * 128 + 128)
            one, two = pack_pair(res[:TS, cols], res[TS:, cols])
            send_ref[head] = one
            send_ref[head + 1] = two
    mixed = mixed_ref[...]
    router_ref[...] = tn(mixed, lg_high) + tn(mixed, lg_low)
    scale_high, scale_low = halves(
        place_t.astype(F32) * slot_share(place, share, own).T
    )
    moe = nn(scale_high, returned) + nn(scale_low, returned)
    result_ref[...] = (hidden + moe).astype(BF)


def final_kernel(
    recv_ref, normed_ref, x_ref, gain_ref, hgrad_ref, wq_ref, wk_ref, wv_ref,
    igrad_ref, gq_ref, gk_ref, gv_ref, gain_out_ref, flat,
):
    normed = normed_ref[...]
    total = None
    for which, (w_ref, g_ref) in enumerate(((wq_ref, gq_ref), (wk_ref, gk_ref), (wv_ref, gv_ref))):

        def emit(pair, first, second):
            flat[0:TS, pair * 128 : pair * 128 + 128] = first
            flat[TS:, pair * 128 : pair * 128 + 128] = second

        unpack_heads(recv_ref, which * TS, emit)
        grad = flat[...]
        g_ref[...] = tn(normed, grad).astype(BF)
        part = nt(grad, w_ref[...])
        total = part if total is None else total + part
    x = x_ref[...].astype(F32)
    factor = lax.rsqrt(jnp.mean(x * x, axis=-1, keepdims=True) + EPS)
    unit = x * factor
    gain_out_ref[...] = jnp.broadcast_to(jnp.sum(total * unit, axis=0, keepdims=True), (8, D))
    scaled = total * gain_ref[...]
    igrad_ref[...] = (
        hgrad_ref[...]
        + factor * (scaled - unit * jnp.mean(scaled * unit, axis=-1, keepdims=True))
    ).astype(BF)


def exchanged(payload):
    return lax.all_to_all(payload, "expert", split_axis=0, concat_axis=0, tiled=True)


def placement(routes, order):
    micro = routes.shape[0]
    slots = routes.reshape(micro, 2 * TS)
    rank_of = order.reshape(micro, 2 * TS)
    same = slots[:, :, None] == slots[:, None, :]
    earlier = rank_of[:, None, :] < rank_of[:, :, None]
    rank = jnp.sum((same & earlier).astype(jnp.int32), axis=2)
    base = slots * (2 * CAP) + jnp.arange(micro, dtype=jnp.int32)[:, None] * CAP
    target = jnp.where(rank < CAP, base + rank, BUF).reshape(micro * TS, 2)
    rows = jnp.arange(BUF, dtype=jnp.int32)
    place = (rows[:, None] == target[None, :, 0]) | (rows[:, None] == target[None, :, 1])
    place_t = (rows[None, :] == target[:, 0:1]) | (rows[None, :] == target[:, 1:2])
    return place.astype(BF), place_t.astype(BF)


def on_device(
    tokens, cotangent, doc_lengths, routes, order, gain_attn, w_query, w_key, w_value, w_out,
    rel_table, gain_moe, w_router, w_gate, w_up, w_down,
):
    expert_shard = jnp.concatenate([w_gate[0].T, w_up[0].T, w_down[0]], axis=0)
    extra = jnp.zeros((8, 128), BF)
    extra = extra.at[:, :EXPERTS].set(w_router).at[:, 16].set(gain_attn).at[:, 17].set(gain_moe)
    shared = jnp.concatenate(
        [
            jnp.concatenate([w_query, w_key, w_value, w_out], axis=0),
            jnp.pad(extra, ((0, 24), (0, 0))),
        ],
        axis=1,
    )
    near_by = lax.all_gather(shared, "expert", axis=0, tiled=False)
    everyone = lax.all_gather(near_by, "fsdp", axis=1, tiled=False)
    table = lax.all_gather(rel_table, "fsdp", axis=0, tiled=True).astype(F32).reshape(1, NB)
    expert_w = lax.all_gather(expert_shard, "fsdp", axis=0, tiled=False)
    wq, wk, wv, wo = (
        everyone[:, :, 8 * k : 8 * k + 8, :D].reshape(D, D) for k in range(4)
    )
    small = everyone[:, :, 0:8, D:].reshape(D, 128)
    wr = jnp.where(jnp.arange(128) < EXPERTS, small, 0).astype(BF)
    attn_gain = small[:, 16].astype(F32).reshape(1, D)
    moe_gain = small[:, 17].astype(F32).reshape(1, D)
    place, place_t = placement(routes[:, 0], order[:, 0, 0])
    lanes = jnp.arange(128, dtype=jnp.int32)
    route_rows = routes.reshape(TOK, 2)
    picked = (
        (route_rows[:, 0:1] == lanes) | (route_rows[:, 1:2] == lanes)
    ).astype(F32)
    x = tokens.reshape(TOK, D)
    dy = cotangent.reshape(TOK, D)
    lengths = doc_lengths[:, 0]

    normed, packed = call(
        qkv_kernel,
        (shape((TOK, D), BF), shape((H, 3 * TS, 128), BF)),
        x, attn_gain, wq, wk, wv,
    )
    heads = exchanged(packed)
    smem = pl.BlockSpec(memory_space=pltpu.SMEM)
    vmem = pl.BlockSpec(memory_space=pltpu.VMEM)
    attn_scratch = [
        pltpu.VMEM((SEQ, 256), BF),
        pltpu.VMEM((EXPERTS, TOK, 256), BF),
        pltpu.VMEM((12 * TS, TOK), F32),
    ]
    attended, lse = call(
        attn_fwd_kernel,
        (shape((EXPERTS, TS, 128), BF), shape((EXPERTS, 8, TOK), F32)),
        lengths, table, heads,
        in_specs=[smem, smem, vmem],
        scratch=attn_scratch + [pltpu.VMEM((128, SEQ), BF)],
    )
    att_back = exchanged(attended)
    att, hidden, mixed, share, send = call(
        mid_kernel,
        (
            shape((TOK, D), BF), shape((TOK, D), F32), shape((TOK, D), BF),
            shape((TOK, 128), F32), shape((BUF, 2 * D), BF),
        ),
        att_back, x, wo, moe_gain, wr, picked, place, dy,
    )
    received = exchanged(send.reshape(EXPERTS, 2 * CAP, 2 * D)).reshape(BUF, 2 * D)
    expert_out, expert_grads = pl.pallas_call(
        expert_kernel,
        grid=(FSDP // 2,),
        out_shape=(shape((BUF, 2 * D), BF), shape((FSDP, 3 * SHARD, D), BF)),
        in_specs=[
            pl.BlockSpec((BUF, 2 * D), lambda i: (0, 0)),
            pl.BlockSpec((2, 3 * SHARD, D), lambda i: (i, 0, 0)),
        ],
        out_specs=(
            pl.BlockSpec((BUF, 2 * D), lambda i: (0, 0)),
            pl.BlockSpec((2, 3 * SHARD, D), lambda i: (i, 0, 0)),
        ),
        scratch_shapes=[pltpu.VMEM((BUF, D), F32), pltpu.VMEM((BUF, D), F32)],
        compiler_params=pltpu.CompilerParams(vmem_limit_bytes=VMEM_LIMIT),
    )(received, expert_w)
    expert_sum = lax.psum_scatter(
        expert_grads.reshape(FSDP * 3 * SHARD, D), "fsdp", scatter_dimension=0, tiled=True
    ).astype(F32)
    returned = exchanged(expert_out.reshape(EXPERTS, 2 * CAP, 2 * D)).reshape(BUF, 2 * D)
    result, hgrad, branch, att_grad, router_grad, moe_gain_grad = call(
        back_kernel,
        (
            shape((TOK, D), BF), shape((TOK, D), F32), shape((TOK, D), BF),
            shape((H, TS, 128), BF), shape((D, 128), F32), shape((8, D), F32),
        ),
        returned, place, place_t, dy, hidden, mixed, share, wr, moe_gain, wo,
    )
    out_grad = tn(att, branch).astype(BF)
    head_grads = exchanged(att_grad)
    qkv_grads, table_grad = call(
        attn_bwd_kernel,
        (shape((EXPERTS, 3 * TS, 128), BF), shape((8, 128), F32)),
        lengths, table, heads, head_grads, lse,
        in_specs=[smem, smem, vmem, vmem, vmem],
        scratch=attn_scratch
        + [
            pltpu.VMEM((144, SEQ), BF),
            pltpu.VMEM((SEQ, 128), F32),
            pltpu.VMEM((SEQ, 128), F32),
            pltpu.VMEM((2 * TS, TOK), F32),
            pltpu.VMEM((8, TOK), F32),
        ],
    )
    token_grads = exchanged(qkv_grads)
    input_grad, gq, gk, gv, attn_gain_grad = call(
        final_kernel,
        (
            shape((TOK, D), BF), shape((D, D), BF), shape((D, D), BF), shape((D, D), BF),
            shape((8, D), F32),
        ),
        token_grads, normed, x, attn_gain, hgrad, wq, wk, wv,
        scratch=[pltpu.VMEM((TOK, D), BF)],
    )
    small_grad = jnp.concatenate(
        [
            router_grad[:, :EXPERTS],
            attn_gain_grad[0][:, None],
            moe_gain_grad[0][:, None],
        ],
        axis=1,
    ).astype(BF)
    small_grad = jnp.pad(small_grad, ((0, 0), (0, 110))).reshape(EXPERTS * FSDP, 8, 128)
    grads = jnp.concatenate(
        [
            jnp.concatenate([g.reshape(EXPERTS * FSDP, 8, D) for g in (gq, gk, gv, out_grad)], axis=1),
            jnp.pad(small_grad, ((0, 0), (0, 24), (0, 0))),
        ],
        axis=2,
    )
    grads = grads.reshape(EXPERTS, FSDP, 32, D + 128).swapaxes(0, 1)
    grads = lax.psum_scatter(grads, "fsdp", scatter_dimension=0, tiled=False)
    grads = lax.psum_scatter(grads, "expert", scatter_dimension=0, tiled=False).astype(F32)
    table_out = lax.psum_scatter(table_grad[0, :NB], "fsdp", scatter_dimension=0, tiled=True)
    return (
        result.reshape(tokens.shape),
        input_grad.reshape(tokens.shape),
        grads[0:8, D + 16],
        grads[0:8, :D],
        grads[8:16, :D],
        grads[16:24, :D],
        grads[24:32, :D],
        table_out,
        grads[0:8, D + 17],
        grads[0:8, D : D + EXPERTS],
        expert_sum[:SHARD].T[None],
        expert_sum[SHARD : 2 * SHARD].T[None],
        expert_sum[2 * SHARD :][None],
    )


def solution(mesh):
    row = P(None, "fsdp", "expert", None)
    flat = P(("expert", "fsdp"))
    matrix = P(("expert", "fsdp"), None)
    columns = P("expert", None, "fsdp")
    deep = P("expert", "fsdp", None)
    return jax.shard_map(
        on_device,
        mesh=mesh,
        in_specs=(
            row, row, P(None, "fsdp", None), row, row, flat, matrix, matrix, matrix, matrix,
            flat, flat, matrix, columns, columns, deep,
        ),
        out_specs=(
            row, row, flat, matrix, matrix, matrix, matrix, flat, flat, matrix, columns, columns, deep,
        ),
        check_vma=False,
    )
```

```python
import jax
import jax.numpy as jnp
from jax import lax
from jax.experimental import pallas as pl
from jax.experimental.pallas import tpu as pltpu
from jax.sharding import PartitionSpec as P

H = 16
HD = 64
NB = 32
D = 1024
FF = 2816
WINDOW = 1024
EXPERTS = 16
CAP = 20
TS = 128
FSDP = 8
SHARD = FF // FSDP
TOK = 2 * TS
BUF = EXPERTS * 2 * CAP
SEQ = EXPERTS * TS
EPS = 1e-06
MASKED = -1e30
EDGES = tuple(range(1, 17)) + (19, 21, 24, 27, 31, 35, 40, 46, 52, 59, 67, 77, 87, 99, 113)
GELU_C = 0.7978845608028654
BF = jnp.bfloat16
F32 = jnp.float32
VMEM_LIMIT = 58 * 1024 * 1024


def nn(left, right):
    return lax.dot_general(left, right, (((1,), (0,)), ((), ())), preferred_element_type=F32)


def nt(left, right):
    return lax.dot_general(left, right, (((1,), (1,)), ((), ())), preferred_element_type=F32)


def tn(left, right):
    return lax.dot_general(left, right, (((0,), (0,)), ((), ())), preferred_element_type=F32)


def halves(value):
    high = value.astype(BF)
    return high, (value - high.astype(F32)).astype(BF)


def call(kernel, out_shape, *args, scratch=(), in_specs=None, collective_id=None):
    return pl.pallas_call(
        kernel,
        out_shape=out_shape,
        in_specs=in_specs or [pl.BlockSpec(memory_space=pltpu.VMEM)] * len(args),
        out_specs=jax.tree.map(lambda _: pl.BlockSpec(memory_space=pltpu.VMEM), out_shape),
        scratch_shapes=list(scratch),
        compiler_params=pltpu.CompilerParams(
            vmem_limit_bytes=VMEM_LIMIT,
            collective_id=collective_id,
            has_side_effects=collective_id is not None,
        ),
    )(*args)


def shape(dims, dtype):
    return jax.ShapeDtypeStruct(dims, dtype)


def lane_half(dims):
    return lax.broadcasted_iota(jnp.int32, dims, 1) % 128 < HD


def pack_pair(first, second):
    left = lane_half(first.shape)
    return (
        jnp.where(left, first, pltpu.roll(second, HD, 1)).astype(BF),
        jnp.where(left, pltpu.roll(first, HD, 1), second).astype(BF),
    )


MESH = pl.DeviceIdType.MESH
WIDE = 2 * D + 128
PARTS = (pl.ds(0, 1152), pl.ds(1152, 1024))


def coords():
    e, f = lax.axis_index("expert"), lax.axis_index("fsdp")
    return lax.div(e, 4), lax.rem(e, 4), lax.div(f, 2), lax.rem(f, 2)


def device(z, y, x, c):
    return (z * 4 + y, x * 2 + c)


def ring(at, step):
    return lax.rem(at + step, 4)


def greet(peers):
    barrier = pltpu.get_barrier_semaphore()
    for peer in peers:
        pl.semaphore_signal(barrier, inc=1, device_id=peer, device_id_type=MESH)
    pl.semaphore_wait(barrier, len(peers))


class Copies:
    def __init__(self, send_sem, recv_sem):
        self.send_sem, self.recv_sem, self.started = send_sem, recv_sem, []

    def go(self, src, dst, peer):
        at = len(self.started)
        copy = pltpu.make_async_remote_copy(
            src_ref=src,
            dst_ref=dst,
            send_sem=self.send_sem.at[at],
            recv_sem=self.recv_sem.at[at],
            device_id=peer,
            device_id_type=MESH,
        )
        copy.start()
        self.started.append(copy)
        return copy

    def drain(self):
        for copy in self.started:
            copy.wait_send()


def chip_peers(z, y, x, c):
    steps = (1, 2, 3)
    return (
        [device(z, y, ring(x, k), c) for k in steps],
        [device(z, ring(y, k), x, c) for k in steps],
        [device(ring(z, k), y, x, c) for k in steps],
        device(z, y, x, 1 - c),
    )


def lane_pick():
    col = lax.broadcasted_iota(jnp.int32, (128, D), 1)
    return (lax.rem(col, 8) == lax.broadcasted_iota(jnp.int32, (128, D), 0)).astype(BF)


def own_columns():
    col = lax.broadcasted_iota(jnp.int32, (128, D), 1)
    low = lax.broadcasted_iota(jnp.int32, (128, D), 0) * 8
    return (col >= low) & (col < low + 8)


def pick_row(values, row):
    at = lax.broadcasted_iota(jnp.int32, values.shape, values.ndim - 2)
    return jnp.sum(jnp.where(at == row, values, 0.0), axis=-2)


def gather_kernel(
    x_ref, wq_ref, wk_ref, wv_ref, wo_ref, small_ref,
    normed_ref, out_ref, wq_out, wk_out, wv_out, wo_out, wr_out, gain_out, tab_out,
    box, send_sem, recv_sem,
):
    z, y, x, c = coords()
    to_x, to_y, to_z, twin = chip_peers(z, y, x, c)
    top = [wq_ref[...].astype(F32), wk_ref[...].astype(F32)]
    bottom = [wv_ref[...].astype(F32), wo_ref[...].astype(F32)]
    for half in range(2):
        value = jnp.concatenate([top[half], bottom[half]], axis=0).astype(BF)
        box[z, y, x, c, :, half * D : (half + 1) * D] = value
    box[z, y, x, c, :, 2 * D :] = small_ref[...]
    greet(to_x + to_y + to_z + [twin])
    copies = Copies(send_sem, recv_sem)
    one, two = PARTS

    def same(ref, peer):
        return copies.go(ref, ref, peer)

    def forward(ref):
        forwards.append(same(ref, twin))

    forwards = []
    back = {k: 4 - k for k in (1, 2, 3)}
    along_x = [same(box.at[z, y, x, c], peer) for peer in to_x]
    forward(box.at[z, y, x, c])
    tokens = x_ref[...].astype(F32)
    unit = tokens * lax.rsqrt(jnp.mean(tokens * tokens, axis=-1, keepdims=True) + EPS)
    for copy in along_x:
        copy.wait_recv()
    second_a = [same(box.at[z, y, :, c, :, one], peer) for peer in to_z]
    second_b = [same(box.at[z, y, :, c, :, two], peer) for peer in to_y]
    for k in (1, 2, 3):
        forward(box.at[z, y, ring(x, back[k]), c])
    for copy in second_a:
        copy.wait_recv()
    third_a = [same(box.at[:, y, :, c, :, one], peer) for peer in to_y]
    for copy in second_b:
        copy.wait_recv()
    third_b = [same(box.at[z, :, :, c, :, two], peer) for peer in to_z]
    for k in (1, 2, 3):
        forward(box.at[ring(z, back[k]), y, :, c, :, one])
        forward(box.at[z, ring(y, back[k]), :, c, :, two])
    for k in (1, 2, 3):
        third_a[k - 1].wait_recv()
        forward(box.at[:, ring(y, back[k]), :, c, :, one])
        third_b[k - 1].wait_recv()
        forward(box.at[ring(z, back[k]), :, :, c, :, two])
    for copy in forwards:
        copy.wait_recv()

    pairs = ((wq_out, wv_out), (wk_out, wo_out))
    for plane in range(4):
        rows = slice(plane * 256, plane * 256 + 256)
        for half in range(2):
            value = box[plane, :, :, :, :, half * D : (half + 1) * D].reshape(32, 16, D).astype(F32)
            pairs[half][0][rows, :] = value[:, :8, :].reshape(256, D).astype(BF)
            pairs[half][1][rows, :] = value[:, 8:, :].reshape(256, D).astype(BF)
    small = box[:, :, :, :, :, 2 * D :].reshape(128, 16, 128).astype(F32)
    lane = lax.broadcasted_iota(jnp.int32, (D, 128), 1)
    wr_out[...] = jnp.where(lane < EXPERTS, small[:, :8, :].reshape(D, 128), 0.0).astype(BF)
    pick, mine = lane_pick(), own_columns()
    gains = [
        jnp.sum(jnp.where(mine, nn(pick_row(small[:, 8:, :], row).astype(BF), pick), 0.0), axis=0, keepdims=True)
        for row in range(2)
    ]
    gain_out[...] = jnp.concatenate(gains + [jnp.zeros((6, D), F32)], axis=0)
    near = box[z, y, :, :, :, 2 * D :].reshape(8, 16, 128).astype(F32)
    tab_out[...] = pick_row(near, 10)

    normed = (unit * gains[0]).astype(BF)
    normed_ref[...] = normed
    for which, w_ref in enumerate((wq_out, wk_out, wv_out)):
        for part in range(4):
            res = nn(normed, w_ref[:, part * 256 : (part + 1) * 256])
            for pair in range(2):
                head = part * 4 + pair * 2
                cols = slice(pair * 128, pair * 128 + 128)
                first, second = pack_pair(res[:TS, cols], res[TS:, cols])
                out_ref[head, which * TS : (which + 1) * TS, :] = first
                out_ref[head + 1, which * TS : (which + 1) * TS, :] = second
    copies.drain()


def attn_setup(len_ref, tab_ref, recv_ref, kext, qext, bias):
    rows = lax.broadcasted_iota(jnp.int32, (SEQ, 128), 0)
    lanes = lax.broadcasted_iota(jnp.int32, (SEQ, 128), 1)
    end1 = [len_ref[m, 0] for m in range(2)]
    end2 = [len_ref[m, 0] + len_ref[m, 1] for m in range(2)]
    kfeat = jnp.where(lanes == 4, 1.0, 0.0)
    for m in range(2):
        kfeat = jnp.where((lanes == 2 * m) & (rows < end1[m]), 1.0, kfeat)
        kfeat = jnp.where((lanes == 2 * m + 1) & (rows < end2[m]), 1.0, kfeat)
    kext[:, 128:] = kfeat.astype(BF)
    for i in range(EXPERTS):
        kext[i * TS : (i + 1) * TS, :128] = recv_ref[i, TS : 2 * TS, :]
    left = lane_half((TS, 128))
    row_in = lax.broadcasted_iota(jnp.int32, (TS, 128), 0)
    lane_in = lax.broadcasted_iota(jnp.int32, (TS, 128), 1)
    for i in range(EXPERTS):
        q2 = recv_ref[i, 0:TS, :].astype(F32) * (HD**-0.5)
        pos = row_in + i * TS
        for m in range(2):
            keep = left if m == 0 else jnp.logical_not(left)
            qext[i, m * TS : (m + 1) * TS, :128] = jnp.where(keep, q2, 0.0).astype(BF)
            feat = jnp.where((lane_in == 2 * m) & (pos >= end1[m]), MASKED, 0.0)
            feat = jnp.where((lane_in == 2 * m + 1) & (pos >= end2[m]), MASKED, feat)
            qext[i, m * TS : (m + 1) * TS, 128:] = feat.astype(BF)
    for block in range(12):
        dist = 1024 - block * TS + lane_in - row_in
        if block in (7, 8):
            value = jnp.broadcast_to(tab_ref[0:1, 0:1], (TS, 128))
            for bucket, edge in enumerate(EDGES):
                b = bucket + 1
                value = jnp.where(dist >= edge, tab_ref[b // 4 : b // 4 + 1, b % 4 : b % 4 + 1], value)
        else:
            value = jnp.broadcast_to(tab_ref[7:8, 3:4], (TS, 128))
        value = jnp.where((dist >= 0) & (dist < WINDOW), value, MASKED)
        bias[block * TS : (block + 1) * TS, :128] = value
        bias[block * TS : (block + 1) * TS, 128:] = value


def eye(size):
    return (
        lax.broadcasted_iota(jnp.int32, (size, size), 0)
        == lax.broadcasted_iota(jnp.int32, (size, size), 1)
    ).astype(BF)


def strip_loops(strip):
    def early(i, carry):
        strip(i, 4, 0)
        return carry

    def middle(i, carry):
        strip(i, 8, 0)
        return carry

    def late(i, carry):
        strip(i, 9, i - 8)
        return carry

    lax.fori_loop(0, 4, early, 0)
    lax.fori_loop(4, 8, middle, 0)
    lax.fori_loop(8, 16, late, 0)


def span(block, count):
    return pl.ds(pl.multiple_of(block * TS, TS), count * TS)


def attn_fwd_kernel(len_ref, tab_ref, recv_ref, out_ref, lse_ref, kext, qext, bias, vt):
    attn_setup(len_ref, tab_ref, recv_ref, kext, qext, bias)
    unit = eye(TS)
    for i in range(EXPERTS):
        vt[:, i * TS : (i + 1) * TS] = nt(unit, recv_ref[i, 2 * TS : 3 * TS, :]).astype(BF)

    def strip(i, count, first):
        s = nt(kext[span(first, count), :], qext[i]) + bias[span(first - i + 8, count), :]
        top = jnp.max(s, axis=0, keepdims=True)
        p = jnp.exp(s - top)
        total = jnp.sum(p, axis=0, keepdims=True)
        res = nn(vt[:, span(first, count)], p.astype(BF)) / total
        both = jnp.concatenate([res[:HD, :TS], res[HD:, TS:]], axis=0)
        out_ref[i] = both.T.astype(BF)
        lse_ref[i] = jnp.broadcast_to(top + jnp.log(total), (8, TOK))

    strip_loops(strip)


def attn_bwd_kernel(
    len_ref, tab_ref, recv_ref, dout_ref, lse_ref, out_ref, tab_out_ref, kext, qext, bias, ktext, dk, dv, near, far
):
    attn_setup(len_ref, tab_ref, recv_ref, kext, qext, bias)
    unit = eye(256)
    for i in range(EXPERTS):
        ktext[:, i * TS : (i + 1) * TS] = nt(unit, kext[i * TS : (i + 1) * TS, :])[:144].astype(BF)
    dk[...] = jnp.zeros_like(dk)
    dv[...] = jnp.zeros_like(dv)
    near[...] = jnp.zeros_like(near)
    far[...] = jnp.zeros_like(far)
    left = lane_half((TS, 128))

    def strip(i, count, first):
        q = qext[i]
        s = nt(kext[span(first, count), :], q) + bias[span(first - i + 8, count), :]
        p = jnp.exp(s - lse_ref[i][0:1])
        do2 = dout_ref[i]
        zero = jnp.zeros_like(do2)
        do = jnp.concatenate([jnp.where(left, do2, zero), jnp.where(left, zero, do2)], axis=0)
        if count == 9:
            v = recv_ref[pl.ds(first, count), 2 * TS : 3 * TS, :].reshape(count * TS, 128)
        else:
            v = recv_ref[0:count, 2 * TS : 3 * TS, :].reshape(count * TS, 128)
        dp = nt(v, do)
        inner = jnp.sum(p * dp, axis=0, keepdims=True)
        ds = (p * (dp - inner)).astype(BF)
        dv[span(first, count), :] += nn(p.astype(BF), do)
        dk[span(first, count), :] += nn(ds, q[:, :128])
        dqt = nn(ktext[:, span(first, count)], ds)
        both = jnp.concatenate([dqt[:HD, :TS], dqt[HD : 2 * HD, TS:]], axis=0) * (HD**-0.5)
        out_ref[i, 0:TS, :] = both.T.astype(BF)
        far[...] += dqt[128:136]
        if count == 9:
            near[...] += ds[7 * TS :].astype(F32)
        else:
            nearby.append(ds)

    nearby = []

    def loop(low, high, count):
        def body(i, carry):
            nearby.clear()
            first = i - 8 if count == 9 else 0
            strip(i, count, first)
            if count != 9:
                ds = nearby[0]
                for block in range(count):
                    value = ds[block * TS : (block + 1) * TS].astype(F32)

                    @pl.when(i == block)
                    def _(value=value):
                        near[TS:] += value

                    @pl.when(i == block + 1)
                    def _(value=value):
                        near[:TS] += value

            return carry

        lax.fori_loop(low, high, body, 0)

    loop(0, 4, 4)
    loop(4, 8, 8)
    loop(8, 16, 9)
    for i in range(EXPERTS):
        out_ref[i, TS : 2 * TS, :] = dk[i * TS : (i + 1) * TS, :].astype(BF)
        out_ref[i, 2 * TS :, :] = dv[i * TS : (i + 1) * TS, :].astype(BF)
    grads = near[:, :TS] + near[:, TS:]
    dist = (
        TS
        + lax.broadcasted_iota(jnp.int32, (TOK, TS), 1)
        - lax.broadcasted_iota(jnp.int32, (TOK, TS), 0)
    )
    total = jnp.sum(far[4:5, :])
    lane = lax.broadcasted_iota(jnp.int32, (8, 128), 1)
    lane = jnp.where(lane < 4, lane + 4 * lax.broadcasted_iota(jnp.int32, (8, 128), 0), NB)
    res = jnp.zeros((8, 128), F32)
    lows = (0,) + EDGES
    seen = 0.0
    for b in range(NB - 1):
        part = jnp.sum(jnp.where((dist >= lows[b]) & (dist < lows[b + 1]), grads, 0.0))
        seen = seen + part
        res = jnp.where(lane == b, part, res)
    res = jnp.where(lane == NB - 1, total - seen, res)
    tab_out_ref[...] = res


def row_expert():
    row = lax.broadcasted_iota(jnp.int32, (BUF, 128), 0)
    lane = lax.broadcasted_iota(jnp.int32, (BUF, 128), 1) * (2 * CAP)
    return (row >= lane) & (row < lane + 2 * CAP)


def unpack_heads(recv_ref, lo, emit):
    for pair in range(H // 2):
        one = recv_ref[2 * pair, lo : lo + TS, :].astype(F32)
        two = recv_ref[2 * pair + 1, lo : lo + TS, :].astype(F32)
        first, second = pack_pair(one, two)
        emit(pair, first, second)


def slot_share(place, share_e, own):
    high, low = halves(share_e)
    return jnp.sum(jnp.where(own, nn(place, high) + nn(place, low), 0.0), axis=1, keepdims=True)


def mid_kernel(
    recv_ref, x_ref, wo_ref, gain_ref, wr_ref, mask_ref, place_ref, dy_ref,
    att_ref, hidden_ref, mixed_ref, share_ref, send_ref,
):
    def emit(pair, first, second):
        att_ref[0:TS, pair * 128 : pair * 128 + 128] = first
        att_ref[TS:, pair * 128 : pair * 128 + 128] = second

    unpack_heads(recv_ref, 0, emit)
    hidden = x_ref[...].astype(F32) + nn(att_ref[...], wo_ref[...])
    hidden_ref[...] = hidden
    factor = lax.rsqrt(jnp.mean(hidden * hidden, axis=-1, keepdims=True) + EPS)
    mixed = (hidden * factor * gain_ref[1:2, :]).astype(BF)
    mixed_ref[...] = mixed
    place = place_ref[...]
    send_ref[:, :D] = nn(place, mixed).astype(BF)
    picked = mask_ref[...] > 0
    logits = jnp.where(picked, nn(mixed, wr_ref[...]), MASKED)
    weight = jnp.exp(logits - jnp.max(logits, axis=1, keepdims=True))
    share = weight / jnp.sum(weight, axis=1, keepdims=True)
    share_ref[...] = share
    send_ref[:, D:] = (slot_share(place, share, row_expert()) * nn(place, dy_ref[...])).astype(BF)


def expert_kernel(rows_ref, w_ref, out_ref, grad_ref, acc_out, acc_row):
    step = pl.program_id(0)

    @pl.when(step == 0)
    def _():
        acc_out[...] = jnp.zeros_like(acc_out)
        acc_row[...] = jnp.zeros_like(acc_row)

    rows = rows_ref[:, :D]
    slot_grad = rows_ref[:, D:]
    gate_w = w_ref[:, 0:SHARD, :].reshape(2 * SHARD, D)
    up_w = w_ref[:, SHARD : 2 * SHARD, :].reshape(2 * SHARD, D)
    down_w = w_ref[:, 2 * SHARD :, :].reshape(2 * SHARD, D)
    gate = nt(rows, gate_w)
    up = nt(rows, up_w)
    act_grad = nt(slot_grad, down_w).astype(BF).astype(F32)
    square = gate * gate
    tanh = jnp.tanh(GELU_C * gate * (1.0 + 0.044715 * square))
    gelu = 0.5 * gate * (1.0 + tanh)
    slope = 0.5 * (1.0 + tanh) + 0.5 * gate * (1.0 - tanh * tanh) * (
        GELU_C * (1.0 + 3 * 0.044715 * square)
    )
    act = (gelu * up).astype(BF)
    gate_grad = (act_grad * up * slope).astype(BF)
    up_grad = (act_grad * gelu).astype(BF)
    acc_out[...] += nn(act, down_w)
    acc_row[...] += nn(gate_grad, gate_w) + nn(up_grad, up_w)
    grad_ref[:, 0:SHARD, :] = tn(gate_grad, rows).astype(BF).reshape(2, SHARD, D)
    grad_ref[:, SHARD : 2 * SHARD, :] = tn(up_grad, rows).astype(BF).reshape(2, SHARD, D)
    grad_ref[:, 2 * SHARD :, :] = tn(act, slot_grad).astype(BF).reshape(2, SHARD, D)

    @pl.when(step == pl.num_programs(0) - 1)
    def _():
        out_ref[:, :D] = acc_out[...].astype(BF)
        out_ref[:, D:] = acc_row[...].astype(BF)


def back_kernel(
    ret_ref, place_ref, place_t_ref, dy_ref, hidden_ref, mixed_ref, share_ref, wr_ref, gain_ref, wo_ref,
    result_ref, hgrad_ref, branch_ref, send_ref, router_ref, gain_out_ref,
):
    place = place_ref[...]
    place_t = place_t_ref[...]
    own = row_expert()
    dy = dy_ref[...]
    returned = ret_ref[:, :D]
    dots = jnp.sum(nn(place, dy) * returned.astype(F32), axis=1, keepdims=True)
    high, low = halves(jnp.where(own, dots, 0.0))
    share = share_ref[...]
    share_grad = nn(place_t, high) + nn(place_t, low)
    inner = jnp.sum(share * share_grad, axis=1, keepdims=True)
    lg_high, lg_low = halves(share * (share_grad - inner))
    wr = wr_ref[...]
    mixed_grad = nn(place_t, ret_ref[:, D:]) + (nt(lg_high, wr) + nt(lg_low, wr))
    hidden = hidden_ref[...]
    factor = lax.rsqrt(jnp.mean(hidden * hidden, axis=-1, keepdims=True) + EPS)
    unit = hidden * factor
    gain_out_ref[...] = jnp.broadcast_to(jnp.sum(mixed_grad * unit, axis=0, keepdims=True), (8, D))
    scaled = mixed_grad * gain_ref[1:2, :]
    hgrad = dy.astype(F32) + factor * (
        scaled - unit * jnp.mean(scaled * unit, axis=-1, keepdims=True)
    )
    hgrad_ref[...] = hgrad
    branch = hgrad.astype(BF)
    branch_ref[...] = branch
    for part in range(4):
        res = nt(branch, wo_ref[part * 256 : (part + 1) * 256, :])
        for pair in range(2):
            head = part * 4 + pair * 2
            cols = slice(pair * 128, pair * 128 + 128)
            one, two = pack_pair(res[:TS, cols], res[TS:, cols])
            send_ref[head] = one
            send_ref[head + 1] = two
    mixed = mixed_ref[...]
    router_ref[...] = tn(mixed, lg_high) + tn(mixed, lg_low)
    scale_high, scale_low = halves(
        place_t.astype(F32) * slot_share(place, share, own).T
    )
    moe = nn(scale_high, returned) + nn(scale_low, returned)
    result_ref[...] = (hidden + moe).astype(BF)


def final_kernel(
    recv_ref, normed_ref, x_ref, gains_ref, hgrad_ref, wq_ref, wk_ref, wv_ref,
    att_ref, branch_ref, router_ref, moe_gain_ref, table_ref,
    igrad_ref, gq_ref, gk_ref, gv_ref, go_ref, small_ref,
    flat_q, flat_k, flat_v, box, from_twin, a1, b1, ta, tb, a2, b2, ua, ub, a3, b3, send_sem, recv_sem,
):
    z, y, x, c = coords()
    to_x, to_y, to_z, twin = chip_peers(z, y, x, c)
    greet(to_x + to_y + to_z + [twin])
    copies = Copies(send_sem, recv_sem)
    one, two = PARTS

    for which, flat in enumerate((flat_q, flat_k, flat_v)):

        def emit(pair, first, second):
            flat[0:TS, pair * 128 : pair * 128 + 128] = first
            flat[TS:, pair * 128 : pair * 128 + 128] = second

        unpack_heads(recv_ref, which * TS, emit)

    total = nt(flat_q[...], wq_ref[...]) + nt(flat_k[...], wk_ref[...]) + nt(flat_v[...], wv_ref[...])
    tokens = x_ref[...].astype(F32)
    factor = lax.rsqrt(jnp.mean(tokens * tokens, axis=-1, keepdims=True) + EPS)
    unit = tokens * factor
    attn_gain_grad = jnp.sum(total * unit, axis=0, keepdims=True)

    pick, mine = lane_pick(), own_columns()
    small = []
    for row in (attn_gain_grad, moe_gain_ref[0:1, :]):
        high, low = halves(jnp.where(mine, row, 0.0))
        small.append(nt(high, pick) + nt(low, pick))
    at = lax.broadcasted_iota(jnp.int32, (128, 8, 128), 1)
    lower = jnp.where(at == 0, small[0][:, None, :], 0.0) + jnp.where(at == 1, small[1][:, None, :], 0.0)
    extra = jnp.concatenate([router_ref[...].reshape(128, 8, 128), lower], axis=1)
    box[:, :, :, :, :, 2 * D :] = extra.astype(BF).reshape(4, 4, 4, 2, 16, 128)
    at = lax.broadcasted_iota(jnp.int32, (8, 16, 128), 1)
    here = box[z, y, :, :, :, 2 * D :].reshape(8, 16, 128).astype(F32)
    here = here + jnp.where(at == 10, table_ref[...][:, None, :], 0.0)
    box[z, y, :, :, :, 2 * D :] = here.astype(BF).reshape(4, 2, 16, 128)

    planes = [ring(z, k) for k in (1, 2, 3, 0)]
    to_twin = []
    for plane in planes:
        cols = pl.ds(pl.multiple_of(plane * 256, 256), 256)
        left = normed_ref[:, cols]
        for half, (upper, low_left, lower) in enumerate(
            ((flat_q, left, flat_v), (flat_k, att_ref[:, cols], branch_ref))
        ):
            value = jnp.concatenate(
                [tn(left, upper[...]).reshape(32, 8, D), tn(low_left, lower[...]).reshape(32, 8, D)], axis=1
            )
            box[plane, :, :, :, :, half * D : (half + 1) * D] = value.astype(BF).reshape(4, 4, 2, 16, D)
        to_twin.append(copies.go(box.at[plane, :, :, 1 - c], from_twin.at[plane], twin))

    first_a = []
    for k, plane in enumerate(planes):
        to_twin[k].wait_recv()
        both = box[plane, :, :, c].astype(F32) + from_twin[plane].astype(F32)
        from_twin[plane] = both.astype(BF)
        if k < 3:
            first_a.append(copies.go(from_twin.at[plane, :, :, :, one], a1.at[k], to_z[k]))
    first_b = [
        copies.go(from_twin.at[:, ring(y, k + 1), :, :, two], b1.at[k], to_y[k]) for k in range(3)
    ]
    scaled = total * gains_ref[0:1, :]
    igrad_ref[...] = (
        hgrad_ref[...]
        + factor * (scaled - unit * jnp.mean(scaled * unit, axis=-1, keepdims=True))
    ).astype(BF)

    for copy in first_a:
        copy.wait_recv()
    value = from_twin[z, :, :, :, one].astype(F32)
    for k in range(3):
        value = value + a1[k].astype(F32)
    ta[...] = value.astype(BF)
    second_a = [copies.go(ta.at[ring(y, k + 1)], a2.at[k], to_y[k]) for k in range(3)]
    for copy in first_b:
        copy.wait_recv()
    value = from_twin[:, y, :, :, two].astype(F32)
    for k in range(3):
        value = value + b1[k].astype(F32)
    tb[...] = value.astype(BF)
    second_b = [copies.go(tb.at[ring(z, k + 1)], b2.at[k], to_z[k]) for k in range(3)]
    thirds = []
    for copies_in, sums, at_axis, landed, held, last, in_part in (
        (second_a, ta, y, a2, ua, a3, one),
        (second_b, tb, z, b2, ub, b3, two),
    ):
        for copy in copies_in:
            copy.wait_recv()
        value = sums[at_axis].astype(F32)
        for k in range(3):
            value = value + landed[k].astype(F32)
        held[...] = value.astype(BF)
        thirds.append([copies.go(held.at[ring(x, k + 1)], last.at[k], to_x[k]) for k in range(3)])
    done = []
    for group, held, last in zip(thirds, (ua, ub), (a3, b3)):
        for copy in group:
            copy.wait_recv()
        value = held[x].astype(F32)
        for k in range(3):
            value = value + last[k].astype(F32)
        done.append(value)
    gq_ref[...] = done[0][:8, :D]
    gv_ref[...] = done[0][8:, :D]
    gk_ref[...] = jnp.concatenate([done[0][:8, D:], done[1][:8, : D - 128]], axis=1)
    go_ref[...] = jnp.concatenate([done[0][8:, D:], done[1][8:, : D - 128]], axis=1)
    small_ref[...] = done[1][:, D - 128 :]
    copies.drain()


def exchanged(payload):
    return lax.all_to_all(payload, "expert", split_axis=0, concat_axis=0, tiled=True)


def placement(routes, order):
    micro = routes.shape[0]
    slots = routes.reshape(micro, 2 * TS)
    rank_of = order.reshape(micro, 2 * TS)
    same = slots[:, :, None] == slots[:, None, :]
    earlier = rank_of[:, None, :] < rank_of[:, :, None]
    rank = jnp.sum((same & earlier).astype(jnp.int32), axis=2)
    base = slots * (2 * CAP) + jnp.arange(micro, dtype=jnp.int32)[:, None] * CAP
    target = jnp.where(rank < CAP, base + rank, BUF).reshape(micro * TS, 2)
    rows = jnp.arange(BUF, dtype=jnp.int32)
    place = (rows[:, None] == target[None, :, 0]) | (rows[:, None] == target[None, :, 1])
    place_t = (rows[None, :] == target[:, 0:1]) | (rows[None, :] == target[:, 1:2])
    return place.astype(BF), place_t.astype(BF)


def on_device(
    tokens, cotangent, doc_lengths, routes, order, gain_attn, w_query, w_key, w_value, w_out,
    rel_table, gain_moe, w_router, w_gate, w_up, w_down,
):
    expert_shard = jnp.concatenate([w_gate[0].T, w_up[0].T, w_down[0]], axis=0)
    expert_w = lax.all_gather(expert_shard, "fsdp", axis=0, tiled=False)

    def padded(value):
        return jnp.pad(value, ((0, 0), (0, 128 - value.shape[1])))

    small = jnp.concatenate(
        [padded(v) for v in (w_router, gain_attn[None], gain_moe[None], rel_table[None])]
        + [jnp.zeros((5, 128), BF)],
        axis=0,
    )
    place, place_t = placement(routes[:, 0], order[:, 0, 0])
    lanes = jnp.arange(128, dtype=jnp.int32)
    route_rows = routes.reshape(TOK, 2)
    picked = (
        (route_rows[:, 0:1] == lanes) | (route_rows[:, 1:2] == lanes)
    ).astype(F32)
    x = tokens.reshape(TOK, D)
    dy = cotangent.reshape(TOK, D)
    lengths = doc_lengths[:, 0]

    normed, packed, wq, wk, wv, wo, wr, gains, table = call(
        gather_kernel,
        (
            shape((TOK, D), BF), shape((H, 3 * TS, 128), BF), shape((D, D), BF), shape((D, D), BF),
            shape((D, D), BF), shape((D, D), BF), shape((D, 128), BF), shape((8, D), F32), shape((8, 128), F32),
        ),
        x, w_query, w_key, w_value, w_out, small,
        scratch=[
            pltpu.VMEM((4, 4, 4, 2, 16, WIDE), BF),
            pltpu.SemaphoreType.DMA((31,)),
            pltpu.SemaphoreType.DMA((31,)),
        ],
        collective_id=1,
    )
    heads = exchanged(packed)
    smem = pl.BlockSpec(memory_space=pltpu.SMEM)
    vmem = pl.BlockSpec(memory_space=pltpu.VMEM)
    attn_scratch = [
        pltpu.VMEM((SEQ, 256), BF),
        pltpu.VMEM((EXPERTS, TOK, 256), BF),
        pltpu.VMEM((12 * TS, TOK), F32),
    ]
    attended, lse = call(
        attn_fwd_kernel,
        (shape((EXPERTS, TS, 128), BF), shape((EXPERTS, 8, TOK), F32)),
        lengths, table, heads,
        in_specs=[smem, vmem, vmem],
        scratch=attn_scratch + [pltpu.VMEM((128, SEQ), BF)],
    )
    att_back = exchanged(attended)
    att, hidden, mixed, share, send = call(
        mid_kernel,
        (
            shape((TOK, D), BF), shape((TOK, D), F32), shape((TOK, D), BF),
            shape((TOK, 128), F32), shape((BUF, 2 * D), BF),
        ),
        att_back, x, wo, gains, wr, picked, place, dy,
    )
    received = exchanged(send.reshape(EXPERTS, 2 * CAP, 2 * D)).reshape(BUF, 2 * D)
    expert_out, expert_grads = pl.pallas_call(
        expert_kernel,
        grid=(FSDP // 2,),
        out_shape=(shape((BUF, 2 * D), BF), shape((FSDP, 3 * SHARD, D), BF)),
        in_specs=[
            pl.BlockSpec((BUF, 2 * D), lambda i: (0, 0)),
            pl.BlockSpec((2, 3 * SHARD, D), lambda i: (i, 0, 0)),
        ],
        out_specs=(
            pl.BlockSpec((BUF, 2 * D), lambda i: (0, 0)),
            pl.BlockSpec((2, 3 * SHARD, D), lambda i: (i, 0, 0)),
        ),
        scratch_shapes=[pltpu.VMEM((BUF, D), F32), pltpu.VMEM((BUF, D), F32)],
        compiler_params=pltpu.CompilerParams(vmem_limit_bytes=VMEM_LIMIT),
    )(received, expert_w)
    expert_sum = lax.psum_scatter(
        expert_grads.reshape(FSDP * 3 * SHARD, D), "fsdp", scatter_dimension=0, tiled=True
    ).astype(F32)
    returned = exchanged(expert_out.reshape(EXPERTS, 2 * CAP, 2 * D)).reshape(BUF, 2 * D)
    result, hgrad, branch, att_grad, router_grad, moe_gain_grad = call(
        back_kernel,
        (
            shape((TOK, D), BF), shape((TOK, D), F32), shape((TOK, D), BF),
            shape((H, TS, 128), BF), shape((D, 128), F32), shape((8, D), F32),
        ),
        returned, place, place_t, dy, hidden, mixed, share, wr, gains, wo,
    )
    head_grads = exchanged(att_grad)
    qkv_grads, table_grad = call(
        attn_bwd_kernel,
        (shape((EXPERTS, 3 * TS, 128), BF), shape((8, 128), F32)),
        lengths, table, heads, head_grads, lse,
        in_specs=[smem, vmem, vmem, vmem, vmem],
        scratch=attn_scratch
        + [
            pltpu.VMEM((144, SEQ), BF),
            pltpu.VMEM((SEQ, 128), F32),
            pltpu.VMEM((SEQ, 128), F32),
            pltpu.VMEM((2 * TS, TOK), F32),
            pltpu.VMEM((8, TOK), F32),
        ],
    )
    token_grads = exchanged(qkv_grads)
    half_a, half_b = 1152, 1024
    input_grad, gq, gk, gv, go, small_grad = call(
        final_kernel,
        (
            shape((TOK, D), BF), shape((8, D), F32), shape((8, D), F32), shape((8, D), F32),
            shape((8, D), F32), shape((16, 128), F32),
        ),
        token_grads, normed, x, gains, hgrad, wq, wk, wv, att, branch, router_grad, moe_gain_grad, table_grad,
        scratch=[
            pltpu.VMEM((TOK, D), BF), pltpu.VMEM((TOK, D), BF), pltpu.VMEM((TOK, D), BF),
            pltpu.VMEM((4, 4, 4, 2, 16, WIDE), BF),
            pltpu.VMEM((4, 4, 4, 16, WIDE), BF),
            pltpu.VMEM((3, 4, 4, 16, half_a), BF), pltpu.VMEM((3, 4, 4, 16, half_b), BF),
            pltpu.VMEM((4, 4, 16, half_a), BF), pltpu.VMEM((4, 4, 16, half_b), BF),
            pltpu.VMEM((3, 4, 16, half_a), BF), pltpu.VMEM((3, 4, 16, half_b), BF),
            pltpu.VMEM((4, 16, half_a), BF), pltpu.VMEM((4, 16, half_b), BF),
            pltpu.VMEM((3, 16, half_a), BF), pltpu.VMEM((3, 16, half_b), BF),
            pltpu.SemaphoreType.DMA((22,)),
            pltpu.SemaphoreType.DMA((22,)),
        ],
        collective_id=2,
    )
    return (
        result.reshape(tokens.shape),
        input_grad.reshape(tokens.shape),
        small_grad[8, :8],
        gq,
        gk,
        gv,
        go,
        small_grad[10, :4],
        small_grad[9, :8],
        small_grad[:8, :EXPERTS],
        expert_sum[:SHARD].T[None],
        expert_sum[SHARD : 2 * SHARD].T[None],
        expert_sum[2 * SHARD :][None],
    )


def solution(mesh):
    row = P(None, "fsdp", "expert", None)
    flat = P(("expert", "fsdp"))
    matrix = P(("expert", "fsdp"), None)
    columns = P("expert", None, "fsdp")
    deep = P("expert", "fsdp", None)
    return jax.shard_map(
        on_device,
        mesh=mesh,
        in_specs=(
            row, row, P(None, "fsdp", None), row, row, flat, matrix, matrix, matrix, matrix,
            flat, flat, matrix, columns, columns, deep,
        ),
        out_specs=(
            row, row, flat, matrix, matrix, matrix, matrix, flat, flat, matrix, columns, columns, deep,
        ),
        check_vma=False,
    )
```

```python
import jax
import jax.numpy as jnp
from jax import lax
from jax.experimental import pallas as pl
from jax.experimental.pallas import tpu as pltpu
from jax.sharding import PartitionSpec as P

H = 16
HD = 64
NB = 32
D = 1024
FF = 2816
WINDOW = 1024
EXPERTS = 16
CAP = 20
TS = 128
FSDP = 8
SHARD = FF // FSDP
TOK = 2 * TS
BUF = EXPERTS * 2 * CAP
SEQ = EXPERTS * TS
EPS = 1e-06
MASKED = -1e30
EDGES = tuple(range(1, 17)) + (19, 21, 24, 27, 31, 35, 40, 46, 52, 59, 67, 77, 87, 99, 113)
GELU_C = 0.7978845608028654
BF = jnp.bfloat16
F32 = jnp.float32
VMEM_LIMIT = 58 * 1024 * 1024


def nn(left, right):
    return lax.dot_general(left, right, (((1,), (0,)), ((), ())), preferred_element_type=F32)


def nt(left, right):
    return lax.dot_general(left, right, (((1,), (1,)), ((), ())), preferred_element_type=F32)


def tn(left, right):
    return lax.dot_general(left, right, (((0,), (0,)), ((), ())), preferred_element_type=F32)


def halves(value):
    high = value.astype(BF)
    return high, (value - high.astype(F32)).astype(BF)


def call(kernel, out_shape, *args, scratch=(), in_specs=None, out_specs=None, collective_id=None):
    return pl.pallas_call(
        kernel,
        out_shape=out_shape,
        in_specs=in_specs or [pl.BlockSpec(memory_space=pltpu.VMEM)] * len(args),
        out_specs=out_specs or jax.tree.map(lambda _: pl.BlockSpec(memory_space=pltpu.VMEM), out_shape),
        scratch_shapes=list(scratch),
        compiler_params=pltpu.CompilerParams(
            vmem_limit_bytes=VMEM_LIMIT,
            collective_id=collective_id,
            has_side_effects=collective_id is not None,
        ),
    )(*args)


def shape(dims, dtype):
    return jax.ShapeDtypeStruct(dims, dtype)


def lane_half(dims):
    return lax.broadcasted_iota(jnp.int32, dims, 1) % 128 < HD


def pack_pair(first, second):
    left = lane_half(first.shape)
    return (
        jnp.where(left, first, pltpu.roll(second, HD, 1)).astype(BF),
        jnp.where(left, pltpu.roll(first, HD, 1), second).astype(BF),
    )


MESH = pl.DeviceIdType.MESH
HALF = D // 2
WIDE = 4 * HALF + 128
GATHER_PARTS = ((pl.ds(0, 896), "xzy"), (pl.ds(896, 896), "xyz"), (pl.ds(1792, 384), "zyx"))
REDUCE_PARTS = ((pl.ds(0, 768), "zyx"), (pl.ds(768, 768), "yzx"), (pl.ds(1536, 640), "xyz"))


def coords():
    e, f = lax.axis_index("expert"), lax.axis_index("fsdp")
    return lax.div(e, 4), lax.rem(e, 4), lax.div(f, 2), lax.rem(f, 2)


def device(z, y, x, c):
    return (z * 4 + y, x * 2 + c)


def ring(at, step):
    return lax.rem(at + step, 4)


def greet(peers):
    barrier = pltpu.get_barrier_semaphore()
    for peer in peers:
        pl.semaphore_signal(barrier, inc=1, device_id=peer, device_id_type=MESH)
    pl.semaphore_wait(barrier, len(peers))


class Copies:
    def __init__(self, send_sem, recv_sem):
        self.send_sem, self.recv_sem, self.started = send_sem, recv_sem, []

    def go(self, src, dst, peer):
        at = len(self.started)
        copy = pltpu.make_async_remote_copy(
            src_ref=src,
            dst_ref=dst,
            send_sem=self.send_sem.at[at],
            recv_sem=self.recv_sem.at[at],
            device_id=peer,
            device_id_type=MESH,
        )
        copy.start()
        self.started.append(copy)
        return copy

    def drain(self):
        for copy in self.started:
            copy.wait_send()


def plane_peers():
    e, f = lax.axis_index("expert"), lax.axis_index("fsdp")
    return [(lax.rem(e + k, EXPERTS), f) for k in range(1, EXPERTS)]


class Exchange:
    def __init__(self, held, landed, send_sem, recv_sem, rows=None):
        self.held, self.landed, self.send_sem, self.recv_sem = held, landed, send_sem, recv_sem
        self.rows = rows or pl.ds(0, held.shape[1])
        self.me, self.f = lax.axis_index("expert"), lax.axis_index("fsdp")

    def copy(self, to):
        step = lax.rem(to - self.me + EXPERTS, EXPERTS)
        return pltpu.make_async_remote_copy(
            src_ref=self.held.at[to, self.rows],
            dst_ref=self.landed.at[self.me, self.rows],
            send_sem=self.send_sem.at[step],
            recv_sem=self.recv_sem.at[step],
            device_id=(to, self.f),
            device_id_type=MESH,
        )

    def others(self, act):
        def body(k, carry):
            act(self.copy(lax.rem(self.me + k, EXPERTS)))
            return carry

        lax.fori_loop(1, EXPERTS, body, 0)

    def keep(self):
        self.landed[self.me, self.rows] = self.held[self.me, self.rows]

    def push(self, to):
        @pl.when(to != self.me)
        def _():
            self.copy(to).start()

        @pl.when(to == self.me)
        def _():
            self.keep()

    def start(self):
        self.others(lambda copy: copy.start())
        self.keep()

    def arrive(self):
        self.others(lambda copy: copy.wait_recv())

    def drain(self):
        self.others(lambda copy: copy.wait_send())


def spread(value):
    half = D // 2
    parts = [value[:, at : at + half].reshape(EXPERTS, 2 * CAP, half) for at in (0, half)]
    return jnp.concatenate(parts, axis=1).astype(BF)


def unspread(ref, into):
    half = D // 2
    value = ref[...].astype(F32)
    for side in range(2):
        part = value[:, side * 2 * CAP : (side + 1) * 2 * CAP, :].reshape(BUF, half)
        into[:, side * half : (side + 1) * half] = part.astype(BF)


class Place:
    def __init__(self):
        self.z, self.y, self.x, self.c = coords()
        self.at = {"z": self.z, "y": self.y, "x": self.x}
        self.twin = device(self.z, self.y, self.x, 1 - self.c)

    def moved(self, axis, step):
        return {**self.at, axis: ring(self.at[axis], step)}

    def peer(self, axis, step):
        to = self.moved(axis, step)
        return device(to["z"], to["y"], to["x"], self.c)

    def peers(self, axes):
        return [self.peer(axis, k) for axis in axes for k in (1, 2, 3)]


class Gather:
    def __init__(self, place, box, copies, lanes, order):
        self.place, self.box, self.copies, self.lanes, self.order = place, box, copies, lanes, order
        self.phases, self.forwards = [], []

    def region(self, known, at):
        spots = tuple(slice(None) if axis in known else at[axis] for axis in "zyx")
        return self.box.at[spots + (self.place.c, slice(None), self.lanes)]

    def start(self, phase):
        axis, known = self.order[phase], self.order[:phase]
        here = self.region(known, self.place.at)
        self.phases.append([self.copies.go(here, here, self.place.peer(axis, k)) for k in (1, 2, 3)])

    def forward_own(self):
        here = self.region("", self.place.at)
        self.forwards.append(self.copies.go(here, here, self.place.twin))

    def forward(self, phase, k):
        axis, known = self.order[phase], self.order[:phase]
        got = self.region(known, self.place.moved(axis, 4 - k))
        self.forwards.append(self.copies.go(got, got, self.place.twin))

    def arrive(self, phase, forward=False):
        for k, copy in enumerate(self.phases[phase]):
            copy.wait_recv()
            if forward:
                self.forward(phase, k + 1)

    def forward_all(self, phase):
        for k in (1, 2, 3):
            self.forward(phase, k)

    def finish(self):
        for copy in self.forwards:
            copy.wait_recv()


class Reduce:
    def __init__(self, place, copies, order, first, held, landed):
        self.place, self.copies, self.order = place, copies, order
        self.sources, self.landed, self.started = [first] + list(held), landed, [[], [], []]

    def pick(self, phase, spot):
        left = [axis for axis in "zyx" if axis in self.order[phase:]]
        return tuple(spot if axis == self.order[phase] else slice(None) for axis in left)

    def send(self, phase, k):
        axis = self.order[phase]
        src, lanes = self.sources[phase]
        spots = self.pick(phase, ring(self.place.at[axis], k))
        src = src.at[spots + (slice(None), lanes)]
        self.started[phase].append(
            self.copies.go(src, self.landed[phase].at[k - 1], self.place.peer(axis, k))
        )

    def start(self, phase):
        for k in (1, 2, 3):
            self.send(phase, k)

    def total(self, phase):
        for copy in self.started[phase]:
            copy.wait_recv()
        src, lanes = self.sources[phase]
        spots = self.pick(phase, self.place.at[self.order[phase]])
        value = src[spots + (slice(None), lanes)].astype(F32)
        for k in range(3):
            value = value + self.landed[phase][k].astype(F32)
        if phase < 2:
            nxt, width = self.sources[phase + 1]
            nxt[...] = value.astype(BF)
        return value


def reduce_scratch(width):
    return [
        pltpu.VMEM((4, 4, 16, width), BF), pltpu.VMEM((4, 16, width), BF),
        pltpu.VMEM((3, 4, 4, 16, width), BF), pltpu.VMEM((3, 4, 16, width), BF), pltpu.VMEM((3, 16, width), BF),
    ]


def folded(value):
    return jnp.concatenate([value[:, : D // 2], value[:, D // 2 :]], axis=0)


def unfolded(value):
    return jnp.concatenate([value[:8], value[8:]], axis=1)


def fold_rows(value):
    half = D // 2
    return jnp.concatenate(
        [value[:, at : at + half].reshape(32, 8, half) for at in (0, half)], axis=1
    )


def unfold_into(ref, plane, value):
    half = D // 2
    rows = slice(plane * 256, plane * 256 + 256)
    ref[rows, :half] = value[:, :8, :].reshape(256, half).astype(BF)
    ref[rows, half:] = value[:, 8:, :].reshape(256, half).astype(BF)


def lane_pick():
    col = lax.broadcasted_iota(jnp.int32, (128, D), 1)
    return (lax.rem(col, 8) == lax.broadcasted_iota(jnp.int32, (128, D), 0)).astype(BF)


def own_columns():
    col = lax.broadcasted_iota(jnp.int32, (128, D), 1)
    low = lax.broadcasted_iota(jnp.int32, (128, D), 0) * 8
    return (col >= low) & (col < low + 8)


def by_device(row):
    high, low = halves(jnp.where(own_columns(), row, 0.0))
    pick = lane_pick()
    return nt(high, pick) + nt(low, pick)


def pick_row(values, row):
    at = lax.broadcasted_iota(jnp.int32, values.shape, values.ndim - 2)
    return jnp.sum(jnp.where(at == row, values, 0.0), axis=-2)


def gather_kernel(
    x_ref, wq_ref, wk_ref, wv_ref, wo_ref, small_ref,
    normed_ref, land_ref, wq_out, wk_out, wv_out, wo_out, wr_out, gain_out, tab_out,
    box, out_ref, send_sem, recv_sem, trade_send, trade_recv,
):
    place = Place()
    z, y, x, c = place.z, place.y, place.x, place.c
    for k, w_ref in enumerate((wq_ref, wk_ref, wv_ref, wo_ref)):
        box[z, y, x, c, :, k * HALF : (k + 1) * HALF] = folded(w_ref[...].astype(F32)).astype(BF)
    box[z, y, x, c, :, 4 * HALF :] = small_ref[...]
    greet(plane_peers() + place.peers("x") + [place.twin])
    copies = Copies(send_sem, recv_sem)
    trade = Exchange(out_ref, land_ref, trade_send, trade_recv)
    both = [Gather(place, box, copies, lanes, order) for lanes, order in GATHER_PARTS]
    for part in both:
        part.start(0)
    for part in both:
        part.forward_own()
    tokens = x_ref[...].astype(F32)
    unit = tokens * lax.rsqrt(jnp.mean(tokens * tokens, axis=-1, keepdims=True) + EPS)
    for phase in (0, 1):
        for part in both:
            part.arrive(phase)
            part.start(phase + 1)
        for part in both:
            part.forward_all(phase)
    for part in both:
        part.arrive(2, forward=True)
    for part in both:
        part.finish()

    def unfold(k, w_out):
        for plane in range(4):
            value = box[plane, :, :, :, :, k * HALF : (k + 1) * HALF].reshape(32, 16, HALF)
            unfold_into(w_out, plane, value.astype(F32))

    for k, w_out in enumerate((wq_out, wk_out, wv_out)):
        unfold(k, w_out)
    small = box[:, :, :, :, :, 4 * HALF :].reshape(128, 16, 128).astype(F32)
    lane = lax.broadcasted_iota(jnp.int32, (D, 128), 1)
    wr_out[...] = jnp.where(lane < EXPERTS, small[:, :8, :].reshape(D, 128), 0.0).astype(BF)
    pick, mine = lane_pick(), own_columns()
    gains = [
        jnp.sum(jnp.where(mine, nn(pick_row(small[:, 8:, :], row).astype(BF), pick), 0.0), axis=0, keepdims=True)
        for row in range(2)
    ]
    gain_out[...] = jnp.concatenate(gains + [jnp.zeros((6, D), F32)], axis=0)
    near = box[z, y, :, :, :, 4 * HALF :].reshape(8, 16, 128).astype(F32)
    tab_out[...] = pick_row(near, 10)

    normed = (unit * gains[0]).astype(BF)
    normed_ref[...] = normed
    for k in (1, 2, 3, 0):
        part = ring(z, k)
        for which, w_ref in enumerate((wq_out, wk_out, wv_out)):
            res = nn(normed, w_ref[:, pl.ds(pl.multiple_of(part * 256, 256), 256)])
            for pair in range(2):
                head = part * 4 + pair * 2
                cols = slice(pair * 128, pair * 128 + 128)
                first, second = pack_pair(res[:TS, cols], res[TS:, cols])
                out_ref[head, which * TS : (which + 1) * TS, :] = first
                out_ref[head + 1, which * TS : (which + 1) * TS, :] = second
        for j in (1, 2, 3, 0):
            if k or j:
                trade.copy(part * 4 + ring(y, j)).start()
            else:
                trade.keep()
    unfold(3, wo_out)
    trade.arrive()
    trade.drain()
    copies.drain()


def attn_setup(len_ref, tab_ref, recv_ref, kext, qext, bias):
    rows = lax.broadcasted_iota(jnp.int32, (SEQ, 128), 0)
    lanes = lax.broadcasted_iota(jnp.int32, (SEQ, 128), 1)
    end1 = [len_ref[m, 0] for m in range(2)]
    end2 = [len_ref[m, 0] + len_ref[m, 1] for m in range(2)]
    kfeat = jnp.where(lanes == 4, 1.0, 0.0)
    for m in range(2):
        kfeat = jnp.where((lanes == 2 * m) & (rows < end1[m]), 1.0, kfeat)
        kfeat = jnp.where((lanes == 2 * m + 1) & (rows < end2[m]), 1.0, kfeat)
    kext[:, 128:] = kfeat.astype(BF)
    for i in range(EXPERTS):
        kext[i * TS : (i + 1) * TS, :128] = recv_ref[i, TS : 2 * TS, :]
    left = lane_half((TS, 128))
    row_in = lax.broadcasted_iota(jnp.int32, (TS, 128), 0)
    lane_in = lax.broadcasted_iota(jnp.int32, (TS, 128), 1)
    for i in range(EXPERTS):
        q2 = recv_ref[i, 0:TS, :].astype(F32) * (HD**-0.5)
        pos = row_in + i * TS
        for m in range(2):
            keep = left if m == 0 else jnp.logical_not(left)
            qext[i, m * TS : (m + 1) * TS, :128] = jnp.where(keep, q2, 0.0).astype(BF)
            feat = jnp.where((lane_in == 2 * m) & (pos >= end1[m]), MASKED, 0.0)
            feat = jnp.where((lane_in == 2 * m + 1) & (pos >= end2[m]), MASKED, feat)
            qext[i, m * TS : (m + 1) * TS, 128:] = feat.astype(BF)
    for block in range(12):
        dist = 1024 - block * TS + lane_in - row_in
        if block in (7, 8):
            value = jnp.broadcast_to(tab_ref[0:1, 0:1], (TS, 128))
            for bucket, edge in enumerate(EDGES):
                b = bucket + 1
                value = jnp.where(dist >= edge, tab_ref[b // 4 : b // 4 + 1, b % 4 : b % 4 + 1], value)
        else:
            value = jnp.broadcast_to(tab_ref[7:8, 3:4], (TS, 128))
        value = jnp.where((dist >= 0) & (dist < WINDOW), value, MASKED)
        bias[block * TS : (block + 1) * TS, :128] = value
        bias[block * TS : (block + 1) * TS, 128:] = value


def eye(size):
    return (
        lax.broadcasted_iota(jnp.int32, (size, size), 0)
        == lax.broadcasted_iota(jnp.int32, (size, size), 1)
    ).astype(BF)


def loop(strip, low, high, count):
    def body(i, carry):
        strip(i, count, i - 8 if count == 9 else 0)
        return carry

    lax.fori_loop(low, high, body, 0)


def span(block, count):
    return pl.ds(pl.multiple_of(block * TS, TS), count * TS)


def attn_fwd_kernel(
    len_ref, tab_ref, recv_ref, land_ref, lse_ref, kext, qext, bias, vt, out_ref, send_sem, recv_sem
):
    greet(plane_peers())
    trade = Exchange(out_ref, land_ref, send_sem, recv_sem)
    attn_setup(len_ref, tab_ref, recv_ref, kext, qext, bias)
    unit = eye(TS)
    for i in range(EXPERTS):
        vt[:, i * TS : (i + 1) * TS] = nt(unit, recv_ref[i, 2 * TS : 3 * TS, :]).astype(BF)

    def strip(i, count, first):
        s = nt(kext[span(first, count), :], qext[i]) + bias[span(first - i + 8, count), :]
        top = jnp.max(s, axis=0, keepdims=True)
        p = jnp.exp(s - top)
        total = jnp.sum(p, axis=0, keepdims=True)
        res = nn(vt[:, span(first, count)], p.astype(BF)) / total
        both = jnp.concatenate([res[:HD, :TS], res[HD:, TS:]], axis=0)
        out_ref[i] = both.T.astype(BF)
        lse_ref[i] = jnp.broadcast_to(top + jnp.log(total), (8, TOK))
        trade.push(i)

    loop(strip, 0, 4, 4)
    loop(strip, 4, 8, 8)
    loop(strip, 8, 16, 9)
    trade.arrive()
    trade.drain()


def attn_bwd_kernel(
    len_ref, tab_ref, recv_ref, dout_ref, lse_ref, land_ref, tab_out_ref,
    kext, qext, bias, ktext, dk, dv, near, far, out_ref, *sems,
):
    greet(plane_peers())
    trade_q = Exchange(out_ref, land_ref, sems[0], sems[1], pl.ds(0, TS))
    trade_kv = Exchange(out_ref, land_ref, sems[2], sems[3], pl.ds(TS, 2 * TS))
    attn_setup(len_ref, tab_ref, recv_ref, kext, qext, bias)
    unit = eye(256)
    for i in range(EXPERTS):
        ktext[:, i * TS : (i + 1) * TS] = nt(unit, kext[i * TS : (i + 1) * TS, :])[:144].astype(BF)
    dk[...] = jnp.zeros_like(dk)
    dv[...] = jnp.zeros_like(dv)
    near[...] = jnp.zeros_like(near)
    far[...] = jnp.zeros_like(far)
    left = lane_half((TS, 128))

    def strip(i, count, first):
        q = qext[i]
        s = nt(kext[span(first, count), :], q) + bias[span(first - i + 8, count), :]
        p = jnp.exp(s - lse_ref[i][0:1])
        do2 = dout_ref[i]
        zero = jnp.zeros_like(do2)
        do = jnp.concatenate([jnp.where(left, do2, zero), jnp.where(left, zero, do2)], axis=0)
        if count == 9:
            v = recv_ref[pl.ds(first, count), 2 * TS : 3 * TS, :].reshape(count * TS, 128)
        else:
            v = recv_ref[0:count, 2 * TS : 3 * TS, :].reshape(count * TS, 128)
        dp = nt(v, do)
        inner = jnp.sum(p * dp, axis=0, keepdims=True)
        ds = (p * (dp - inner)).astype(BF)
        dv[span(first, count), :] += nn(p.astype(BF), do)
        dk[span(first, count), :] += nn(ds, q[:, :128])
        dqt = nn(ktext[:, span(first, count)], ds)
        both = jnp.concatenate([dqt[:HD, :TS], dqt[HD : 2 * HD, TS:]], axis=0) * (HD**-0.5)
        out_ref[i, 0:TS, :] = both.T.astype(BF)
        trade_q.push(i)
        far[...] += dqt[128:136]
        if count == 9:
            near[...] += ds[7 * TS :].astype(F32)
        else:
            nearby.append(ds)

    nearby = []

    def finish(block):
        out_ref[block, TS : 2 * TS, :] = dk[span(block, 1), :].astype(BF)
        out_ref[block, 2 * TS :, :] = dv[span(block, 1), :].astype(BF)
        trade_kv.push(block)

    def sweep(low, high, count):
        def body(i, carry):
            nearby.clear()
            first = i - 8 if count == 9 else 0
            strip(i, count, first)
            if count == 9:
                finish(first)
            else:
                ds = nearby[0]
                for block in range(count):
                    value = ds[block * TS : (block + 1) * TS].astype(F32)

                    @pl.when(i == block)
                    def _(value=value):
                        near[TS:] += value

                    @pl.when(i == block + 1)
                    def _(value=value):
                        near[:TS] += value

            return carry

        lax.fori_loop(low, high, body, 0)

    sweep(0, 4, 4)
    sweep(4, 8, 8)
    sweep(8, 16, 9)

    def rest(block, carry):
        finish(block)
        return carry

    lax.fori_loop(8, EXPERTS, rest, 0)
    grads = near[:, :TS] + near[:, TS:]
    dist = (
        TS
        + lax.broadcasted_iota(jnp.int32, (TOK, TS), 1)
        - lax.broadcasted_iota(jnp.int32, (TOK, TS), 0)
    )
    total = jnp.sum(far[4:5, :])
    lane = lax.broadcasted_iota(jnp.int32, (8, 128), 1)
    lane = jnp.where(lane < 4, lane + 4 * lax.broadcasted_iota(jnp.int32, (8, 128), 0), NB)
    res = jnp.zeros((8, 128), F32)
    lows = (0,) + EDGES
    seen = 0.0
    for b in range(NB - 1):
        part = jnp.sum(jnp.where((dist >= lows[b]) & (dist < lows[b + 1]), grads, 0.0))
        seen = seen + part
        res = jnp.where(lane == b, part, res)
    res = jnp.where(lane == NB - 1, total - seen, res)
    tab_out_ref[...] = res
    for trade in (trade_q, trade_kv):
        trade.arrive()
        trade.drain()


def row_expert():
    row = lax.broadcasted_iota(jnp.int32, (BUF, 128), 0)
    lane = lax.broadcasted_iota(jnp.int32, (BUF, 128), 1) * (2 * CAP)
    return (row >= lane) & (row < lane + 2 * CAP)


def unpack_heads(recv_ref, lo, emit):
    for pair in range(H // 2):
        one = recv_ref[2 * pair, lo : lo + TS, :].astype(F32)
        two = recv_ref[2 * pair + 1, lo : lo + TS, :].astype(F32)
        first, second = pack_pair(one, two)
        emit(pair, first, second)


def slot_share(place, share_e, own):
    high, low = halves(share_e)
    return jnp.sum(jnp.where(own, nn(place, high) + nn(place, low), 0.0), axis=1, keepdims=True)


FFC = 2 * SHARD
STEPS = FF // FFC


def moe_kernel(
    recv_ref, x_ref, wo_ref, gain_ref, wr_ref, mask_ref, place_ref, dy_ref, w_ref,
    att_ref, hidden_ref, mixed_ref, share_ref, back_out, back_row, grads_ref,
    w_buf, hold_a, hold_b, land_a, land_b, rows, slots, act, first, second, acc, stage,
    w_sem, stage_sem, *sems,
):
    def load(step):
        slot = lax.rem(step, 2)
        return pltpu.make_async_copy(w_ref.at[pl.ds(step * 2, 2)], w_buf.at[slot], w_sem.at[slot])

    load(0).start()
    load(1).start()
    greet(plane_peers())
    to_rows = Exchange(hold_a, land_a, sems[0], sems[1])
    to_slots = Exchange(hold_b, land_b, sems[2], sems[3])
    from_out = Exchange(hold_a, back_out, sems[4], sems[5])
    from_row = Exchange(hold_b, back_row, sems[6], sems[7])

    def emit(pair, one, two):
        att_ref[0:TS, pair * 128 : pair * 128 + 128] = one
        att_ref[TS:, pair * 128 : pair * 128 + 128] = two

    unpack_heads(recv_ref, 0, emit)
    hidden = x_ref[...].astype(F32) + nn(att_ref[...], wo_ref[...])
    hidden_ref[...] = hidden
    factor = lax.rsqrt(jnp.mean(hidden * hidden, axis=-1, keepdims=True) + EPS)
    mixed = (hidden * factor * gain_ref[1:2, :]).astype(BF)
    mixed_ref[...] = mixed
    place = place_ref[...]
    hold_a[...] = spread(nn(place, mixed))
    to_rows.start()
    picked = mask_ref[...] > 0
    logits = jnp.where(picked, nn(mixed, wr_ref[...]), MASKED)
    weight = jnp.exp(logits - jnp.max(logits, axis=1, keepdims=True))
    share = weight / jnp.sum(weight, axis=1, keepdims=True)
    share_ref[...] = share
    hold_b[...] = spread(slot_share(place, share, row_expert()) * nn(place, dy_ref[...]))

    to_rows.arrive()
    to_slots.start()
    unspread(land_a, rows)
    acc[...] = jnp.zeros_like(acc)

    def weights(step):
        w = w_buf[lax.rem(step, 2)]
        return [w[:, k * SHARD : (k + 1) * SHARD, :].reshape(FFC, D) for k in range(3)]

    def forward(step, carry):
        load(step).wait()
        gate_w, up_w, down_w = weights(step)
        gate = nt(rows[...], gate_w)
        up = nt(rows[...], up_w)
        square = gate * gate
        tanh = jnp.tanh(GELU_C * gate * (1.0 + 0.044715 * square))
        half_up = 0.5 * (1.0 + tanh)
        gelu = gate * half_up
        slope = half_up + 0.5 * gate * (1.0 - tanh * tanh) * (
            GELU_C * (1.0 + 3 * 0.044715 * square)
        )
        acted = (gelu * up).astype(BF)
        act[step] = acted
        first[step] = (up * slope).astype(BF)
        second[step] = gelu.astype(BF)
        acc[...] += nn(acted, down_w)

        @pl.when(step < STEPS - 2)
        def _():
            load(step + 2).start()

        return carry

    lax.fori_loop(0, STEPS, forward, 0)
    to_rows.drain()
    hold_a[...] = spread(acc[...])
    from_out.start()
    to_slots.arrive()
    unspread(land_b, slots)
    acc[...] = jnp.zeros_like(acc)

    def backward(at, carry):
        step = STEPS - 1 - at

        @pl.when(at >= 2)
        def _():
            load(step).wait()

        gate_w, up_w, down_w = weights(step)
        act_grad = nt(slots[...], down_w).astype(BF).astype(F32)
        gate_grad = (act_grad * first[step].astype(F32)).astype(BF)
        up_grad = (act_grad * second[step].astype(F32)).astype(BF)
        first[step] = gate_grad
        second[step] = up_grad
        acc[...] += nn(gate_grad, gate_w) + nn(up_grad, up_w)

        @pl.when(at < 2)
        def _():
            load(step - 2).start()

        return carry

    lax.fori_loop(0, STEPS, backward, 0)
    to_slots.drain()
    hold_b[...] = spread(acc[...])
    from_row.start()

    def store(step, which):
        return pltpu.make_async_copy(
            stage.at[which],
            grads_ref.at[pl.ds(step * 2, 2), pl.ds(which * SHARD, SHARD)],
            stage_sem.at[which],
        )

    def weight_grads(step, carry):
        for which, (left, right) in enumerate(((first, rows), (second, rows), (act, slots))):
            value = tn(left[step], right[...]).astype(BF).reshape(2, SHARD, D)

            @pl.when(step > 0)
            def _(which=which):
                store(step - 1, which).wait()

            stage[which] = value
            store(step, which).start()
        return carry

    lax.fori_loop(0, STEPS, weight_grads, 0)
    for which in range(3):
        store(STEPS - 1, which).wait()
    from_out.arrive()
    from_row.arrive()
    from_out.drain()
    from_row.drain()


def back_kernel(
    out_ref, row_ref, place_ref, place_t_ref, dy_ref, hidden_ref, mixed_ref, share_ref, wr_ref, gain_ref, wo_ref,
    result_ref, hgrad_ref, branch_ref, land_ref, router_ref, gain_out_ref,
    send_ref, outs, rows, send_sem, recv_sem,
):
    greet(plane_peers())
    z, y, _, _ = coords()
    trade = Exchange(send_ref, land_ref, send_sem, recv_sem)
    unspread(out_ref, outs)
    unspread(row_ref, rows)
    place = place_ref[...]
    place_t = place_t_ref[...]
    own = row_expert()
    dy = dy_ref[...]
    returned = outs[...]
    dots = jnp.sum(nn(place, dy) * returned.astype(F32), axis=1, keepdims=True)
    high, low = halves(jnp.where(own, dots, 0.0))
    share = share_ref[...]
    share_grad = nn(place_t, high) + nn(place_t, low)
    inner = jnp.sum(share * share_grad, axis=1, keepdims=True)
    lg_high, lg_low = halves(share * (share_grad - inner))
    wr = wr_ref[...]
    mixed_grad = nn(place_t, rows[...]) + (nt(lg_high, wr) + nt(lg_low, wr))
    hidden = hidden_ref[...]
    factor = lax.rsqrt(jnp.mean(hidden * hidden, axis=-1, keepdims=True) + EPS)
    unit = hidden * factor
    gain_out_ref[...] = jnp.broadcast_to(jnp.sum(mixed_grad * unit, axis=0, keepdims=True), (8, D))
    scaled = mixed_grad * gain_ref[1:2, :]
    hgrad = dy.astype(F32) + factor * (
        scaled - unit * jnp.mean(scaled * unit, axis=-1, keepdims=True)
    )
    hgrad_ref[...] = hgrad
    branch = hgrad.astype(BF)
    branch_ref[...] = branch
    for k in (1, 2, 3, 0):
        part = ring(z, k)
        res = nt(branch, wo_ref[pl.ds(pl.multiple_of(part * 256, 256), 256), :])
        for pair in range(2):
            head = part * 4 + pair * 2
            cols = slice(pair * 128, pair * 128 + 128)
            one, two = pack_pair(res[:TS, cols], res[TS:, cols])
            send_ref[head] = one
            send_ref[head + 1] = two
        for j in (1, 2, 3, 0):
            if k or j:
                trade.copy(part * 4 + ring(y, j)).start()
            else:
                trade.keep()
    mixed = mixed_ref[...]
    router_ref[...] = tn(mixed, lg_high) + tn(mixed, lg_low)
    scale_high, scale_low = halves(
        place_t.astype(F32) * slot_share(place, share, own).T
    )
    moe = nn(scale_high, returned) + nn(scale_low, returned)
    result_ref[...] = (hidden + moe).astype(BF)
    trade.arrive()
    trade.drain()


def final_kernel(
    recv_ref, normed_ref, x_ref, gains_ref, hgrad_ref, wq_ref, wk_ref, wv_ref,
    att_ref, branch_ref, router_ref, moe_gain_ref, table_ref, igrad_ref, sum_ref,
    flat_q, flat_k, flat_v, box, from_twin, *rest,
):
    place = Place()
    z, y, c = place.z, place.y, place.c
    greet(place.peers("xyz") + [place.twin])
    copies = Copies(rest[15], rest[16])
    parts = [
        Reduce(
            place, copies, order, (from_twin, lanes),
            [(bufs[0], pl.ds(0, lanes.size)), (bufs[1], pl.ds(0, lanes.size))], bufs[2:],
        )
        for (lanes, order), bufs in zip(REDUCE_PARTS, (rest[0:5], rest[5:10], rest[10:15]))
    ]
    flats = (flat_q, flat_k, flat_v)
    for which, flat in enumerate(flats):

        def emit(pair, first, second):
            flat[0:TS, pair * 128 : pair * 128 + 128] = first
            flat[TS:, pair * 128 : pair * 128 + 128] = second

        unpack_heads(recv_ref, which * TS, emit)

    total = nt(flat_q[...], wq_ref[...]) + nt(flat_k[...], wk_ref[...]) + nt(flat_v[...], wv_ref[...])
    tokens = x_ref[...].astype(F32)
    factor = lax.rsqrt(jnp.mean(tokens * tokens, axis=-1, keepdims=True) + EPS)
    unit = tokens * factor

    at = lax.broadcasted_iota(jnp.int32, (128, 8, 128), 1)
    gains = [by_device(row) for row in (jnp.sum(total * unit, axis=0, keepdims=True), moe_gain_ref[0:1, :])]
    lower = jnp.where(at == 0, gains[0][:, None, :], 0.0) + jnp.where(at == 1, gains[1][:, None, :], 0.0)
    extra = jnp.concatenate([router_ref[...].reshape(128, 8, 128), lower], axis=1)
    box[:, :, :, :, :, 4 * HALF :] = extra.astype(BF).reshape(4, 4, 4, 2, 16, 128)
    at = lax.broadcasted_iota(jnp.int32, (8, 16, 128), 1)
    here = box[z, y, :, :, :, 4 * HALF :].reshape(8, 16, 128).astype(F32)
    here = here + jnp.where(at == 10, table_ref[...][:, None, :], 0.0)
    box[z, y, :, :, :, 4 * HALF :] = here.astype(BF).reshape(4, 2, 16, 128)

    planes = [ring(z, k) for k in (1, 2, 3, 0)]
    to_twin = []
    for plane in planes:
        cols = pl.ds(pl.multiple_of(plane * 256, 256), 256)
        for which, (left, flat) in enumerate(
            ((normed_ref, flat_q), (normed_ref, flat_k), (normed_ref, flat_v), (att_ref, branch_ref))
        ):
            value = fold_rows(tn(left[:, cols], flat[...])).astype(BF)
            box[plane, :, :, :, :, which * HALF : (which + 1) * HALF] = value.reshape(4, 4, 2, 16, HALF)
        to_twin.append(copies.go(box.at[plane, :, :, 1 - c], from_twin.at[plane], place.twin))

    for k, plane in enumerate(planes):
        to_twin[k].wait_recv()
        both = box[plane, :, :, c].astype(F32) + from_twin[plane].astype(F32)
        from_twin[plane] = both.astype(BF)
        if k < 3:
            parts[0].send(0, k + 1)
    parts[1].start(0)
    parts[2].start(0)
    scaled = total * gains_ref[0:1, :]
    igrad_ref[...] = (
        hgrad_ref[...]
        + factor * (scaled - unit * jnp.mean(scaled * unit, axis=-1, keepdims=True))
    ).astype(BF)
    for phase in range(2):
        for part in parts:
            part.total(phase)
            part.start(phase + 1)
    value = jnp.concatenate([part.total(2) for part in parts], axis=1)
    for which in range(4):
        sum_ref[which * 8 : which * 8 + 8, :] = unfolded(value[:, which * HALF : (which + 1) * HALF])
    sum_ref[32:48, 0:128] = value[:, 4 * HALF :]
    copies.drain()


def placement(routes, order):
    micro = routes.shape[0]
    slots = routes.reshape(micro, 2 * TS)
    rank_of = order.reshape(micro, 2 * TS)
    same = slots[:, :, None] == slots[:, None, :]
    earlier = rank_of[:, None, :] < rank_of[:, :, None]
    rank = jnp.sum((same & earlier).astype(jnp.int32), axis=2)
    base = slots * (2 * CAP) + jnp.arange(micro, dtype=jnp.int32)[:, None] * CAP
    target = jnp.where(rank < CAP, base + rank, BUF).reshape(micro * TS, 2)
    rows = jnp.arange(BUF, dtype=jnp.int32)
    place = (rows[:, None] == target[None, :, 0]) | (rows[:, None] == target[None, :, 1])
    place_t = (rows[None, :] == target[:, 0:1]) | (rows[None, :] == target[:, 1:2])
    return place.astype(BF), place_t.astype(BF)


def on_device(
    tokens, cotangent, doc_lengths, routes, order, gain_attn, w_query, w_key, w_value, w_out,
    rel_table, gain_moe, w_router, w_gate, w_up, w_down,
):
    expert_shard = jnp.concatenate([w_gate[0].T, w_up[0].T, w_down[0]], axis=0)
    expert_w = lax.all_gather(expert_shard, "fsdp", axis=0, tiled=False)

    def padded(value):
        return jnp.pad(value, ((0, 0), (0, 128 - value.shape[1])))

    small = jnp.concatenate(
        [padded(v) for v in (w_router, gain_attn[None], gain_moe[None], rel_table[None])]
        + [jnp.zeros((5, 128), BF)],
        axis=0,
    )
    place, place_t = placement(routes[:, 0], order[:, 0, 0])
    lanes = jnp.arange(128, dtype=jnp.int32)
    route_rows = routes.reshape(TOK, 2)
    picked = (
        (route_rows[:, 0:1] == lanes) | (route_rows[:, 1:2] == lanes)
    ).astype(F32)
    x = tokens.reshape(TOK, D)
    dy = cotangent.reshape(TOK, D)
    lengths = doc_lengths[:, 0]

    normed, heads, wq, wk, wv, wo, wr, gains, table = call(
        gather_kernel,
        (
            shape((TOK, D), BF), shape((H, 3 * TS, 128), BF), shape((D, D), BF), shape((D, D), BF),
            shape((D, D), BF), shape((D, D), BF), shape((D, 128), BF), shape((8, D), F32), shape((8, 128), F32),
        ),
        x, w_query, w_key, w_value, w_out, small,
        scratch=[
            pltpu.VMEM((4, 4, 4, 2, 16, WIDE), BF),
            pltpu.VMEM((H, 3 * TS, 128), BF),
            pltpu.SemaphoreType.DMA((57,)),
            pltpu.SemaphoreType.DMA((57,)),
            pltpu.SemaphoreType.DMA((EXPERTS,)),
            pltpu.SemaphoreType.DMA((EXPERTS,)),
        ],
        collective_id=1,
    )
    smem = pl.BlockSpec(memory_space=pltpu.SMEM)
    vmem = pl.BlockSpec(memory_space=pltpu.VMEM)
    attn_scratch = [
        pltpu.VMEM((SEQ, 256), BF),
        pltpu.VMEM((EXPERTS, TOK, 256), BF),
        pltpu.VMEM((12 * TS, TOK), F32),
    ]
    att_back, lse = call(
        attn_fwd_kernel,
        (shape((EXPERTS, TS, 128), BF), shape((EXPERTS, 8, TOK), F32)),
        lengths, table, heads,
        in_specs=[smem, vmem, vmem],
        scratch=attn_scratch
        + [pltpu.VMEM((128, SEQ), BF), pltpu.VMEM((EXPERTS, TS, 128), BF)]
        + [pltpu.SemaphoreType.DMA((EXPERTS,))] * 2,
        collective_id=5,
    )
    chunk = (EXPERTS, 4 * CAP, D // 2)
    anywhere = pl.BlockSpec(memory_space=pl.ANY)
    att, hidden, mixed, share, outs, row_grads, expert_grads = call(
        moe_kernel,
        (
            shape((TOK, D), BF), shape((TOK, D), F32), shape((TOK, D), BF), shape((TOK, 128), F32),
            shape(chunk, BF), shape(chunk, BF), shape((FSDP, 3 * SHARD, D), BF),
        ),
        att_back, x, wo, gains, wr, picked, place, dy, expert_w,
        in_specs=[vmem] * 8 + [anywhere],
        out_specs=(vmem,) * 6 + (anywhere,),
        scratch=[
            pltpu.VMEM((2, 2, 3 * SHARD, D), BF),
            pltpu.VMEM(chunk, BF), pltpu.VMEM(chunk, BF), pltpu.VMEM(chunk, BF), pltpu.VMEM(chunk, BF),
            pltpu.VMEM((BUF, D), BF), pltpu.VMEM((BUF, D), BF),
            pltpu.VMEM((STEPS, BUF, FFC), BF), pltpu.VMEM((STEPS, BUF, FFC), BF), pltpu.VMEM((STEPS, BUF, FFC), BF),
            pltpu.VMEM((BUF, D), F32),
            pltpu.VMEM((3, 2, SHARD, D), BF),
            pltpu.SemaphoreType.DMA((2,)), pltpu.SemaphoreType.DMA((3,)),
        ]
        + [pltpu.SemaphoreType.DMA((EXPERTS,))] * 8,
        collective_id=3,
    )
    expert_sum = lax.psum_scatter(
        expert_grads.reshape(FSDP * 3 * SHARD, D), "fsdp", scatter_dimension=0, tiled=True
    )
    result, hgrad, branch, head_grads, router_grad, moe_gain_grad = call(
        back_kernel,
        (
            shape((TOK, D), BF), shape((TOK, D), F32), shape((TOK, D), BF),
            shape((H, TS, 128), BF), shape((D, 128), F32), shape((8, D), F32),
        ),
        outs, row_grads, place, place_t, dy, hidden, mixed, share, wr, gains, wo,
        scratch=[
            pltpu.VMEM((H, TS, 128), BF), pltpu.VMEM((BUF, D), BF), pltpu.VMEM((BUF, D), BF),
            pltpu.SemaphoreType.DMA((EXPERTS,)), pltpu.SemaphoreType.DMA((EXPERTS,)),
        ],
        collective_id=4,
    )
    token_grads, table_grad = call(
        attn_bwd_kernel,
        (shape((EXPERTS, 3 * TS, 128), BF), shape((8, 128), F32)),
        lengths, table, heads, head_grads, lse,
        in_specs=[smem] + [vmem] * 4,
        scratch=attn_scratch
        + [
            pltpu.VMEM((144, SEQ), BF),
            pltpu.VMEM((SEQ, 128), F32),
            pltpu.VMEM((SEQ, 128), F32),
            pltpu.VMEM((2 * TS, TOK), F32),
            pltpu.VMEM((8, TOK), F32),
            pltpu.VMEM((EXPERTS, 3 * TS, 128), BF),
        ]
        + [pltpu.SemaphoreType.DMA((EXPERTS,))] * 4,
        collective_id=6,
    )
    input_grad, sums = call(
        final_kernel,
        (shape((TOK, D), BF), shape((48, D), F32)),
        token_grads, normed, x, gains, hgrad, wq, wk, wv, att, branch, router_grad, moe_gain_grad, table_grad,
        scratch=[
            pltpu.VMEM((TOK, D), BF), pltpu.VMEM((TOK, D), BF), pltpu.VMEM((TOK, D), BF),
            pltpu.VMEM((4, 4, 4, 2, 16, WIDE), BF),
            pltpu.VMEM((4, 4, 4, 16, WIDE), BF),
        ]
        + [buf for lanes, _ in REDUCE_PARTS for buf in reduce_scratch(lanes.size)]
        + [pltpu.SemaphoreType.DMA((31,))] * 2,
        collective_id=2,
    )
    return (
        result.reshape(tokens.shape),
        input_grad.reshape(tokens.shape),
        sums[40, :8],
        sums[0:8],
        sums[8:16],
        sums[16:24],
        sums[24:32],
        sums[42, :4],
        sums[41, :8],
        sums[32:40, :EXPERTS],
        expert_sum[:SHARD].astype(F32).T[None],
        expert_sum[SHARD : 2 * SHARD].astype(F32).T[None],
        expert_sum[2 * SHARD :].astype(F32)[None],
    )


def solution(mesh):
    row = P(None, "fsdp", "expert", None)
    flat = P(("expert", "fsdp"))
    matrix = P(("expert", "fsdp"), None)
    columns = P("expert", None, "fsdp")
    deep = P("expert", "fsdp", None)
    return jax.shard_map(
        on_device,
        mesh=mesh,
        in_specs=(
            row, row, P(None, "fsdp", None), row, row, flat, matrix, matrix, matrix, matrix,
            flat, flat, matrix, columns, columns, deep,
        ),
        out_specs=(
            row, row, flat, matrix, matrix, matrix, matrix, flat, flat, matrix, columns, columns, deep,
        ),
        check_vma=False,
    )
```

```python
import jax
import jax.numpy as jnp
from jax import lax
from jax.experimental import pallas as pl
from jax.experimental.pallas import tpu as pltpu
from jax.sharding import PartitionSpec as P

H = 16
HD = 64
NB = 32
D = 1024
FF = 2816
WINDOW = 1024
EXPERTS = 16
CAP = 20
TS = 128
FSDP = 8
SHARD = FF // FSDP
TOK = 2 * TS
BUF = EXPERTS * 2 * CAP
SEQ = EXPERTS * TS
EPS = 1e-06
MASKED = -1e30
EDGES = tuple(range(1, 17)) + (19, 21, 24, 27, 31, 35, 40, 46, 52, 59, 67, 77, 87, 99, 113)
GELU_C = 0.7978845608028654
BF = jnp.bfloat16
F32 = jnp.float32
VMEM_LIMIT = 58 * 1024 * 1024


def nn(left, right):
    return lax.dot_general(left, right, (((1,), (0,)), ((), ())), preferred_element_type=F32)


def nt(left, right):
    return lax.dot_general(left, right, (((1,), (1,)), ((), ())), preferred_element_type=F32)


def tn(left, right):
    return lax.dot_general(left, right, (((0,), (0,)), ((), ())), preferred_element_type=F32)


def halves(value):
    high = value.astype(BF)
    return high, (value - high.astype(F32)).astype(BF)


def call(kernel, out_shape, *args, scratch=(), in_specs=None, out_specs=None, collective_id=None):
    return pl.pallas_call(
        kernel,
        out_shape=out_shape,
        in_specs=in_specs or [pl.BlockSpec(memory_space=pltpu.VMEM)] * len(args),
        out_specs=out_specs or jax.tree.map(lambda _: pl.BlockSpec(memory_space=pltpu.VMEM), out_shape),
        scratch_shapes=list(scratch),
        compiler_params=pltpu.CompilerParams(
            vmem_limit_bytes=VMEM_LIMIT,
            collective_id=collective_id,
            has_side_effects=collective_id is not None,
        ),
    )(*args)


def shape(dims, dtype):
    return jax.ShapeDtypeStruct(dims, dtype)


def lane_half(dims):
    return lax.broadcasted_iota(jnp.int32, dims, 1) % 128 < HD


def pack_pair(first, second):
    left = lane_half(first.shape)
    return (
        jnp.where(left, first, pltpu.roll(second, HD, 1)).astype(BF),
        jnp.where(left, pltpu.roll(first, HD, 1), second).astype(BF),
    )


MESH = pl.DeviceIdType.MESH
HALF = D // 2
WIDE = 4 * HALF + 128
SMALL, OUT = 3 * HALF, 3 * HALF + 128
GATHER_PARTS = ((pl.ds(0, 896), "xzy"), (pl.ds(896, 768), "xyz"))
LATE_PARTS = ((pl.ds(OUT, 256), "xzy"), (pl.ds(OUT + 256, 256), "xyz"))
REDUCE_PARTS = (
    (pl.ds(0, 1024), "zyx"), (pl.ds(1024, 640), "yzx"), (pl.ds(1664, 384), "xyz"), (pl.ds(2048, 128), "yzx"),
)
EARLY = 32
MAIN = pl.ds(0, 4 * HALF)
REST = pl.ds(4 * HALF, 128)


def coords():
    e, f = lax.axis_index("expert"), lax.axis_index("fsdp")
    return lax.div(e, 4), lax.rem(e, 4), lax.div(f, 2), lax.rem(f, 2)


def device(z, y, x, c):
    return (z * 4 + y, x * 2 + c)


def ring(at, step):
    return lax.rem(at + step, 4)


def greet(peers):
    barrier = pltpu.get_barrier_semaphore()
    for peer in peers:
        pl.semaphore_signal(barrier, inc=1, device_id=peer, device_id_type=MESH)
    pl.semaphore_wait(barrier, len(peers))


class Copies:
    def __init__(self, send_sem, recv_sem):
        self.send_sem, self.recv_sem, self.started = send_sem, recv_sem, []

    def go(self, src, dst, peer):
        at = len(self.started)
        copy = pltpu.make_async_remote_copy(
            src_ref=src,
            dst_ref=dst,
            send_sem=self.send_sem.at[at],
            recv_sem=self.recv_sem.at[at],
            device_id=peer,
            device_id_type=MESH,
        )
        copy.start()
        self.started.append(copy)
        return copy

    def drain(self):
        for copy in self.started:
            copy.wait_send()


def plane_peers():
    e, f = lax.axis_index("expert"), lax.axis_index("fsdp")
    return [(lax.rem(e + k, EXPERTS), f) for k in range(1, EXPERTS)]


class Exchange:
    def __init__(self, held, landed, send_sem, recv_sem, rows=None):
        self.held, self.landed, self.send_sem, self.recv_sem = held, landed, send_sem, recv_sem
        self.rows = rows or pl.ds(0, held.shape[1])
        self.me, self.f = lax.axis_index("expert"), lax.axis_index("fsdp")

    def copy(self, to):
        step = lax.rem(to - self.me + EXPERTS, EXPERTS)
        return pltpu.make_async_remote_copy(
            src_ref=self.held.at[to, self.rows],
            dst_ref=self.landed.at[self.me, self.rows],
            send_sem=self.send_sem.at[step],
            recv_sem=self.recv_sem.at[step],
            device_id=(to, self.f),
            device_id_type=MESH,
        )

    def others(self, act):
        def body(k, carry):
            act(self.copy(lax.rem(self.me + k, EXPERTS)))
            return carry

        lax.fori_loop(1, EXPERTS, body, 0)

    def keep(self):
        self.landed[self.me, self.rows] = self.held[self.me, self.rows]

    def push(self, to):
        @pl.when(to != self.me)
        def _():
            self.copy(to).start()

        @pl.when(to == self.me)
        def _():
            self.keep()

    def start(self):
        self.others(lambda copy: copy.start())
        self.keep()

    def arrive(self):
        self.others(lambda copy: copy.wait_recv())

    def drain(self):
        self.others(lambda copy: copy.wait_send())


def spread(value):
    half = D // 2
    parts = [value[:, at : at + half].reshape(EXPERTS, 2 * CAP, half) for at in (0, half)]
    return jnp.concatenate(parts, axis=1).astype(BF)


def unspread(into, *refs):
    half = D // 2
    value = jnp.concatenate([ref[...].astype(F32) for ref in refs], axis=1)
    for side in range(2):
        part = value[:, side * 2 * CAP : (side + 1) * 2 * CAP, :].reshape(BUF, half)
        into[:, side * half : (side + 1) * half] = part.astype(BF)


class Place:
    def __init__(self):
        self.z, self.y, self.x, self.c = coords()
        self.at = {"z": self.z, "y": self.y, "x": self.x}
        self.twin = device(self.z, self.y, self.x, 1 - self.c)

    def moved(self, axis, step):
        return {**self.at, axis: ring(self.at[axis], step)}

    def peer(self, axis, step):
        to = self.moved(axis, step)
        return device(to["z"], to["y"], to["x"], self.c)

    def peers(self, axes):
        return [self.peer(axis, k) for axis in axes for k in (1, 2, 3)]


class Gather:
    def __init__(self, place, box, copies, lanes, order):
        self.place, self.box, self.copies, self.lanes, self.order = place, box, copies, lanes, order
        self.phases, self.forwards = [], []

    def region(self, known, at):
        spots = tuple(slice(None) if axis in known else at[axis] for axis in "zyx")
        return self.box.at[spots + (self.place.c, slice(None), self.lanes)]

    def start(self, phase):
        axis, known = self.order[phase], self.order[:phase]
        here = self.region(known, self.place.at)
        self.phases.append([self.copies.go(here, here, self.place.peer(axis, k)) for k in (1, 2, 3)])

    def forward_own(self):
        here = self.region("", self.place.at)
        self.forwards.append(self.copies.go(here, here, self.place.twin))

    def forward(self, phase, k):
        axis, known = self.order[phase], self.order[:phase]
        got = self.region(known, self.place.moved(axis, 4 - k))
        self.forwards.append(self.copies.go(got, got, self.place.twin))

    def start_relay(self, phase):
        axis, known = self.order[phase], self.order[:phase]
        here = self.region(known, self.place.at)
        self.phases.append([self.copies.go(here, here, self.place.peer(axis, k)) for k in (1, 3)])

    def arrive_relay(self, phase):
        axis, known = self.order[phase], self.order[:phase]
        lanes, middle = self.lanes, (self.lanes.size // 256) * 128
        relayed = []
        for copy, k, start, size in zip(
            self.phases[phase], (1, 3), (lanes.start, lanes.start + middle), (middle, lanes.size - middle)
        ):
            copy.wait_recv()
            self.lanes = pl.ds(start, size)
            got = self.region(known, self.place.moved(axis, 4 - k))
            relayed.append(self.copies.go(got, got, self.place.peer(axis, k)))
            self.lanes = lanes
            self.forward(phase, k)
        for copy in relayed:
            copy.wait_recv()
        self.forward(phase, 2)

    def arrive(self, phase, forward=False):
        for k, copy in enumerate(self.phases[phase]):
            copy.wait_recv()
            if forward:
                self.forward(phase, k + 1)

    def forward_all(self, phase):
        for k in (1, 2, 3):
            self.forward(phase, k)

    def finish(self):
        for copy in self.forwards:
            copy.wait_recv()


class Reduce:
    def __init__(self, place, copies, order, first, held, landed):
        self.place, self.copies, self.order = place, copies, order
        self.sources, self.landed, self.started = [first] + list(held), landed, [[], [], []]

    def pick(self, phase, spot):
        left = [axis for axis in "zyx" if axis in self.order[phase:]]
        return tuple(spot if axis == self.order[phase] else slice(None) for axis in left)

    def send(self, phase, k):
        axis = self.order[phase]
        src, lanes = self.sources[phase]
        spots = self.pick(phase, ring(self.place.at[axis], k))
        src = src.at[spots + (slice(None), lanes)]
        self.started[phase].append(
            self.copies.go(src, self.landed[phase].at[k - 1], self.place.peer(axis, k))
        )

    def start(self, phase):
        for k in (1, 2, 3):
            self.send(phase, k)

    def total(self, phase):
        for copy in self.started[phase]:
            copy.wait_recv()
        src, lanes = self.sources[phase]
        spots = self.pick(phase, self.place.at[self.order[phase]])
        value = src[spots + (slice(None), lanes)].astype(F32)
        for k in range(3):
            value = value + self.landed[phase][k].astype(F32)
        if phase < 2:
            nxt, width = self.sources[phase + 1]
            nxt[...] = value.astype(BF)
        return value


def reduce_scratch(width):
    return [
        pltpu.VMEM((4, 4, 16, width), BF), pltpu.VMEM((4, 16, width), BF),
        pltpu.VMEM((3, 4, 4, 16, width), BF), pltpu.VMEM((3, 4, 16, width), BF), pltpu.VMEM((3, 16, width), BF),
    ]


def folded(value):
    return jnp.concatenate([value[:, : D // 2], value[:, D // 2 :]], axis=0)


def unfolded(value):
    return jnp.concatenate([value[:8], value[8:]], axis=1)


def fold_rows(value):
    half = D // 2
    return jnp.concatenate(
        [value[:, at : at + half].reshape(32, 8, half) for at in (0, half)], axis=1
    )


def unfold_into(ref, plane, value):
    half = D // 2
    rows = slice(plane * 256, plane * 256 + 256)
    ref[rows, :half] = value[:, :8, :].reshape(256, half).astype(BF)
    ref[rows, half:] = value[:, 8:, :].reshape(256, half).astype(BF)


def lane_pick():
    col = lax.broadcasted_iota(jnp.int32, (128, D), 1)
    return (lax.rem(col, 8) == lax.broadcasted_iota(jnp.int32, (128, D), 0)).astype(BF)


def own_columns():
    col = lax.broadcasted_iota(jnp.int32, (128, D), 1)
    low = lax.broadcasted_iota(jnp.int32, (128, D), 0) * 8
    return (col >= low) & (col < low + 8)


def by_device(row):
    high, low = halves(jnp.where(own_columns(), row, 0.0))
    pick = lane_pick()
    return nt(high, pick) + nt(low, pick)


def pick_row(values, row):
    at = lax.broadcasted_iota(jnp.int32, values.shape, values.ndim - 2)
    return jnp.sum(jnp.where(at == row, values, 0.0), axis=-2)


def gather_kernel(
    x_ref, wq_ref, wk_ref, wv_ref, wo_ref, small_ref, place_ref, dy_ref,
    normed_ref, land_ref, dy_land, dy_rest, wq_out, wk_out, wv_out, wo_out, wr_out, gain_out, tab_out,
    box, out_ref, dy_hold, send_sem, recv_sem, *sems,
):
    place = Place()
    z, y, x, c = place.z, place.y, place.x, place.c
    for at, w_ref in ((0, wq_ref), (HALF, wk_ref), (2 * HALF, wv_ref), (OUT, wo_ref)):
        box[z, y, x, c, :, at : at + HALF] = folded(w_ref[...].astype(F32)).astype(BF)
    box[z, y, x, c, :, SMALL:OUT] = small_ref[...]
    greet(plane_peers() + place.peers("x") + [place.twin])
    copies = Copies(send_sem, recv_sem)
    trade = Exchange(out_ref, land_ref, sems[0], sems[1])
    early = Exchange(dy_hold, dy_land, sems[2], sems[3])
    both = [Gather(place, box, copies, lanes, order) for lanes, order in GATHER_PARTS]
    late = [Gather(place, box, copies, lanes, order) for lanes, order in LATE_PARTS]
    for part in both:
        part.start(0)
    for part in both + late:
        part.forward_own()
    for part in late:
        part.start(0)
    tokens = x_ref[...].astype(F32)
    unit = tokens * lax.rsqrt(jnp.mean(tokens * tokens, axis=-1, keepdims=True) + EPS)
    for part in both:
        part.arrive(0)
        part.start(1)
    for part in both:
        part.forward_all(0)
    for part in both:
        part.arrive(1)
        part.start_relay(2)
    for part in both:
        part.forward_all(1)
    dy_rows = spread(nn(place_ref[...], dy_ref[...]))
    dy_hold[...] = dy_rows[:, :EARLY]
    dy_rest[...] = dy_rows[:, EARLY:]
    for part in both:
        part.arrive_relay(2)
    for part in late:
        part.arrive(0, forward=True)
        part.start(1)
    early.start()
    for part in both:
        part.finish()

    def unfold(at, w_out):
        for plane in range(4):
            value = box[plane, :, :, :, :, at : at + HALF].reshape(32, 16, HALF)
            unfold_into(w_out, plane, value.astype(F32))

    for k, w_out in enumerate((wq_out, wk_out, wv_out)):
        unfold(k * HALF, w_out)
    small = box[:, :, :, :, :, SMALL:OUT].reshape(128, 16, 128).astype(F32)
    lane = lax.broadcasted_iota(jnp.int32, (D, 128), 1)
    wr_out[...] = jnp.where(lane < EXPERTS, small[:, :8, :].reshape(D, 128), 0.0).astype(BF)
    pick, mine = lane_pick(), own_columns()
    gains = [
        jnp.sum(jnp.where(mine, nn(pick_row(small[:, 8:, :], row).astype(BF), pick), 0.0), axis=0, keepdims=True)
        for row in range(2)
    ]
    gain_out[...] = jnp.concatenate(gains + [jnp.zeros((6, D), F32)], axis=0)
    near = box[z, y, :, :, :, SMALL:OUT].reshape(8, 16, 128).astype(F32)
    tab_out[...] = pick_row(near, 10)

    normed = (unit * gains[0]).astype(BF)
    normed_ref[...] = normed
    for k in (1, 2, 3, 0):
        part = ring(z, k)
        for which, w_ref in enumerate((wq_out, wk_out, wv_out)):
            res = nn(normed, w_ref[:, pl.ds(pl.multiple_of(part * 256, 256), 256)])
            for pair in range(2):
                head = part * 4 + pair * 2
                cols = slice(pair * 128, pair * 128 + 128)
                first, second = pack_pair(res[:TS, cols], res[TS:, cols])
                out_ref[head, which * TS : (which + 1) * TS, :] = first
                out_ref[head + 1, which * TS : (which + 1) * TS, :] = second
        if k == 1:
            for part_late in late:
                part_late.arrive(1, forward=True)
                part_late.start(2)
        for j in (1, 2, 3, 0):
            if k or j:
                trade.copy(part * 4 + ring(y, j)).start()
            else:
                trade.keep()
    for part in late:
        part.arrive(2, forward=True)
    for part in late:
        part.finish()
    unfold(OUT, wo_out)
    trade.arrive()
    early.arrive()
    trade.drain()
    early.drain()
    copies.drain()


def attn_setup(len_ref, tab_ref, recv_ref, kext, qext, bias):
    rows = lax.broadcasted_iota(jnp.int32, (SEQ, 128), 0)
    lanes = lax.broadcasted_iota(jnp.int32, (SEQ, 128), 1)
    end1 = [len_ref[m, 0] for m in range(2)]
    end2 = [len_ref[m, 0] + len_ref[m, 1] for m in range(2)]
    kfeat = jnp.where(lanes == 4, 1.0, 0.0)
    for m in range(2):
        kfeat = jnp.where((lanes == 2 * m) & (rows < end1[m]), 1.0, kfeat)
        kfeat = jnp.where((lanes == 2 * m + 1) & (rows < end2[m]), 1.0, kfeat)
    kext[:, 128:] = kfeat.astype(BF)
    for i in range(EXPERTS):
        kext[i * TS : (i + 1) * TS, :128] = recv_ref[i, TS : 2 * TS, :]
    left = lane_half((TS, 128))
    row_in = lax.broadcasted_iota(jnp.int32, (TS, 128), 0)
    lane_in = lax.broadcasted_iota(jnp.int32, (TS, 128), 1)
    for i in range(EXPERTS):
        q2 = recv_ref[i, 0:TS, :].astype(F32) * (HD**-0.5)
        pos = row_in + i * TS
        for m in range(2):
            keep = left if m == 0 else jnp.logical_not(left)
            qext[i, m * TS : (m + 1) * TS, :128] = jnp.where(keep, q2, 0.0).astype(BF)
            feat = jnp.where((lane_in == 2 * m) & (pos >= end1[m]), MASKED, 0.0)
            feat = jnp.where((lane_in == 2 * m + 1) & (pos >= end2[m]), MASKED, feat)
            qext[i, m * TS : (m + 1) * TS, 128:] = feat.astype(BF)
    for block in range(12):
        dist = 1024 - block * TS + lane_in - row_in
        if block in (7, 8):
            value = jnp.broadcast_to(tab_ref[0:1, 0:1], (TS, 128))
            for bucket, edge in enumerate(EDGES):
                b = bucket + 1
                value = jnp.where(dist >= edge, tab_ref[b // 4 : b // 4 + 1, b % 4 : b % 4 + 1], value)
        else:
            value = jnp.broadcast_to(tab_ref[7:8, 3:4], (TS, 128))
        value = jnp.where((dist >= 0) & (dist < WINDOW), value, MASKED)
        bias[block * TS : (block + 1) * TS, :128] = value
        bias[block * TS : (block + 1) * TS, 128:] = value


def eye(size):
    return (
        lax.broadcasted_iota(jnp.int32, (size, size), 0)
        == lax.broadcasted_iota(jnp.int32, (size, size), 1)
    ).astype(BF)


def strips(strip, after):
    def run(low, count):
        def body(at, carry):
            i = low + at
            strip(i + 8, 9, i)
            strip(i, count, 0)
            after(i)
            return carry

        lax.fori_loop(0, 4, body, 0)

    run(0, 4)
    run(4, 8)


def span(block, count):
    return pl.ds(pl.multiple_of(block * TS, TS), count * TS)


def attn_fwd_kernel(
    len_ref, tab_ref, recv_ref, dy_ref, land_ref, lse_ref, dy_land, kext, qext, bias, vt, out_ref, *sems
):
    greet(plane_peers())
    trade = Exchange(out_ref, land_ref, sems[0], sems[1])
    early = Exchange(dy_ref, dy_land, sems[2], sems[3])
    early.start()
    attn_setup(len_ref, tab_ref, recv_ref, kext, qext, bias)
    unit = eye(TS)
    for i in range(EXPERTS):
        vt[:, i * TS : (i + 1) * TS] = nt(unit, recv_ref[i, 2 * TS : 3 * TS, :]).astype(BF)

    def strip(i, count, first):
        s = nt(kext[span(first, count), :], qext[i]) + bias[span(first - i + 8, count), :]
        top = jnp.max(s, axis=0, keepdims=True)
        p = jnp.exp(s - top)
        total = jnp.sum(p, axis=0, keepdims=True)
        res = nn(vt[:, span(first, count)], p.astype(BF)) / total
        both = jnp.concatenate([res[:HD, :TS], res[HD:, TS:]], axis=0)
        out_ref[i] = both.T.astype(BF)
        lse_ref[i] = jnp.broadcast_to(top + jnp.log(total), (8, TOK))

    def after(i):
        trade.push(i + 8)
        trade.push(i)

    strips(strip, after)
    trade.arrive()
    early.arrive()
    trade.drain()
    early.drain()


def attn_bwd_kernel(
    len_ref, tab_ref, recv_ref, dout_ref, lse_ref, land_ref, tab_out_ref,
    kext, qext, bias, ktext, dk, dv, near, far, out_ref, *sems,
):
    greet(plane_peers())
    trade_q = Exchange(out_ref, land_ref, sems[0], sems[1], pl.ds(0, TS))
    trade_kv = Exchange(out_ref, land_ref, sems[2], sems[3], pl.ds(TS, 2 * TS))
    attn_setup(len_ref, tab_ref, recv_ref, kext, qext, bias)
    unit = eye(256)
    for i in range(EXPERTS):
        ktext[:, i * TS : (i + 1) * TS] = nt(unit, kext[i * TS : (i + 1) * TS, :])[:144].astype(BF)
    dk[...] = jnp.zeros_like(dk)
    dv[...] = jnp.zeros_like(dv)
    near[...] = jnp.zeros_like(near)
    far[...] = jnp.zeros_like(far)
    left = lane_half((TS, 128))

    def strip(i, count, first):
        q = qext[i]
        s = nt(kext[span(first, count), :], q) + bias[span(first - i + 8, count), :]
        p = jnp.exp(s - lse_ref[i][0:1])
        do2 = dout_ref[i]
        zero = jnp.zeros_like(do2)
        do = jnp.concatenate([jnp.where(left, do2, zero), jnp.where(left, zero, do2)], axis=0)
        if count == 9:
            v = recv_ref[pl.ds(first, count), 2 * TS : 3 * TS, :].reshape(count * TS, 128)
        else:
            v = recv_ref[0:count, 2 * TS : 3 * TS, :].reshape(count * TS, 128)
        dp = nt(v, do)
        inner = jnp.sum(p * dp, axis=0, keepdims=True)
        ds = (p * (dp - inner)).astype(BF)
        dv[span(first, count), :] += nn(p.astype(BF), do)
        dk[span(first, count), :] += nn(ds, q[:, :128])
        dqt = nn(ktext[:, span(first, count)], ds)
        both = jnp.concatenate([dqt[:HD, :TS], dqt[HD : 2 * HD, TS:]], axis=0) * (HD**-0.5)
        out_ref[i, 0:TS, :] = both.T.astype(BF)
        far[...] += dqt[128:136]
        if count == 9:
            near[...] += ds[7 * TS :].astype(F32)
        else:
            for block in range(count):
                value = ds[block * TS : (block + 1) * TS].astype(F32)
                near[TS:] += value * (i == block).astype(F32)
                near[:TS] += value * (i == block + 1).astype(F32)

    def finish(i):
        out_ref[i, TS : 2 * TS, :] = dk[span(i, 1), :].astype(BF)
        out_ref[i, 2 * TS :, :] = dv[span(i, 1), :].astype(BF)
        trade_kv.push(i)

    odd = lax.rem(trade_kv.me, 2)

    def first_half(low, count):
        def body(at, carry):
            i = low + 2 * at
            strip(i, count, 0)
            strip(i + 1, count, 0)
            trade_q.push(i)
            trade_q.push(i + 1)
            return carry

        lax.fori_loop(0, 2, body, 0)

    first_half(0, 4)
    first_half(4, 8)

    def second_half(at, carry):
        blocks = [odd * (8 + step) + (1 - odd) * (15 - step) for step in (2 * at, 2 * at + 1)]
        for i in blocks:
            strip(i, 9, i - 8)
        for i in blocks:
            trade_q.push(i)
            finish(i - 8 * odd)
        return carry

    lax.fori_loop(0, 4, second_half, 0)

    def rest(step, carry):
        finish(lax.rem(step + lax.div(trade_kv.me, 2), 8) + 8 * odd)
        return carry

    lax.fori_loop(0, 8, rest, 0)
    grads = near[:, :TS] + near[:, TS:]
    dist = (
        TS
        + lax.broadcasted_iota(jnp.int32, (TOK, TS), 1)
        - lax.broadcasted_iota(jnp.int32, (TOK, TS), 0)
    )
    total = jnp.sum(far[4:5, :])
    lane = lax.broadcasted_iota(jnp.int32, (8, 128), 1)
    lane = jnp.where(lane < 4, lane + 4 * lax.broadcasted_iota(jnp.int32, (8, 128), 0), NB)
    res = jnp.zeros((8, 128), F32)
    lows = (0,) + EDGES
    seen = 0.0
    for b in range(NB - 1):
        part = jnp.sum(jnp.where((dist >= lows[b]) & (dist < lows[b + 1]), grads, 0.0))
        seen = seen + part
        res = jnp.where(lane == b, part, res)
    res = jnp.where(lane == NB - 1, total - seen, res)
    tab_out_ref[...] = res
    for trade in (trade_q, trade_kv):
        trade.arrive()
        trade.drain()


def row_expert():
    row = lax.broadcasted_iota(jnp.int32, (BUF, 128), 0)
    lane = lax.broadcasted_iota(jnp.int32, (BUF, 128), 1) * (2 * CAP)
    return (row >= lane) & (row < lane + 2 * CAP)


def unpack_heads(recv_ref, lo, emit):
    for pair in range(H // 2):
        one = recv_ref[2 * pair, lo : lo + TS, :].astype(F32)
        two = recv_ref[2 * pair + 1, lo : lo + TS, :].astype(F32)
        first, second = pack_pair(one, two)
        emit(pair, first, second)


def slot_share(place, share_e, own):
    high, low = halves(share_e)
    return jnp.sum(jnp.where(own, nn(place, high) + nn(place, low), 0.0), axis=1, keepdims=True)


CHUNKS = ((0, 768), (768, 768), (1536, 768), (2304, 512))


def pieces(at, size):
    found, row = [], at
    while row < at + size:
        end = min(at + size, (row // SHARD + 1) * SHARD)
        found.append((row // SHARD, row % SHARD, row - at, end - row))
        row = end
    return found


STAGED = 3 * sum(len(pieces(at, size)) for at, size in CHUNKS)


def moe_kernel(
    recv_ref, x_ref, wo_ref, gain_ref, wr_ref, mask_ref, place_ref, dy_ref, dy_late_ref, w_ref,
    att_ref, hidden_ref, mixed_ref, share_ref, back_out, back_row, grads_ref,
    w_buf, hold_a, hold_b, land_a, hold_s, land_s, rows, slots, act, first, second, acc, stage,
    w_sem, stage_sem, *sems,
):
    loads = [
        [
            pltpu.make_async_copy(
                w_ref.at[s, pl.ds(k * SHARD, SHARD)],
                w_buf.at[k, pl.ds(s * SHARD, SHARD)],
                w_sem.at[k * FSDP + s],
            )
            for s in range(FSDP)
        ]
        for k in range(3)
    ]
    for k in (2, 0, 1):
        for copy in loads[k]:
            copy.start()
    greet(plane_peers())
    to_rows = Exchange(hold_a, land_a, sems[0], sems[1])
    to_shares = Exchange(hold_s, land_s, sems[2], sems[3])
    from_out = Exchange(hold_a, back_out, sems[4], sems[5])
    from_row = Exchange(hold_b, back_row, sems[6], sems[7])

    def emit(pair, one, two):
        att_ref[0:TS, pair * 128 : pair * 128 + 128] = one
        att_ref[TS:, pair * 128 : pair * 128 + 128] = two

    unpack_heads(recv_ref, 0, emit)
    hidden = x_ref[...].astype(F32) + nn(att_ref[...], wo_ref[...])
    hidden_ref[...] = hidden
    factor = lax.rsqrt(jnp.mean(hidden * hidden, axis=-1, keepdims=True) + EPS)
    mixed = (hidden * factor * gain_ref[1:2, :]).astype(BF)
    mixed_ref[...] = mixed
    place = place_ref[...]
    hold_a[...] = spread(nn(place, mixed))
    to_rows.start()
    picked = mask_ref[...] > 0
    logits = jnp.where(picked, nn(mixed, wr_ref[...]), MASKED)
    weight = jnp.exp(logits - jnp.max(logits, axis=1, keepdims=True))
    share = weight / jnp.sum(weight, axis=1, keepdims=True)
    share_ref[...] = share
    high, low = halves(slot_share(place, share, row_expert()))
    lane = lax.broadcasted_iota(jnp.int32, (BUF, 128), 1)
    value = jnp.where(lane == 0, high.astype(F32), 0.0) + jnp.where(lane == 1, low.astype(F32), 0.0)
    value = value.reshape(EXPERTS, 2 * CAP, 128)
    hold_s[...] = jnp.concatenate([value, jnp.zeros((EXPERTS, 8, 128), F32)], axis=1).astype(BF)
    to_shares.start()

    unspread(slots, dy_ref, dy_late_ref)
    for copy in loads[2]:
        copy.wait()
    for at, size in CHUNKS:
        first[:, at : at + size] = nt(slots[...], w_buf[2, at : at + size, :]).astype(BF)
    for k in range(2):
        for copy in loads[k]:
            copy.wait()
    to_rows.arrive()
    unspread(rows, land_a)
    for at, size in CHUNKS:
        cols = slice(at, at + size)
        gate = nt(rows[...], w_buf[0, cols, :])
        up = nt(rows[...], w_buf[1, cols, :])
        square = gate * gate
        tanh = jnp.tanh(GELU_C * gate * (1.0 + 0.044715 * square))
        half_up = 0.5 * (1.0 + tanh)
        gelu = gate * half_up
        slope = half_up + 0.5 * gate * (1.0 - tanh * tanh) * (
            GELU_C * (1.0 + 3 * 0.044715 * square)
        )
        act_grad = first[:, cols].astype(F32)
        act[:, cols] = (gelu * up).astype(BF)
        first[:, cols] = (act_grad * up * slope).astype(BF)
        second[:, cols] = (act_grad * gelu).astype(BF)
    for half in range(2):
        cols = slice(half * HALF, half * HALF + HALF)
        acc[:, cols] = nn(act[...], w_buf[2, :, cols])
    to_rows.drain()
    hold_a[...] = spread(acc[...])
    from_out.start()
    for half in range(2):
        cols = slice(half * HALF, half * HALF + HALF)
        acc[:, cols] = nn(first[...], w_buf[0, :, cols]) + nn(second[...], w_buf[1, :, cols])
    hold_b[...] = spread(acc[...])
    from_row.start()

    to_shares.arrive()
    value = land_s[...].astype(F32)[:, : 2 * CAP, :].reshape(BUF, 128)
    scale = jnp.sum(value, axis=1, keepdims=True)
    rows[...] = (rows[...].astype(F32) * scale).astype(BF)
    slots[...] = (slots[...].astype(F32) * scale).astype(BF)
    pending = [[], [], []]
    count = turn = 0
    for which, (left, right) in ((2, (act, slots)), (0, (first, rows)), (1, (second, rows))):
        for at, size in CHUNKS:
            value = tn(left[:, at : at + size], right[...]).astype(BF)
            for copy in pending[turn]:
                copy.wait()
            stage[turn, :size, :] = value
            pending[turn] = []
            for shard, row, local, amount in pieces(at, size):
                copy = pltpu.make_async_copy(
                    stage.at[turn, pl.ds(local, amount)],
                    grads_ref.at[shard, pl.ds(which * SHARD + row, amount)],
                    stage_sem.at[count],
                )
                copy.start()
                pending[turn].append(copy)
                count += 1
            turn = (turn + 1) % 3
    for group in pending:
        for copy in group:
            copy.wait()
    from_out.arrive()
    from_row.arrive()
    from_out.drain()
    from_row.drain()
    to_shares.drain()


def back_kernel(
    out_ref, row_ref, place_ref, place_t_ref, dy_ref, hidden_ref, mixed_ref, share_ref, wr_ref, gain_ref, wo_ref,
    result_ref, hgrad_ref, branch_ref, land_ref, router_ref, gain_out_ref,
    send_ref, outs, rows, send_sem, recv_sem,
):
    greet(plane_peers())
    z, y, _, _ = coords()
    trade = Exchange(send_ref, land_ref, send_sem, recv_sem)
    unspread(outs, out_ref)
    unspread(rows, row_ref)
    place = place_ref[...]
    place_t = place_t_ref[...]
    own = row_expert()
    dy = dy_ref[...]
    returned = outs[...]
    dots = jnp.sum(nn(place, dy) * returned.astype(F32), axis=1, keepdims=True)
    high, low = halves(jnp.where(own, dots, 0.0))
    share = share_ref[...]
    share_grad = nn(place_t, high) + nn(place_t, low)
    inner = jnp.sum(share * share_grad, axis=1, keepdims=True)
    lg_high, lg_low = halves(share * (share_grad - inner))
    wr = wr_ref[...]
    scale_high, scale_low = halves(
        place_t.astype(F32) * slot_share(place, share, own).T
    )
    mixed_grad = (nn(scale_high, rows[...]) + nn(scale_low, rows[...])) + (
        nt(lg_high, wr) + nt(lg_low, wr)
    )
    hidden = hidden_ref[...]
    factor = lax.rsqrt(jnp.mean(hidden * hidden, axis=-1, keepdims=True) + EPS)
    unit = hidden * factor
    gain_out_ref[...] = jnp.broadcast_to(jnp.sum(mixed_grad * unit, axis=0, keepdims=True), (8, D))
    scaled = mixed_grad * gain_ref[1:2, :]
    hgrad = dy.astype(F32) + factor * (
        scaled - unit * jnp.mean(scaled * unit, axis=-1, keepdims=True)
    )
    hgrad_ref[...] = hgrad
    branch = hgrad.astype(BF)
    branch_ref[...] = branch
    for k in (1, 2, 3, 0):
        part = ring(z, k)
        res = nt(branch, wo_ref[pl.ds(pl.multiple_of(part * 256, 256), 256), :])
        for pair in range(2):
            head = part * 4 + pair * 2
            cols = slice(pair * 128, pair * 128 + 128)
            one, two = pack_pair(res[:TS, cols], res[TS:, cols])
            send_ref[head] = one
            send_ref[head + 1] = two
        for j in (1, 2, 3, 0):
            if k or j:
                trade.copy(part * 4 + ring(y, j)).start()
            else:
                trade.keep()
    mixed = mixed_ref[...]
    router_ref[...] = tn(mixed, lg_high) + tn(mixed, lg_low)
    moe = nn(scale_high, returned) + nn(scale_low, returned)
    result_ref[...] = (hidden + moe).astype(BF)
    trade.arrive()
    trade.drain()


def final_kernel(
    recv_ref, normed_ref, x_ref, gains_ref, hgrad_ref, wq_ref, wk_ref, wv_ref,
    att_ref, branch_ref, router_ref, moe_gain_ref, table_ref, igrad_ref, sum_ref,
    flat_q, flat_k, flat_v, box, from_twin, *rest,
):
    place = Place()
    z, y, c = place.z, place.y, place.c
    greet(place.peers("xyz") + [place.twin])
    copies = Copies(rest[20], rest[21])
    parts = [
        Reduce(
            place, copies, order, (from_twin, lanes),
            [(bufs[0], pl.ds(0, lanes.size)), (bufs[1], pl.ds(0, lanes.size))], bufs[2:],
        )
        for (lanes, order), bufs in zip(REDUCE_PARTS, (rest[0:5], rest[5:10], rest[10:15], rest[15:20]))
    ]
    flats = (flat_q, flat_k, flat_v)
    for which, flat in enumerate(flats):

        def emit(pair, first, second):
            flat[0:TS, pair * 128 : pair * 128 + 128] = first
            flat[TS:, pair * 128 : pair * 128 + 128] = second

        unpack_heads(recv_ref, which * TS, emit)

    planes = [ring(z, k) for k in (1, 2, 3, 0)]
    to_twin = []

    def pair_sum(k):
        plane = planes[k]
        to_twin[k].wait_recv()
        both = box[plane, :, :, c, :, MAIN].astype(F32) + from_twin[plane, :, :, :, MAIN].astype(F32)
        from_twin[plane, :, :, :, MAIN] = both.astype(BF)
        if k < 3:
            parts[0].send(0, k + 1)

    for k, plane in enumerate(planes):
        cols = pl.ds(pl.multiple_of(plane * 256, 256), 256)
        for which, (left, flat) in enumerate(
            ((normed_ref, flat_q), (normed_ref, flat_k), (normed_ref, flat_v), (att_ref, branch_ref))
        ):
            value = fold_rows(tn(left[:, cols], flat[...])).astype(BF)
            box[plane, :, :, :, :, which * HALF : (which + 1) * HALF] = value.reshape(4, 4, 2, 16, HALF)
        to_twin.append(
            copies.go(
                box.at[plane, :, :, 1 - c, :, MAIN], from_twin.at[plane, :, :, :, MAIN], place.twin
            )
        )
        if k:
            pair_sum(k - 1)
    pair_sum(3)
    parts[1].start(0)
    parts[2].start(0)

    total = nt(flat_q[...], wq_ref[...]) + nt(flat_k[...], wk_ref[...]) + nt(flat_v[...], wv_ref[...])
    tokens = x_ref[...].astype(F32)
    factor = lax.rsqrt(jnp.mean(tokens * tokens, axis=-1, keepdims=True) + EPS)
    unit = tokens * factor

    at = lax.broadcasted_iota(jnp.int32, (128, 8, 128), 1)
    gains = [by_device(row) for row in (jnp.sum(total * unit, axis=0, keepdims=True), moe_gain_ref[0:1, :])]
    lower = jnp.where(at == 0, gains[0][:, None, :], 0.0) + jnp.where(at == 1, gains[1][:, None, :], 0.0)
    extra = jnp.concatenate([router_ref[...].reshape(128, 8, 128), lower], axis=1)
    box[:, :, :, :, :, REST] = extra.astype(BF).reshape(4, 4, 4, 2, 16, 128)
    at = lax.broadcasted_iota(jnp.int32, (8, 16, 128), 1)
    here = box[z, y, :, :, :, REST].reshape(8, 16, 128).astype(F32)
    here = here + jnp.where(at == 10, table_ref[...][:, None, :], 0.0)
    box[z, y, :, :, :, REST] = here.astype(BF).reshape(4, 2, 16, 128)
    rest_copy = copies.go(
        box.at[:, :, :, 1 - c, :, REST], from_twin.at[:, :, :, :, REST], place.twin
    )
    rest_copy.wait_recv()
    both = box[:, :, :, c, :, REST].astype(F32) + from_twin[:, :, :, :, REST].astype(F32)
    from_twin[:, :, :, :, REST] = both.astype(BF)
    parts[3].start(0)
    scaled = total * gains_ref[0:1, :]
    igrad_ref[...] = (
        hgrad_ref[...]
        + factor * (scaled - unit * jnp.mean(scaled * unit, axis=-1, keepdims=True))
    ).astype(BF)
    for phase in range(2):
        for part in parts:
            part.total(phase)
            part.start(phase + 1)
    value = jnp.concatenate([part.total(2) for part in parts], axis=1)
    for which in range(4):
        sum_ref[which * 8 : which * 8 + 8, :] = unfolded(value[:, which * HALF : (which + 1) * HALF])
    sum_ref[32:48, 0:128] = value[:, 4 * HALF :]
    copies.drain()


def emit_kernel(expert_ref, sum_ref, gate, up, down, gq, gk, gv, go, router, gain_attn, gain_moe, table):
    for k, ref in enumerate((gate, up, down)):
        ref[...] = expert_ref[k * SHARD : (k + 1) * SHARD, :].astype(F32)
    for k, ref in enumerate((gq, gk, gv, go)):
        ref[...] = sum_ref[k * 8 : k * 8 + 8, :]
    router[...] = sum_ref[32:40, :EXPERTS]
    gain_attn[...] = sum_ref[40:41, :8]
    gain_moe[...] = sum_ref[41:42, :8]
    table[...] = sum_ref[42:43, :4]


def placement(routes, order):
    micro = routes.shape[0]
    slots = routes.reshape(micro, 2 * TS)
    rank_of = order.reshape(micro, 2 * TS)
    same = slots[:, :, None] == slots[:, None, :]
    earlier = rank_of[:, None, :] < rank_of[:, :, None]
    rank = jnp.sum((same & earlier).astype(jnp.int32), axis=2)
    base = slots * (2 * CAP) + jnp.arange(micro, dtype=jnp.int32)[:, None] * CAP
    target = jnp.where(rank < CAP, base + rank, BUF).reshape(micro * TS, 2)
    rows = jnp.arange(BUF, dtype=jnp.int32)
    place = (rows[:, None] == target[None, :, 0]) | (rows[:, None] == target[None, :, 1])
    place_t = (rows[None, :] == target[:, 0:1]) | (rows[None, :] == target[:, 1:2])
    return place.astype(BF), place_t.astype(BF)


def on_device(
    tokens, cotangent, doc_lengths, routes, order, gain_attn, w_query, w_key, w_value, w_out,
    rel_table, gain_moe, w_router, w_gate, w_up, w_down,
):
    expert_shard = jnp.concatenate([w_gate[0].T, w_up[0].T, w_down[0]], axis=0)
    expert_w = lax.all_gather(expert_shard, "fsdp", axis=0, tiled=False)

    def padded(value):
        return jnp.pad(value, ((0, 0), (0, 128 - value.shape[1])))

    small = jnp.concatenate(
        [padded(v) for v in (w_router, gain_attn[None], gain_moe[None], rel_table[None])]
        + [jnp.zeros((5, 128), BF)],
        axis=0,
    )
    place, place_t = placement(routes[:, 0], order[:, 0, 0])
    lanes = jnp.arange(128, dtype=jnp.int32)
    route_rows = routes.reshape(TOK, 2)
    picked = (
        (route_rows[:, 0:1] == lanes) | (route_rows[:, 1:2] == lanes)
    ).astype(F32)
    x = tokens.reshape(TOK, D)
    dy = cotangent.reshape(TOK, D)
    lengths = doc_lengths[:, 0]

    chunk = (EXPERTS, 4 * CAP, HALF)
    early, rest = (EXPERTS, EARLY, HALF), (EXPERTS, 4 * CAP - EARLY, HALF)
    normed, heads, dy_early, dy_rest, wq, wk, wv, wo, wr, gains, table = call(
        gather_kernel,
        (
            shape((TOK, D), BF), shape((H, 3 * TS, 128), BF), shape(early, BF), shape(rest, BF), shape((D, D), BF), shape((D, D), BF),
            shape((D, D), BF), shape((D, D), BF), shape((D, 128), BF), shape((8, D), F32), shape((8, 128), F32),
        ),
        x, w_query, w_key, w_value, w_out, small, place, dy,
        scratch=[
            pltpu.VMEM((4, 4, 4, 2, 16, WIDE), BF),
            pltpu.VMEM((H, 3 * TS, 128), BF),
            pltpu.VMEM(early, BF),
            pltpu.SemaphoreType.DMA((78,)),
            pltpu.SemaphoreType.DMA((78,)),
        ]
        + [pltpu.SemaphoreType.DMA((EXPERTS,))] * 4,
        collective_id=1,
    )
    smem = pl.BlockSpec(memory_space=pltpu.SMEM)
    vmem = pl.BlockSpec(memory_space=pltpu.VMEM)
    attn_scratch = [
        pltpu.VMEM((SEQ, 256), BF),
        pltpu.VMEM((EXPERTS, TOK, 256), BF),
        pltpu.VMEM((12 * TS, TOK), F32),
    ]
    att_back, lse, dy_late = call(
        attn_fwd_kernel,
        (shape((EXPERTS, TS, 128), BF), shape((EXPERTS, 8, TOK), F32), shape(rest, BF)),
        lengths, table, heads, dy_rest,
        in_specs=[smem] + [vmem] * 3,
        scratch=attn_scratch
        + [pltpu.VMEM((128, SEQ), BF), pltpu.VMEM((EXPERTS, TS, 128), BF)]
        + [pltpu.SemaphoreType.DMA((EXPERTS,))] * 4,
        collective_id=5,
    )
    anywhere = pl.BlockSpec(memory_space=pl.ANY)
    att, hidden, mixed, share, outs, row_grads, expert_grads = call(
        moe_kernel,
        (
            shape((TOK, D), BF), shape((TOK, D), F32), shape((TOK, D), BF), shape((TOK, 128), F32),
            shape(chunk, BF), shape(chunk, BF), shape((FSDP, 3 * SHARD, D), BF),
        ),
        att_back, x, wo, gains, wr, picked, place, dy_early, dy_late, expert_w,
        in_specs=[vmem] * 9 + [anywhere],
        out_specs=(vmem,) * 6 + (anywhere,),
        scratch=[
            pltpu.VMEM((3, FF, D), BF),
            pltpu.VMEM(chunk, BF), pltpu.VMEM(chunk, BF), pltpu.VMEM(chunk, BF),
            pltpu.VMEM((EXPERTS, 48, 128), BF), pltpu.VMEM((EXPERTS, 48, 128), BF),
            pltpu.VMEM((BUF, D), BF), pltpu.VMEM((BUF, D), BF),
            pltpu.VMEM((BUF, FF), BF), pltpu.VMEM((BUF, FF), BF), pltpu.VMEM((BUF, FF), BF),
            pltpu.VMEM((BUF, D), F32),
            pltpu.VMEM((3, 768, D), BF),
            pltpu.SemaphoreType.DMA((3 * FSDP,)), pltpu.SemaphoreType.DMA((STAGED,)),
        ]
        + [pltpu.SemaphoreType.DMA((EXPERTS,))] * 8,
        collective_id=3,
    )
    expert_sum = lax.psum_scatter(
        expert_grads.reshape(FSDP * 3 * SHARD, D), "fsdp", scatter_dimension=0, tiled=True
    )
    result, hgrad, branch, head_grads, router_grad, moe_gain_grad = call(
        back_kernel,
        (
            shape((TOK, D), BF), shape((TOK, D), F32), shape((TOK, D), BF),
            shape((H, TS, 128), BF), shape((D, 128), F32), shape((8, D), F32),
        ),
        outs, row_grads, place, place_t, dy, hidden, mixed, share, wr, gains, wo,
        scratch=[
            pltpu.VMEM((H, TS, 128), BF), pltpu.VMEM((BUF, D), BF), pltpu.VMEM((BUF, D), BF),
            pltpu.SemaphoreType.DMA((EXPERTS,)), pltpu.SemaphoreType.DMA((EXPERTS,)),
        ],
        collective_id=4,
    )
    token_grads, table_grad = call(
        attn_bwd_kernel,
        (shape((EXPERTS, 3 * TS, 128), BF), shape((8, 128), F32)),
        lengths, table, heads, head_grads, lse,
        in_specs=[smem] + [vmem] * 4,
        scratch=attn_scratch
        + [
            pltpu.VMEM((144, SEQ), BF),
            pltpu.VMEM((SEQ, 128), F32),
            pltpu.VMEM((SEQ, 128), F32),
            pltpu.VMEM((2 * TS, TOK), F32),
            pltpu.VMEM((8, TOK), F32),
            pltpu.VMEM((EXPERTS, 3 * TS, 128), BF),
        ]
        + [pltpu.SemaphoreType.DMA((EXPERTS,))] * 4,
        collective_id=6,
    )
    input_grad, sums = call(
        final_kernel,
        (shape((TOK, D), BF), shape((48, D), F32)),
        token_grads, normed, x, gains, hgrad, wq, wk, wv, att, branch, router_grad, moe_gain_grad, table_grad,
        scratch=[
            pltpu.VMEM((TOK, D), BF), pltpu.VMEM((TOK, D), BF), pltpu.VMEM((TOK, D), BF),
            pltpu.VMEM((4, 4, 4, 2, 16, WIDE), BF),
            pltpu.VMEM((4, 4, 4, 16, WIDE), BF),
        ]
        + [buf for lanes, _ in REDUCE_PARTS for buf in reduce_scratch(lanes.size)]
        + [pltpu.SemaphoreType.DMA((41,))] * 2,
        collective_id=2,
    )
    block = shape((SHARD, D), F32)
    rows = shape((8, D), F32)
    gate, up, down, gq, gk, gv, go, router, gain_a, gain_m, table_sum = call(
        emit_kernel,
        (block, block, block, rows, rows, rows, rows)
        + tuple(shape(dims, F32) for dims in ((8, EXPERTS), (1, 8), (1, 8), (1, 4))),
        expert_sum, sums,
    )
    return (
        result.reshape(tokens.shape), input_grad.reshape(tokens.shape), gain_a[0], gq, gk, gv, go,
        table_sum[0], gain_m[0], router, gate.T[None], up.T[None], down[None],
    )


def solution(mesh):
    row = P(None, "fsdp", "expert", None)
    flat = P(("expert", "fsdp"))
    matrix = P(("expert", "fsdp"), None)
    columns = P("expert", None, "fsdp")
    deep = P("expert", "fsdp", None)
    return jax.shard_map(
        on_device,
        mesh=mesh,
        in_specs=(
            row, row, P(None, "fsdp", None), row, row, flat, matrix, matrix, matrix, matrix,
            flat, flat, matrix, columns, columns, deep,
        ),
        out_specs=(
            row, row, flat, matrix, matrix, matrix, matrix, flat, flat, matrix, columns, columns, deep,
        ),
        check_vma=False,
    )
```

```python
import jax
import jax.numpy as jnp
from jax import lax
from jax.experimental import pallas as pl
from jax.experimental.pallas import tpu as pltpu
from jax.sharding import PartitionSpec as P

H = 16
HD = 64
NB = 32
D = 1024
FF = 2816
WINDOW = 1024
EXPERTS = 16
CAP = 20
TS = 128
FSDP = 8
SHARD = FF // FSDP
TOK = 2 * TS
BUF = EXPERTS * 2 * CAP
SEQ = EXPERTS * TS
EPS = 1e-06
MASKED = -1e30
EDGES = tuple(range(1, 17)) + (19, 21, 24, 27, 31, 35, 40, 46, 52, 59, 67, 77, 87, 99, 113)
GELU_C = 0.7978845608028654
BF = jnp.bfloat16
F32 = jnp.float32
VMEM_LIMIT = 60 * 1024 * 1024


def nn(left, right):
    return lax.dot_general(left, right, (((1,), (0,)), ((), ())), preferred_element_type=F32)


def nt(left, right):
    return lax.dot_general(left, right, (((1,), (1,)), ((), ())), preferred_element_type=F32)


def tn(left, right):
    return lax.dot_general(left, right, (((0,), (0,)), ((), ())), preferred_element_type=F32)


def halves(value):
    high = value.astype(BF)
    return high, (value - high.astype(F32)).astype(BF)


def call(kernel, out_shape, *args, scratch=(), in_specs=None, out_specs=None, collective_id=None):
    return pl.pallas_call(
        kernel,
        out_shape=out_shape,
        in_specs=in_specs or [pl.BlockSpec(memory_space=pltpu.VMEM)] * len(args),
        out_specs=out_specs or jax.tree.map(lambda _: pl.BlockSpec(memory_space=pltpu.VMEM), out_shape),
        scratch_shapes=list(scratch),
        compiler_params=pltpu.CompilerParams(
            vmem_limit_bytes=VMEM_LIMIT,
            collective_id=collective_id,
            has_side_effects=collective_id is not None,
        ),
    )(*args)


def shape(dims, dtype):
    return jax.ShapeDtypeStruct(dims, dtype)


def lane_half(dims):
    return lax.broadcasted_iota(jnp.int32, dims, 1) % 128 < HD


def pack_pair(first, second):
    left = lane_half(first.shape)
    return (
        jnp.where(left, first, pltpu.roll(second, HD, 1)).astype(BF),
        jnp.where(left, pltpu.roll(first, HD, 1), second).astype(BF),
    )


MESH = pl.DeviceIdType.MESH
HALF = D // 2
WIDE = 4 * HALF + 128
SMALL, OUT = 3 * HALF, 3 * HALF + 128
GATHER_PARTS = ((pl.ds(0, 896), "xzy"), (pl.ds(896, 768), "xyz"))
LATE_PARTS = ((pl.ds(OUT, 256), "xzy"), (pl.ds(OUT + 256, 256), "xyz"))
REDUCE_PARTS = (
    (pl.ds(0, 1024), "zyx"), (pl.ds(1024, 768), "yzx"), (pl.ds(1792, 256), "xyz"), (pl.ds(2048, 128), "yzx"),
)
MAIN = pl.ds(0, 4 * HALF)
REST = pl.ds(4 * HALF, 128)


def coords():
    e, f = lax.axis_index("expert"), lax.axis_index("fsdp")
    return lax.div(e, 4), lax.rem(e, 4), lax.div(f, 2), lax.rem(f, 2)


def device(z, y, x, c):
    return (z * 4 + y, x * 2 + c)


def ring(at, step):
    return lax.rem(at + step, 4)


def greet(peers):
    barrier = pltpu.get_barrier_semaphore()
    for peer in peers:
        pl.semaphore_signal(barrier, inc=1, device_id=peer, device_id_type=MESH)
    pl.semaphore_wait(barrier, len(peers))


class Copies:
    def __init__(self, send_sem, recv_sem):
        self.send_sem, self.recv_sem, self.started = send_sem, recv_sem, []

    def go(self, src, dst, peer):
        at = len(self.started)
        copy = pltpu.make_async_remote_copy(
            src_ref=src,
            dst_ref=dst,
            send_sem=self.send_sem.at[at],
            recv_sem=self.recv_sem.at[at],
            device_id=peer,
            device_id_type=MESH,
        )
        copy.start()
        self.started.append(copy)
        return copy

    def drain(self):
        for copy in self.started:
            copy.wait_send()


def plane_peers():
    e, f = lax.axis_index("expert"), lax.axis_index("fsdp")
    return [(lax.rem(e + k, EXPERTS), f) for k in range(1, EXPERTS)]


class Exchange:
    def __init__(self, held, landed, send_sem, recv_sem, rows=None):
        self.held, self.landed, self.send_sem, self.recv_sem = held, landed, send_sem, recv_sem
        self.rows = rows or pl.ds(0, held.shape[1])
        self.me, self.f = lax.axis_index("expert"), lax.axis_index("fsdp")

    def copy(self, to):
        step = lax.rem(to - self.me + EXPERTS, EXPERTS)
        return pltpu.make_async_remote_copy(
            src_ref=self.held.at[to, self.rows],
            dst_ref=self.landed.at[self.me, self.rows],
            send_sem=self.send_sem.at[step],
            recv_sem=self.recv_sem.at[step],
            device_id=(to, self.f),
            device_id_type=MESH,
        )

    def others(self, act):
        def body(k, carry):
            act(self.copy(lax.rem(self.me + k, EXPERTS)))
            return carry

        lax.fori_loop(1, EXPERTS, body, 0)

    def keep(self):
        self.landed[self.me, self.rows] = self.held[self.me, self.rows]

    def push(self, to):
        @pl.when(to != self.me)
        def _():
            self.copy(to).start()

        @pl.when(to == self.me)
        def _():
            self.keep()

    def start(self):
        self.others(lambda copy: copy.start())
        self.keep()

    def arrive(self):
        self.others(lambda copy: copy.wait_recv())

    def drain(self):
        self.others(lambda copy: copy.wait_send())


def spread(value):
    half = D // 2
    parts = [value[:, at : at + half].reshape(EXPERTS, 2 * CAP, half) for at in (0, half)]
    return jnp.concatenate(parts, axis=1).astype(BF)


def unspread(into, *refs):
    half = D // 2
    value = jnp.concatenate([ref[...].astype(F32) for ref in refs], axis=1)
    for side in range(2):
        part = value[:, side * 2 * CAP : (side + 1) * 2 * CAP, :].reshape(BUF, half)
        into[:, side * half : (side + 1) * half] = part.astype(BF)


class Place:
    def __init__(self):
        self.z, self.y, self.x, self.c = coords()
        self.at = {"z": self.z, "y": self.y, "x": self.x}
        self.twin = device(self.z, self.y, self.x, 1 - self.c)

    def moved(self, axis, step):
        return {**self.at, axis: ring(self.at[axis], step)}

    def peer(self, axis, step):
        to = self.moved(axis, step)
        return device(to["z"], to["y"], to["x"], self.c)

    def peers(self, axes):
        return [self.peer(axis, k) for axis in axes for k in (1, 2, 3)]


class Gather:
    def __init__(self, place, box, copies, lanes, order):
        self.place, self.box, self.copies, self.lanes, self.order = place, box, copies, lanes, order
        self.phases, self.forwards = [], []

    def region(self, known, at):
        spots = tuple(slice(None) if axis in known else at[axis] for axis in "zyx")
        return self.box.at[spots + (self.place.c, slice(None), self.lanes)]

    def start(self, phase):
        axis, known = self.order[phase], self.order[:phase]
        here = self.region(known, self.place.at)
        self.phases.append([self.copies.go(here, here, self.place.peer(axis, k)) for k in (1, 2, 3)])

    def forward_own(self):
        here = self.region("", self.place.at)
        self.forwards.append(self.copies.go(here, here, self.place.twin))

    def forward(self, phase, k):
        axis, known = self.order[phase], self.order[:phase]
        got = self.region(known, self.place.moved(axis, 4 - k))
        self.forwards.append(self.copies.go(got, got, self.place.twin))

    def start_relay(self, phase):
        axis, known = self.order[phase], self.order[:phase]
        here = self.region(known, self.place.at)
        self.phases.append([self.copies.go(here, here, self.place.peer(axis, k)) for k in (1, 3)])

    def arrive_relay(self, phase):
        axis, known = self.order[phase], self.order[:phase]
        lanes, middle = self.lanes, (self.lanes.size // 256) * 128
        relayed = []
        for copy, k, start, size in zip(
            self.phases[phase], (1, 3), (lanes.start, lanes.start + middle), (middle, lanes.size - middle)
        ):
            copy.wait_recv()
            self.lanes = pl.ds(start, size)
            got = self.region(known, self.place.moved(axis, 4 - k))
            relayed.append(self.copies.go(got, got, self.place.peer(axis, k)))
            self.lanes = lanes
            self.forward(phase, k)
        for copy in relayed:
            copy.wait_recv()
        self.forward(phase, 2)

    def arrive(self, phase, forward=False):
        for k, copy in enumerate(self.phases[phase]):
            copy.wait_recv()
            if forward:
                self.forward(phase, k + 1)

    def forward_all(self, phase):
        for k in (1, 2, 3):
            self.forward(phase, k)

    def finish(self):
        for copy in self.forwards:
            copy.wait_recv()


class Reduce:
    def __init__(self, place, copies, order, first, held, landed):
        self.place, self.copies, self.order = place, copies, order
        self.sources, self.landed, self.started = [first] + list(held), landed, [[], [], []]

    def pick(self, phase, spot):
        left = [axis for axis in "zyx" if axis in self.order[phase:]]
        return tuple(spot if axis == self.order[phase] else slice(None) for axis in left)

    def send(self, phase, k):
        axis = self.order[phase]
        src, lanes = self.sources[phase]
        spots = self.pick(phase, ring(self.place.at[axis], k))
        src = src.at[spots + (slice(None), lanes)]
        self.started[phase].append(
            self.copies.go(src, self.landed[phase].at[k - 1], self.place.peer(axis, k))
        )

    def start(self, phase):
        for k in (1, 2, 3):
            self.send(phase, k)

    def total(self, phase):
        for copy in self.started[phase]:
            copy.wait_recv()
        src, lanes = self.sources[phase]
        spots = self.pick(phase, self.place.at[self.order[phase]])
        value = src[spots + (slice(None), lanes)].astype(F32)
        for k in range(3):
            value = value + self.landed[phase][k].astype(F32)
        if phase < 2:
            nxt, width = self.sources[phase + 1]
            nxt[...] = value.astype(BF)
        return value


def reduce_scratch(width):
    return [
        pltpu.VMEM((4, 4, 16, width), BF), pltpu.VMEM((4, 16, width), BF),
        pltpu.VMEM((3, 4, 4, 16, width), BF), pltpu.VMEM((3, 4, 16, width), BF), pltpu.VMEM((3, 16, width), BF),
    ]


def folded(value):
    return jnp.concatenate([value[:, : D // 2], value[:, D // 2 :]], axis=0)


def unfolded(value):
    return jnp.concatenate([value[:8], value[8:]], axis=1)


def fold_rows(value):
    half = D // 2
    return jnp.concatenate(
        [value[:, at : at + half].reshape(32, 8, half) for at in (0, half)], axis=1
    )


def unfold_into(ref, plane, value):
    half = D // 2
    rows = slice(plane * 256, plane * 256 + 256)
    ref[rows, :half] = value[:, :8, :].reshape(256, half).astype(BF)
    ref[rows, half:] = value[:, 8:, :].reshape(256, half).astype(BF)


def lane_pick():
    col = lax.broadcasted_iota(jnp.int32, (128, D), 1)
    return (lax.rem(col, 8) == lax.broadcasted_iota(jnp.int32, (128, D), 0)).astype(BF)


def own_columns():
    col = lax.broadcasted_iota(jnp.int32, (128, D), 1)
    low = lax.broadcasted_iota(jnp.int32, (128, D), 0) * 8
    return (col >= low) & (col < low + 8)


def by_device(row):
    high, low = halves(jnp.where(own_columns(), row, 0.0))
    pick = lane_pick()
    return nt(high, pick) + nt(low, pick)


def pick_row(values, row):
    at = lax.broadcasted_iota(jnp.int32, values.shape, values.ndim - 2)
    return jnp.sum(jnp.where(at == row, values, 0.0), axis=-2)


def gather_part(
    place, x_ref, wq_ref, wk_ref, wv_ref, wo_ref, small_ref, place_ref, dy_ref,
    normed_ref, land_ref, dy_land, wq_out, wk_out, wv_out, wr_out, gain_out, tab_out,
    box, out_ref, dy_hold, send_sem, recv_sem, sems,
):
    z, y, x, c = place.z, place.y, place.x, place.c
    for at, w_ref in ((0, wq_ref), (HALF, wk_ref), (2 * HALF, wv_ref), (OUT, wo_ref)):
        box[z, y, x, c, :, at : at + HALF] = folded(w_ref[...].astype(F32)).astype(BF)
    box[z, y, x, c, :, SMALL:OUT] = small_ref[...]
    greet(plane_peers() + place.peers("x") + [place.twin])
    copies = Copies(send_sem, recv_sem)
    trade = Exchange(out_ref, land_ref, sems[0], sems[1])
    early = Exchange(dy_hold, dy_land, sems[2], sems[3])
    both = [Gather(place, box, copies, lanes, order) for lanes, order in GATHER_PARTS]
    late = [Gather(place, box, copies, lanes, order) for lanes, order in LATE_PARTS]
    for part in both:
        part.start(0)
    for part in both + late:
        part.forward_own()
    for part in late:
        part.start(0)
    tokens = x_ref[...].astype(F32)
    unit = tokens * lax.rsqrt(jnp.mean(tokens * tokens, axis=-1, keepdims=True) + EPS)
    for part in both:
        part.arrive(0)
        part.start(1)
    for part in both:
        part.forward_all(0)
    for part in both:
        part.arrive(1)
        part.start_relay(2)
    for part in both:
        part.forward_all(1)
    dy_hold[...] = spread(nn(place_ref[...], dy_ref[...]))
    for part in both:
        part.arrive_relay(2)
    for part in late:
        part.arrive(0, forward=True)
        part.start(1)
    for part in both:
        part.finish()

    for k, w_out in enumerate((wq_out, wk_out, wv_out)):
        unfold(box, k * HALF, w_out)
    small = box[:, :, :, :, :, SMALL:OUT].reshape(128, 16, 128).astype(F32)
    lane = lax.broadcasted_iota(jnp.int32, (D, 128), 1)
    wr_out[...] = jnp.where(lane < EXPERTS, small[:, :8, :].reshape(D, 128), 0.0).astype(BF)
    pick, mine = lane_pick(), own_columns()
    gains = [
        jnp.sum(jnp.where(mine, nn(pick_row(small[:, 8:, :], row).astype(BF), pick), 0.0), axis=0, keepdims=True)
        for row in range(2)
    ]
    gain_out[...] = jnp.concatenate(gains + [jnp.zeros((6, D), F32)], axis=0)
    near = box[z, y, :, :, :, SMALL:OUT].reshape(8, 16, 128).astype(F32)
    tab_out[...] = pick_row(near, 10)

    normed = (unit * gains[0]).astype(BF)
    normed_ref[...] = normed
    for k in (1, 2, 3, 0):
        part = ring(z, k)
        for which, w_ref in enumerate((wq_out, wk_out, wv_out)):
            res = nn(normed, w_ref[:, pl.ds(pl.multiple_of(part * 256, 256), 256)])
            for pair in range(2):
                head = part * 4 + pair * 2
                cols = slice(pair * 128, pair * 128 + 128)
                first, second = pack_pair(res[:TS, cols], res[TS:, cols])
                out_ref[head, which * TS : (which + 1) * TS, :] = first
                out_ref[head + 1, which * TS : (which + 1) * TS, :] = second
        if k == 1:
            for part_late in late:
                part_late.arrive(1, forward=True)
                part_late.start(2)
        for j in (1, 2, 3, 0):
            if k or j:
                trade.copy(part * 4 + ring(y, j)).start()
            else:
                trade.keep()
    early.start()
    return copies, trade, early, late


def unfold(box, at, w_out):
    for plane in range(4):
        value = box[plane, :, :, :, :, at : at + HALF].reshape(32, 16, HALF)
        unfold_into(w_out, plane, value.astype(F32))


def attn_setup(len_ref, recv_ref, kext, qext):
    rows = lax.broadcasted_iota(jnp.int32, (SEQ, 128), 0)
    lanes = lax.broadcasted_iota(jnp.int32, (SEQ, 128), 1)
    end1 = [len_ref[m, 0] for m in range(2)]
    end2 = [len_ref[m, 0] + len_ref[m, 1] for m in range(2)]
    kfeat = jnp.where(lanes == 4, 1.0, 0.0)
    for m in range(2):
        kfeat = jnp.where((lanes == 2 * m) & (rows < end1[m]), 1.0, kfeat)
        kfeat = jnp.where((lanes == 2 * m + 1) & (rows < end2[m]), 1.0, kfeat)
    kext[:, 128:] = kfeat.astype(BF)
    for i in range(EXPERTS):
        kext[i * TS : (i + 1) * TS, :128] = recv_ref[i, TS : 2 * TS, :]
    left = lane_half((TS, 128))
    row_in = lax.broadcasted_iota(jnp.int32, (TS, 128), 0)
    lane_in = lax.broadcasted_iota(jnp.int32, (TS, 128), 1)
    for i in range(EXPERTS):
        q2 = recv_ref[i, 0:TS, :].astype(F32) * (HD**-0.5)
        pos = row_in + i * TS
        for m in range(2):
            keep = left if m == 0 else jnp.logical_not(left)
            qext[i, m * TS : (m + 1) * TS, :128] = jnp.where(keep, q2, 0.0).astype(BF)
            feat = jnp.where((lane_in == 2 * m) & (pos >= end1[m]), MASKED, 0.0)
            feat = jnp.where((lane_in == 2 * m + 1) & (pos >= end2[m]), MASKED, feat)
            qext[i, m * TS : (m + 1) * TS, 128:] = feat.astype(BF)

def bias_setup(tab_ref, bias):
    row_in = lax.broadcasted_iota(jnp.int32, (TS, 128), 0)
    lane_in = lax.broadcasted_iota(jnp.int32, (TS, 128), 1)
    for block in range(12):
        dist = 1024 - block * TS + lane_in - row_in
        if block in (7, 8):
            value = jnp.broadcast_to(tab_ref[0:1, 0:1], (TS, 128))
            for bucket, edge in enumerate(EDGES):
                b = bucket + 1
                value = jnp.where(dist >= edge, tab_ref[b // 4 : b // 4 + 1, b % 4 : b % 4 + 1], value)
        else:
            value = jnp.broadcast_to(tab_ref[7:8, 3:4], (TS, 128))
        value = jnp.where((dist >= 0) & (dist < WINDOW), value, MASKED)
        bias[block * TS : (block + 1) * TS, :128] = value
        bias[block * TS : (block + 1) * TS, 128:] = value


def eye(size):
    return (
        lax.broadcasted_iota(jnp.int32, (size, size), 0)
        == lax.broadcasted_iota(jnp.int32, (size, size), 1)
    ).astype(BF)


def strips(strip, after):
    def run(low, count):
        def body(at, carry):
            i = low + at
            strip(i + 8, 9, i)
            strip(i, count, 0)
            after(i)
            return carry

        lax.fori_loop(0, 4, body, 0)

    run(0, 4)
    run(4, 8)


def span(block, count):
    return pl.ds(pl.multiple_of(block * TS, TS), count * TS)


def attn_fwd_part(len_ref, recv_ref, land_ref, lse_ref, kext, qext, bias, vt, out_ref, sems):
    trade = Exchange(out_ref, land_ref, sems[0], sems[1])
    attn_setup(len_ref, recv_ref, kext, qext)
    unit = eye(TS)
    for i in range(EXPERTS):
        vt[:, i * TS : (i + 1) * TS] = nt(unit, recv_ref[i, 2 * TS : 3 * TS, :]).astype(BF)

    def strip(i, count, first):
        s = nt(kext[span(first, count), :], qext[i]) + bias[span(first - i + 8, count), :]
        top = jnp.max(s, axis=0, keepdims=True)
        p = jnp.exp(s - top)
        total = jnp.sum(p, axis=0, keepdims=True)
        res = nn(vt[:, span(first, count)], p.astype(BF)) / total
        both = jnp.concatenate([res[:HD, :TS], res[HD:, TS:]], axis=0)
        out_ref[i] = both.T.astype(BF)
        lse_ref[i] = jnp.broadcast_to(top + jnp.log(total), (8, TOK))

    def after(i):
        trade.push(i + 8)
        trade.push(i)

    strips(strip, after)
    return trade


def head_kernel(
    len_ref, x_ref, wq_ref, wk_ref, wv_ref, wo_ref, small_ref, place_ref, dy_ref,
    normed_ref, heads_ref, dy_land, wq_out, wk_out, wv_out, wo_out, wr_out, gain_out, tab_out, att_land, lse_ref,
    box, head_hold, dy_hold, kext, qext, bias, vt, att_hold, send_sem, recv_sem, *sems,
):
    copies, trade, early, late = gather_part(
        Place(), x_ref, wq_ref, wk_ref, wv_ref, wo_ref, small_ref, place_ref, dy_ref,
        normed_ref, heads_ref, dy_land, wq_out, wk_out, wv_out, wr_out, gain_out, tab_out,
        box, head_hold, dy_hold, send_sem, recv_sem, sems[0:4],
    )
    bias_setup(tab_out, bias)
    trade.arrive()
    for part in late:
        part.arrive(2, forward=True)
    back = attn_fwd_part(len_ref, heads_ref, att_land, lse_ref, kext, qext, bias, vt, att_hold, sems[4:6])
    for part in late:
        part.finish()
    unfold(box, OUT, wo_out)
    for sent in (back, early):
        sent.arrive()
    for sent in (trade, back, early):
        sent.drain()
    copies.drain()


def attn_bwd_part(
    len_ref, tab_ref, recv_ref, dout_ref, lse_ref, land_ref, tab_out_ref,
    kext, qext, bias, ktext, dk, dv, near, far, out_ref, sems, ready, meanwhile,
):
    trade_q = Exchange(out_ref, land_ref, sems[0], sems[1], pl.ds(0, TS))
    trade_kv = Exchange(out_ref, land_ref, sems[2], sems[3], pl.ds(TS, 2 * TS))
    attn_setup(len_ref, recv_ref, kext, qext)
    bias_setup(tab_ref, bias)
    unit = eye(256)
    for i in range(EXPERTS):
        ktext[:, i * TS : (i + 1) * TS] = nt(unit, kext[i * TS : (i + 1) * TS, :])[:144].astype(BF)
    dk[...] = jnp.zeros_like(dk)
    dv[...] = jnp.zeros_like(dv)
    near[...] = jnp.zeros_like(near)
    far[...] = jnp.zeros_like(far)
    left = lane_half((TS, 128))

    def strip(i, count, first):
        q = qext[i]
        s = nt(kext[span(first, count), :], q) + bias[span(first - i + 8, count), :]
        p = jnp.exp(s - lse_ref[i][0:1])
        do2 = dout_ref[i]
        zero = jnp.zeros_like(do2)
        do = jnp.concatenate([jnp.where(left, do2, zero), jnp.where(left, zero, do2)], axis=0)
        if count == 9:
            v = recv_ref[pl.ds(first, count), 2 * TS : 3 * TS, :].reshape(count * TS, 128)
        else:
            v = recv_ref[0:count, 2 * TS : 3 * TS, :].reshape(count * TS, 128)
        dp = nt(v, do)
        inner = jnp.sum(p * dp, axis=0, keepdims=True)
        ds = (p * (dp - inner)).astype(BF)
        dv[span(first, count), :] += nn(p.astype(BF), do)
        dk[span(first, count), :] += nn(ds, q[:, :128])
        dqt = nn(ktext[:, span(first, count)], ds)
        both = jnp.concatenate([dqt[:HD, :TS], dqt[HD : 2 * HD, TS:]], axis=0) * (HD**-0.5)
        out_ref[i, 0:TS, :] = both.T.astype(BF)
        far[...] += dqt[128:136]
        if count == 9:
            near[...] += ds[7 * TS :].astype(F32)
        else:
            for block in range(count):
                value = ds[block * TS : (block + 1) * TS].astype(F32)
                near[TS:] += value * (i == block).astype(F32)
                near[:TS] += value * (i == block + 1).astype(F32)

    def finish(i):
        out_ref[i, TS : 2 * TS, :] = dk[span(i, 1), :].astype(BF)
        out_ref[i, 2 * TS :, :] = dv[span(i, 1), :].astype(BF)
        trade_kv.push(i)

    ready()

    odd = lax.rem(trade_kv.me, 2)

    def first_half(low, count):
        def body(at, carry):
            i = low + 2 * at
            strip(i, count, 0)
            strip(i + 1, count, 0)
            trade_q.push(i)
            trade_q.push(i + 1)
            return carry

        lax.fori_loop(0, 2, body, 0)

    first_half(0, 4)
    first_half(4, 8)

    def second_half(at, carry):
        blocks = [odd * (8 + step) + (1 - odd) * (15 - step) for step in (2 * at, 2 * at + 1)]
        for i in blocks:
            strip(i, 9, i - 8)
        for i in blocks:
            trade_q.push(i)
            finish(i - 8 * odd)
        return carry

    lax.fori_loop(0, 4, second_half, 0)

    def rest(step, carry):
        finish(lax.rem(step + lax.div(trade_kv.me, 2), 8) + 8 * odd)
        return carry

    lax.fori_loop(0, 8, rest, 0)
    grads = near[:, :TS] + near[:, TS:]
    dist = (
        TS
        + lax.broadcasted_iota(jnp.int32, (TOK, TS), 1)
        - lax.broadcasted_iota(jnp.int32, (TOK, TS), 0)
    )
    total = jnp.sum(far[4:5, :])
    lane = lax.broadcasted_iota(jnp.int32, (8, 128), 1)
    lane = jnp.where(lane < 4, lane + 4 * lax.broadcasted_iota(jnp.int32, (8, 128), 0), NB)
    res = jnp.zeros((8, 128), F32)
    lows = (0,) + EDGES
    seen = 0.0
    for b in range(NB - 1):
        part = jnp.sum(jnp.where((dist >= lows[b]) & (dist < lows[b + 1]), grads, 0.0))
        seen = seen + part
        res = jnp.where(lane == b, part, res)
    res = jnp.where(lane == NB - 1, total - seen, res)
    tab_out_ref[...] = res
    meanwhile()
    for trade in (trade_q, trade_kv):
        trade.arrive()
    return trade_q, trade_kv


def row_expert():
    row = lax.broadcasted_iota(jnp.int32, (BUF, 128), 0)
    lane = lax.broadcasted_iota(jnp.int32, (BUF, 128), 1) * (2 * CAP)
    return (row >= lane) & (row < lane + 2 * CAP)


def unpack_heads(recv_ref, lo, emit):
    for pair in range(H // 2):
        one = recv_ref[2 * pair, lo : lo + TS, :].astype(F32)
        two = recv_ref[2 * pair + 1, lo : lo + TS, :].astype(F32)
        first, second = pack_pair(one, two)
        emit(pair, first, second)


def slot_share(place, share_e, own):
    high, low = halves(share_e)
    return jnp.sum(jnp.where(own, nn(place, high) + nn(place, low), 0.0), axis=1, keepdims=True)


CHUNKS = ((0, 768), (768, 768), (1536, 768), (2304, 512))


def pieces(at, size):
    found, row = [], at
    while row < at + size:
        end = min(at + size, (row // SHARD + 1) * SHARD)
        found.append((row // SHARD, row % SHARD, row - at, end - row))
        row = end
    return found


STAGED = 3 * sum(len(pieces(at, size)) for at, size in CHUNKS)


def moe_kernel(
    recv_ref, x_ref, wo_ref, gain_ref, wr_ref, mask_ref, place_ref, dy_ref, w_ref,
    att_ref, hidden_ref, mixed_ref, share_ref, back_out, back_row, grads_ref,
    w_buf, hold_a, hold_b, land_a, hold_s, land_s, rows, slots, act, first, second, acc, stage,
    w_sem, stage_sem, *sems,
):
    loads = [
        [
            pltpu.make_async_copy(
                w_ref.at[s, pl.ds(k * SHARD, SHARD)],
                w_buf.at[k, pl.ds(s * SHARD, SHARD)],
                w_sem.at[k * FSDP + s],
            )
            for s in range(FSDP)
        ]
        for k in range(3)
    ]
    for k in (2, 0, 1):
        for copy in loads[k]:
            copy.start()
    greet(plane_peers())
    to_rows = Exchange(hold_a, land_a, sems[0], sems[1])
    to_shares = Exchange(hold_s, land_s, sems[2], sems[3])
    from_out = Exchange(hold_a, back_out, sems[4], sems[5])
    from_row = Exchange(hold_b, back_row, sems[6], sems[7])

    def emit(pair, one, two):
        att_ref[0:TS, pair * 128 : pair * 128 + 128] = one
        att_ref[TS:, pair * 128 : pair * 128 + 128] = two

    unpack_heads(recv_ref, 0, emit)
    hidden = x_ref[...].astype(F32) + nn(att_ref[...], wo_ref[...])
    hidden_ref[...] = hidden
    factor = lax.rsqrt(jnp.mean(hidden * hidden, axis=-1, keepdims=True) + EPS)
    mixed = (hidden * factor * gain_ref[1:2, :]).astype(BF)
    mixed_ref[...] = mixed
    place = place_ref[...]
    hold_a[...] = spread(nn(place, mixed))
    to_rows.start()
    picked = mask_ref[...] > 0
    logits = jnp.where(picked, nn(mixed, wr_ref[...]), MASKED)
    weight = jnp.exp(logits - jnp.max(logits, axis=1, keepdims=True))
    share = weight / jnp.sum(weight, axis=1, keepdims=True)
    share_ref[...] = share
    high, low = halves(slot_share(place, share, row_expert()))
    lane = lax.broadcasted_iota(jnp.int32, (BUF, 128), 1)
    value = jnp.where(lane == 0, high.astype(F32), 0.0) + jnp.where(lane == 1, low.astype(F32), 0.0)
    value = value.reshape(EXPERTS, 2 * CAP, 128)
    hold_s[...] = jnp.concatenate([value, jnp.zeros((EXPERTS, 8, 128), F32)], axis=1).astype(BF)
    to_shares.start()

    unspread(slots, dy_ref)
    for copy in loads[2]:
        copy.wait()
    for at, size in CHUNKS:
        first[:, at : at + size] = nt(slots[...], w_buf[2, at : at + size, :]).astype(BF)
    for k in range(2):
        for copy in loads[k]:
            copy.wait()
    to_rows.arrive()
    unspread(rows, land_a)
    for at, size in CHUNKS:
        cols = slice(at, at + size)
        gate = nt(rows[...], w_buf[0, cols, :])
        up = nt(rows[...], w_buf[1, cols, :])
        square = gate * gate
        tanh = jnp.tanh(GELU_C * gate * (1.0 + 0.044715 * square))
        half_up = 0.5 * (1.0 + tanh)
        gelu = gate * half_up
        slope = half_up + 0.5 * gate * (1.0 - tanh * tanh) * (
            GELU_C * (1.0 + 3 * 0.044715 * square)
        )
        act_grad = first[:, cols].astype(F32)
        act[:, cols] = (gelu * up).astype(BF)
        first[:, cols] = (act_grad * up * slope).astype(BF)
        second[:, cols] = (act_grad * gelu).astype(BF)
    for half in range(2):
        cols = slice(half * HALF, half * HALF + HALF)
        acc[:, cols] = nn(act[...], w_buf[2, :, cols])
    to_rows.drain()
    hold_a[...] = spread(acc[...])
    from_out.start()
    for half in range(2):
        cols = slice(half * HALF, half * HALF + HALF)
        acc[:, cols] = nn(first[...], w_buf[0, :, cols]) + nn(second[...], w_buf[1, :, cols])
    hold_b[...] = spread(acc[...])
    from_row.start()

    to_shares.arrive()
    value = land_s[...].astype(F32)[:, : 2 * CAP, :].reshape(BUF, 128)
    scale = jnp.sum(value, axis=1, keepdims=True)
    rows[...] = (rows[...].astype(F32) * scale).astype(BF)
    slots[...] = (slots[...].astype(F32) * scale).astype(BF)
    pending = [[], [], []]
    count = turn = 0
    for which, (left, right) in ((2, (act, slots)), (0, (first, rows)), (1, (second, rows))):
        for at, size in CHUNKS:
            value = tn(left[:, at : at + size], right[...]).astype(BF)
            for copy in pending[turn]:
                copy.wait()
            stage[turn, :size, :] = value
            pending[turn] = []
            for shard, row, local, amount in pieces(at, size):
                copy = pltpu.make_async_copy(
                    stage.at[turn, pl.ds(local, amount)],
                    grads_ref.at[shard, pl.ds(which * SHARD + row, amount)],
                    stage_sem.at[count],
                )
                copy.start()
                pending[turn].append(copy)
                count += 1
            turn = (turn + 1) % 3
    for group in pending:
        for copy in group:
            copy.wait()
    from_out.arrive()
    from_row.arrive()
    from_out.drain()
    from_row.drain()
    to_shares.drain()


def back_part(
    out_ref, row_ref, place_ref, place_t_ref, dy_ref, hidden_ref, mixed_ref, share_ref, wr_ref, gain_ref, wo_ref,
    result_ref, hgrad_ref, branch_ref, land_ref, router_ref, gain_out_ref,
    send_ref, outs, rows, send_sem, recv_sem,
):
    z, y, _, _ = coords()
    trade = Exchange(send_ref, land_ref, send_sem, recv_sem)
    unspread(outs, out_ref)
    unspread(rows, row_ref)
    place = place_ref[...]
    place_t = place_t_ref[...]
    own = row_expert()
    dy = dy_ref[...]
    returned = outs[...]
    dots = jnp.sum(nn(place, dy) * returned.astype(F32), axis=1, keepdims=True)
    high, low = halves(jnp.where(own, dots, 0.0))
    share = share_ref[...]
    share_grad = nn(place_t, high) + nn(place_t, low)
    inner = jnp.sum(share * share_grad, axis=1, keepdims=True)
    lg_high, lg_low = halves(share * (share_grad - inner))
    wr = wr_ref[...]
    scale_high, scale_low = halves(
        place_t.astype(F32) * slot_share(place, share, own).T
    )
    mixed_grad = (nn(scale_high, rows[...]) + nn(scale_low, rows[...])) + (
        nt(lg_high, wr) + nt(lg_low, wr)
    )
    hidden = hidden_ref[...]
    factor = lax.rsqrt(jnp.mean(hidden * hidden, axis=-1, keepdims=True) + EPS)
    unit = hidden * factor
    gain_out_ref[...] = jnp.broadcast_to(jnp.sum(mixed_grad * unit, axis=0, keepdims=True), (8, D))
    scaled = mixed_grad * gain_ref[1:2, :]
    hgrad = dy.astype(F32) + factor * (
        scaled - unit * jnp.mean(scaled * unit, axis=-1, keepdims=True)
    )
    hgrad_ref[...] = hgrad
    branch = hgrad.astype(BF)
    branch_ref[...] = branch
    for k in (1, 2, 3, 0):
        part = ring(z, k)
        res = nt(branch, wo_ref[pl.ds(pl.multiple_of(part * 256, 256), 256), :])
        for pair in range(2):
            head = part * 4 + pair * 2
            cols = slice(pair * 128, pair * 128 + 128)
            one, two = pack_pair(res[:TS, cols], res[TS:, cols])
            send_ref[head] = one
            send_ref[head + 1] = two
        for j in (1, 2, 3, 0):
            if k or j:
                trade.copy(part * 4 + ring(y, j)).start()
            else:
                trade.keep()
    mixed = mixed_ref[...]
    router_ref[...] = tn(mixed, lg_high) + tn(mixed, lg_low)
    moe = nn(scale_high, returned) + nn(scale_low, returned)
    result_ref[...] = (hidden + moe).astype(BF)
    return trade


def final_part(
    place, copies, recv_ref, normed_ref, x_ref, gains_ref, hgrad_ref, wq_ref, wk_ref, wv_ref,
    router_ref, moe_gain_ref, table_ref, igrad_ref, sum_ref,
    flat_q, flat_k, flat_v, box, from_twin, rest,
):
    z, y, c = place.z, place.y, place.c
    parts = [
        Reduce(
            place, copies, order, (from_twin, lanes),
            [(bufs[0], pl.ds(0, lanes.size)), (bufs[1], pl.ds(0, lanes.size))], bufs[2:],
        )
        for (lanes, order), bufs in zip(REDUCE_PARTS, (rest[0:5], rest[5:10], rest[10:15], rest[15:20]))
    ]
    flats = (flat_q, flat_k, flat_v)
    for which, flat in enumerate(flats):

        def emit(pair, first, second):
            flat[0:TS, pair * 128 : pair * 128 + 128] = first
            flat[TS:, pair * 128 : pair * 128 + 128] = second

        unpack_heads(recv_ref, which * TS, emit)

    planes = [ring(z, k) for k in (1, 2, 3, 0)]
    to_twin = []

    def pair_sum(k):
        plane = planes[k]
        to_twin[k].wait_recv()
        both = box[plane, :, :, c, :, MAIN].astype(F32) + from_twin[plane, :, :, :, MAIN].astype(F32)
        from_twin[plane, :, :, :, MAIN] = both.astype(BF)
        if k < 3:
            parts[0].send(0, k + 1)

    for k, plane in enumerate(planes):
        for which, flat in enumerate(flats):
            plane_grads(box, plane, which, normed_ref, flat)
        to_twin.append(
            copies.go(
                box.at[plane, :, :, 1 - c, :, MAIN], from_twin.at[plane, :, :, :, MAIN], place.twin
            )
        )
        if k:
            pair_sum(k - 1)
    pair_sum(3)
    parts[1].start(0)
    parts[2].start(0)

    total = nt(flat_q[...], wq_ref[...]) + nt(flat_k[...], wk_ref[...]) + nt(flat_v[...], wv_ref[...])
    tokens = x_ref[...].astype(F32)
    factor = lax.rsqrt(jnp.mean(tokens * tokens, axis=-1, keepdims=True) + EPS)
    unit = tokens * factor

    at = lax.broadcasted_iota(jnp.int32, (128, 8, 128), 1)
    gains = [by_device(row) for row in (jnp.sum(total * unit, axis=0, keepdims=True), moe_gain_ref[0:1, :])]
    lower = jnp.where(at == 0, gains[0][:, None, :], 0.0) + jnp.where(at == 1, gains[1][:, None, :], 0.0)
    extra = jnp.concatenate([router_ref[...].reshape(128, 8, 128), lower], axis=1)
    box[:, :, :, :, :, REST] = extra.astype(BF).reshape(4, 4, 4, 2, 16, 128)
    at = lax.broadcasted_iota(jnp.int32, (8, 16, 128), 1)
    here = box[z, y, :, :, :, REST].reshape(8, 16, 128).astype(F32)
    here = here + jnp.where(at == 10, table_ref[...][:, None, :], 0.0)
    box[z, y, :, :, :, REST] = here.astype(BF).reshape(4, 2, 16, 128)
    rest_copy = copies.go(
        box.at[:, :, :, 1 - c, :, REST], from_twin.at[:, :, :, :, REST], place.twin
    )
    rest_copy.wait_recv()
    both = box[:, :, :, c, :, REST].astype(F32) + from_twin[:, :, :, :, REST].astype(F32)
    from_twin[:, :, :, :, REST] = both.astype(BF)
    parts[3].start(0)
    scaled = total * gains_ref[0:1, :]
    igrad_ref[...] = (
        hgrad_ref[...]
        + factor * (scaled - unit * jnp.mean(scaled * unit, axis=-1, keepdims=True))
    ).astype(BF)
    for phase in range(2):
        for part in parts:
            part.total(phase)
            part.start(phase + 1)
    value = jnp.concatenate([part.total(2) for part in parts], axis=1)
    for which in range(4):
        sum_ref[which * 8 : which * 8 + 8, :] = unfolded(value[:, which * HALF : (which + 1) * HALF])
    sum_ref[32:48, 0:128] = value[:, 4 * HALF :]


def plane_grads(box, plane, which, left, right):
    cols = pl.ds(pl.multiple_of(plane * 256, 256), 256)
    value = fold_rows(tn(left[:, cols], right[...])).astype(BF)
    box[plane, :, :, :, :, which * HALF : (which + 1) * HALF] = value.reshape(4, 4, 2, 16, HALF)


def tail_kernel(
    len_ref, tab_ref, out_ref, row_ref, place_ref, place_t_ref, dy_ref, hidden_ref, mixed_ref, share_ref,
    wr_ref, gains_ref, wo_ref, heads_ref, lse_ref, normed_ref, x_ref, wq_ref, wk_ref, wv_ref, att_ref,
    result_ref, igrad_ref, sum_ref,
    hgrad, branch, head_grads, router, moe_gain, head_send, outs, rows,
    kext, qext, bias, ktext, dk, dv, near, far, grads_send, token_grads, table,
    flat_q, flat_k, flat_v, box, from_twin, *rest,
):
    place = Place()
    greet(plane_peers() + place.peers("x") + [place.twin])
    copies = Copies(rest[20], rest[21])
    sems = rest[22:]
    trade = back_part(
        out_ref, row_ref, place_ref, place_t_ref, dy_ref, hidden_ref, mixed_ref, share_ref, wr_ref, gains_ref,
        wo_ref, result_ref, hgrad, branch, head_grads, router, moe_gain, head_send, outs, rows, sems[0], sems[1],
    )

    def out_grads():
        for plane in range(4):
            plane_grads(box, plane, 3, att_ref, branch)

    trades = attn_bwd_part(
        len_ref, tab_ref, heads_ref, head_grads, lse_ref, token_grads, table,
        kext, qext, bias, ktext, dk, dv, near, far, grads_send, sems[2:6], trade.arrive, out_grads,
    )
    final_part(
        place, copies, token_grads, normed_ref, x_ref, gains_ref, hgrad, wq_ref, wk_ref, wv_ref,
        router, moe_gain, table, igrad_ref, sum_ref, flat_q, flat_k, flat_v, box, from_twin, rest,
    )
    for sent in (trade,) + trades:
        sent.drain()
    copies.drain()


def emit_kernel(expert_ref, sum_ref, gate, up, down, gq, gk, gv, go, router, gain_attn, gain_moe, table):
    for k, ref in enumerate((gate, up, down)):
        ref[...] = expert_ref[k * SHARD : (k + 1) * SHARD, :].astype(F32)
    for k, ref in enumerate((gq, gk, gv, go)):
        ref[...] = sum_ref[k * 8 : k * 8 + 8, :]
    router[...] = sum_ref[32:40, :EXPERTS]
    gain_attn[...] = sum_ref[40:41, :8]
    gain_moe[...] = sum_ref[41:42, :8]
    table[...] = sum_ref[42:43, :4]


def placement(routes, order):
    micro = routes.shape[0]
    slots = routes.reshape(micro, 2 * TS)
    rank_of = order.reshape(micro, 2 * TS)
    same = slots[:, :, None] == slots[:, None, :]
    earlier = rank_of[:, None, :] < rank_of[:, :, None]
    rank = jnp.sum((same & earlier).astype(jnp.int32), axis=2)
    base = slots * (2 * CAP) + jnp.arange(micro, dtype=jnp.int32)[:, None] * CAP
    target = jnp.where(rank < CAP, base + rank, BUF).reshape(micro * TS, 2)
    rows = jnp.arange(BUF, dtype=jnp.int32)
    place = (rows[:, None] == target[None, :, 0]) | (rows[:, None] == target[None, :, 1])
    place_t = (rows[None, :] == target[:, 0:1]) | (rows[None, :] == target[:, 1:2])
    return place.astype(BF), place_t.astype(BF)


def on_device(
    tokens, cotangent, doc_lengths, routes, order, gain_attn, w_query, w_key, w_value, w_out,
    rel_table, gain_moe, w_router, w_gate, w_up, w_down,
):
    expert_shard = jnp.concatenate([w_gate[0].T, w_up[0].T, w_down[0]], axis=0)
    expert_w = lax.all_gather(expert_shard, "fsdp", axis=0, tiled=False)

    def padded(value):
        return jnp.pad(value, ((0, 0), (0, 128 - value.shape[1])))

    small = jnp.concatenate(
        [padded(v) for v in (w_router, gain_attn[None], gain_moe[None], rel_table[None])]
        + [jnp.zeros((5, 128), BF)],
        axis=0,
    )
    place, place_t = placement(routes[:, 0], order[:, 0, 0])
    lanes = jnp.arange(128, dtype=jnp.int32)
    route_rows = routes.reshape(TOK, 2)
    picked = (
        (route_rows[:, 0:1] == lanes) | (route_rows[:, 1:2] == lanes)
    ).astype(F32)
    x = tokens.reshape(TOK, D)
    dy = cotangent.reshape(TOK, D)
    lengths = doc_lengths[:, 0]

    chunk = (EXPERTS, 4 * CAP, HALF)
    chunk = (EXPERTS, 4 * CAP, HALF)
    smem = pl.BlockSpec(memory_space=pltpu.SMEM)
    vmem = pl.BlockSpec(memory_space=pltpu.VMEM)
    attn_scratch = [
        pltpu.VMEM((SEQ, 256), BF), pltpu.VMEM((EXPERTS, TOK, 256), BF), pltpu.VMEM((12 * TS, TOK), F32),
    ]
    matrix = shape((D, D), BF)
    normed, heads, dy_rows, wq, wk, wv, wo, wr, gains, table, att_back, lse = call(
        head_kernel,
        (
            shape((TOK, D), BF), shape((H, 3 * TS, 128), BF), shape(chunk, BF), matrix, matrix, matrix, matrix,
            shape((D, 128), BF), shape((8, D), F32), shape((8, 128), F32),
            shape((EXPERTS, TS, 128), BF), shape((EXPERTS, 8, TOK), F32),
        ),
        lengths, x, w_query, w_key, w_value, w_out, small, place, dy,
        in_specs=[smem] + [vmem] * 8,
        scratch=[
            pltpu.VMEM((4, 4, 4, 2, 16, WIDE), BF), pltpu.VMEM((H, 3 * TS, 128), BF), pltpu.VMEM(chunk, BF),
        ]
        + attn_scratch
        + [pltpu.VMEM((128, SEQ), BF), pltpu.VMEM((EXPERTS, TS, 128), BF)]
        + [pltpu.SemaphoreType.DMA((78,))] * 2
        + [pltpu.SemaphoreType.DMA((EXPERTS,))] * 6,
        collective_id=1,
    )
    anywhere = pl.BlockSpec(memory_space=pl.ANY)
    att, hidden, mixed, share, outs, row_grads, expert_grads = call(
        moe_kernel,
        (
            shape((TOK, D), BF), shape((TOK, D), F32), shape((TOK, D), BF), shape((TOK, 128), F32),
            shape(chunk, BF), shape(chunk, BF), shape((FSDP, 3 * SHARD, D), BF),
        ),
        att_back, x, wo, gains, wr, picked, place, dy_rows, expert_w,
        in_specs=[vmem] * 8 + [anywhere],
        out_specs=(vmem,) * 6 + (anywhere,),
        scratch=[
            pltpu.VMEM((3, FF, D), BF),
            pltpu.VMEM(chunk, BF), pltpu.VMEM(chunk, BF), pltpu.VMEM(chunk, BF),
            pltpu.VMEM((EXPERTS, 48, 128), BF), pltpu.VMEM((EXPERTS, 48, 128), BF),
            pltpu.VMEM((BUF, D), BF), pltpu.VMEM((BUF, D), BF),
            pltpu.VMEM((BUF, FF), BF), pltpu.VMEM((BUF, FF), BF), pltpu.VMEM((BUF, FF), BF),
            pltpu.VMEM((BUF, D), F32),
            pltpu.VMEM((3, 768, D), BF),
            pltpu.SemaphoreType.DMA((3 * FSDP,)), pltpu.SemaphoreType.DMA((STAGED,)),
        ]
        + [pltpu.SemaphoreType.DMA((EXPERTS,))] * 8,
        collective_id=3,
    )
    expert_sum = lax.psum_scatter(
        expert_grads.reshape(FSDP * 3 * SHARD, D), "fsdp", scatter_dimension=0, tiled=True
    )
    result, input_grad, sums = call(
        tail_kernel,
        (shape((TOK, D), BF), shape((TOK, D), BF), shape((48, D), F32)),
        lengths, table, outs, row_grads, place, place_t, dy, hidden, mixed, share, wr, gains, wo,
        heads, lse, normed, x, wq, wk, wv, att,
        in_specs=[smem] + [vmem] * 20,
        scratch=[
            pltpu.VMEM((TOK, D), F32), pltpu.VMEM((TOK, D), BF), pltpu.VMEM((H, TS, 128), BF),
            pltpu.VMEM((D, 128), F32), pltpu.VMEM((8, D), F32), pltpu.VMEM((H, TS, 128), BF),
            pltpu.VMEM((BUF, D), BF), pltpu.VMEM((BUF, D), BF),
        ]
        + attn_scratch
        + [
            pltpu.VMEM((144, SEQ), BF), pltpu.VMEM((SEQ, 128), F32), pltpu.VMEM((SEQ, 128), F32),
            pltpu.VMEM((2 * TS, TOK), F32), pltpu.VMEM((8, TOK), F32),
            pltpu.VMEM((EXPERTS, 3 * TS, 128), BF), pltpu.VMEM((EXPERTS, 3 * TS, 128), BF),
            pltpu.VMEM((8, 128), F32),
            pltpu.VMEM((TOK, D), BF), pltpu.VMEM((TOK, D), BF), pltpu.VMEM((TOK, D), BF),
            pltpu.VMEM((4, 4, 4, 2, 16, WIDE), BF),
            pltpu.VMEM((4, 4, 4, 16, WIDE), BF),
        ]
        + [buf for lanes, _ in REDUCE_PARTS for buf in reduce_scratch(lanes.size)]
        + [pltpu.SemaphoreType.DMA((41,))] * 2
        + [pltpu.SemaphoreType.DMA((EXPERTS,))] * 6,
        collective_id=2,
    )
    block = shape((SHARD, D), F32)
    rows = shape((8, D), F32)
    gate, up, down, gq, gk, gv, go, router, gain_a, gain_m, table_sum = call(
        emit_kernel,
        (block, block, block, rows, rows, rows, rows)
        + tuple(shape(dims, F32) for dims in ((8, EXPERTS), (1, 8), (1, 8), (1, 4))),
        expert_sum, sums,
    )
    return (
        result.reshape(tokens.shape), input_grad.reshape(tokens.shape), gain_a[0], gq, gk, gv, go,
        table_sum[0], gain_m[0], router, gate.T[None], up.T[None], down[None],
    )


def solution(mesh):
    row = P(None, "fsdp", "expert", None)
    flat = P(("expert", "fsdp"))
    matrix = P(("expert", "fsdp"), None)
    columns = P("expert", None, "fsdp")
    deep = P("expert", "fsdp", None)
    return jax.shard_map(
        on_device,
        mesh=mesh,
        in_specs=(
            row, row, P(None, "fsdp", None), row, row, flat, matrix, matrix, matrix, matrix,
            flat, flat, matrix, columns, columns, deep,
        ),
        out_specs=(
            row, row, flat, matrix, matrix, matrix, matrix, flat, flat, matrix, columns, columns, deep,
        ),
        check_vma=False,
    )
```

```python
import jax
import jax.numpy as jnp
from jax import lax
from jax.experimental import pallas as pl
from jax.experimental.pallas import tpu as pltpu
from jax.sharding import PartitionSpec as P

H = 16
HD = 64
NB = 32
D = 1024
FF = 2816
WINDOW = 1024
EXPERTS = 16
CAP = 20
TS = 128
FSDP = 8
SHARD = FF // FSDP
TOK = 2 * TS
BUF = EXPERTS * 2 * CAP
SEQ = EXPERTS * TS
EPS = 1e-06
MASKED = -1e30
EDGES = tuple(range(1, 17)) + (19, 21, 24, 27, 31, 35, 40, 46, 52, 59, 67, 77, 87, 99, 113)
GELU_C = 0.7978845608028654
BF = jnp.bfloat16
F32 = jnp.float32
VMEM_LIMIT = 60 * 1024 * 1024


def nn(left, right):
    return lax.dot_general(left, right, (((1,), (0,)), ((), ())), preferred_element_type=F32)


def nt(left, right):
    return lax.dot_general(left, right, (((1,), (1,)), ((), ())), preferred_element_type=F32)


def tn(left, right):
    return lax.dot_general(left, right, (((0,), (0,)), ((), ())), preferred_element_type=F32)


def halves(value):
    high = value.astype(BF)
    return high, (value - high.astype(F32)).astype(BF)


def call(kernel, out_shape, *args, scratch=(), in_specs=None, out_specs=None, collective_id=None):
    return pl.pallas_call(
        kernel,
        out_shape=out_shape,
        in_specs=in_specs or [pl.BlockSpec(memory_space=pltpu.VMEM)] * len(args),
        out_specs=out_specs or jax.tree.map(lambda _: pl.BlockSpec(memory_space=pltpu.VMEM), out_shape),
        scratch_shapes=list(scratch),
        compiler_params=pltpu.CompilerParams(
            vmem_limit_bytes=VMEM_LIMIT,
            collective_id=collective_id,
            has_side_effects=collective_id is not None,
        ),
    )(*args)


def shape(dims, dtype):
    return jax.ShapeDtypeStruct(dims, dtype)


def lane_half(dims):
    return lax.broadcasted_iota(jnp.int32, dims, 1) % 128 < HD


def pack_pair(first, second):
    left = lane_half(first.shape)
    return (
        jnp.where(left, first, pltpu.roll(second, HD, 1)).astype(BF),
        jnp.where(left, pltpu.roll(first, HD, 1), second).astype(BF),
    )


MESH = pl.DeviceIdType.MESH
HALF = D // 2
WIDE = 4 * HALF + 128
SMALL, OUT = 3 * HALF, 3 * HALF + 128
GATHER_PARTS = ((pl.ds(0, 896), "xzy"), (pl.ds(896, 768), "xyz"))
LATE_PARTS = ((pl.ds(OUT, 256), "xzy"), (pl.ds(OUT + 256, 256), "xyz"))
REDUCE_PARTS = (
    (pl.ds(0, 1152), "zyx"), (pl.ds(1152, 640), "yzx"), (pl.ds(1792, 256), "xyz"), (pl.ds(2048, 128), "yzx"),
)
MAIN = pl.ds(0, 4 * HALF)
REST = pl.ds(4 * HALF, 128)


def coords():
    e, f = lax.axis_index("expert"), lax.axis_index("fsdp")
    return lax.div(e, 4), lax.rem(e, 4), lax.div(f, 2), lax.rem(f, 2)


def device(z, y, x, c):
    return (z * 4 + y, x * 2 + c)


def ring(at, step):
    return lax.rem(at + step, 4)


def greet(peers):
    barrier = pltpu.get_barrier_semaphore()
    for peer in peers:
        pl.semaphore_signal(barrier, inc=1, device_id=peer, device_id_type=MESH)
    pl.semaphore_wait(barrier, len(peers))


class Copies:
    def __init__(self, send_sem, recv_sem):
        self.send_sem, self.recv_sem, self.started = send_sem, recv_sem, []

    def go(self, src, dst, peer):
        at = len(self.started)
        copy = pltpu.make_async_remote_copy(
            src_ref=src,
            dst_ref=dst,
            send_sem=self.send_sem.at[at],
            recv_sem=self.recv_sem.at[at],
            device_id=peer,
            device_id_type=MESH,
        )
        copy.start()
        self.started.append(copy)
        return copy

    def drain(self):
        for copy in self.started:
            copy.wait_send()


def plane_peers():
    e, f = lax.axis_index("expert"), lax.axis_index("fsdp")
    return [(lax.rem(e + k, EXPERTS), f) for k in range(1, EXPERTS)]


class Exchange:
    def __init__(self, held, landed, send_sem, recv_sem, rows=None):
        self.held, self.landed, self.send_sem, self.recv_sem = held, landed, send_sem, recv_sem
        self.rows = rows or pl.ds(0, held.shape[1])
        self.me, self.f = lax.axis_index("expert"), lax.axis_index("fsdp")

    def copy(self, to):
        step = lax.rem(to - self.me + EXPERTS, EXPERTS)
        return pltpu.make_async_remote_copy(
            src_ref=self.held.at[to, self.rows],
            dst_ref=self.landed.at[self.me, self.rows],
            send_sem=self.send_sem.at[step],
            recv_sem=self.recv_sem.at[step],
            device_id=(to, self.f),
            device_id_type=MESH,
        )

    def others(self, act):
        def body(k, carry):
            act(self.copy(lax.rem(self.me + k, EXPERTS)))
            return carry

        lax.fori_loop(1, EXPERTS, body, 0)

    def keep(self):
        self.landed[self.me, self.rows] = self.held[self.me, self.rows]

    def push(self, to):
        @pl.when(to != self.me)
        def _():
            self.copy(to).start()

        @pl.when(to == self.me)
        def _():
            self.keep()

    def start(self):
        self.others(lambda copy: copy.start())
        self.keep()

    def arrive(self):
        self.others(lambda copy: copy.wait_recv())

    def drain(self):
        self.others(lambda copy: copy.wait_send())


def spread(value):
    half = D // 2
    parts = [value[:, at : at + half].reshape(EXPERTS, 2 * CAP, half) for at in (0, half)]
    return jnp.concatenate(parts, axis=1).astype(BF)


def unspread(into, *refs):
    half = D // 2
    value = jnp.concatenate([ref[...].astype(F32) for ref in refs], axis=1)
    for side in range(2):
        part = value[:, side * 2 * CAP : (side + 1) * 2 * CAP, :].reshape(BUF, half)
        into[:, side * half : (side + 1) * half] = part.astype(BF)


class Place:
    def __init__(self):
        self.z, self.y, self.x, self.c = coords()
        self.at = {"z": self.z, "y": self.y, "x": self.x}
        self.twin = device(self.z, self.y, self.x, 1 - self.c)

    def moved(self, axis, step):
        return {**self.at, axis: ring(self.at[axis], step)}

    def peer(self, axis, step):
        to = self.moved(axis, step)
        return device(to["z"], to["y"], to["x"], self.c)

    def peers(self, axes):
        return [self.peer(axis, k) for axis in axes for k in (1, 2, 3)]


class Gather:
    def __init__(self, place, box, copies, lanes, order):
        self.place, self.box, self.copies, self.lanes, self.order = place, box, copies, lanes, order
        self.phases, self.forwards = [], []

    def region(self, known, at):
        spots = tuple(slice(None) if axis in known else at[axis] for axis in "zyx")
        return self.box.at[spots + (self.place.c, slice(None), self.lanes)]

    def start(self, phase):
        axis, known = self.order[phase], self.order[:phase]
        here = self.region(known, self.place.at)
        self.phases.append([self.copies.go(here, here, self.place.peer(axis, k)) for k in (1, 2, 3)])

    def forward_own(self):
        here = self.region("", self.place.at)
        self.forwards.append(self.copies.go(here, here, self.place.twin))

    def forward(self, phase, k):
        axis, known = self.order[phase], self.order[:phase]
        got = self.region(known, self.place.moved(axis, 4 - k))
        self.forwards.append(self.copies.go(got, got, self.place.twin))

    def start_relay(self, phase):
        axis, known = self.order[phase], self.order[:phase]
        here = self.region(known, self.place.at)
        self.phases.append([self.copies.go(here, here, self.place.peer(axis, k)) for k in (1, 3)])

    def arrive_relay(self, phase):
        axis, known = self.order[phase], self.order[:phase]
        lanes, middle = self.lanes, (self.lanes.size // 256) * 128
        relayed = []
        for copy, k, start, size in zip(
            self.phases[phase], (1, 3), (lanes.start, lanes.start + middle), (middle, lanes.size - middle)
        ):
            copy.wait_recv()
            self.lanes = pl.ds(start, size)
            got = self.region(known, self.place.moved(axis, 4 - k))
            relayed.append(self.copies.go(got, got, self.place.peer(axis, k)))
            self.lanes = lanes
            self.forward(phase, k)
        for copy in relayed:
            copy.wait_recv()
        self.forward(phase, 2)

    def arrive(self, phase, forward=False):
        for k, copy in enumerate(self.phases[phase]):
            copy.wait_recv()
            if forward:
                self.forward(phase, k + 1)

    def forward_all(self, phase):
        for k in (1, 2, 3):
            self.forward(phase, k)

    def finish(self):
        for copy in self.forwards:
            copy.wait_recv()


class Reduce:
    def __init__(self, place, copies, order, first, held, landed):
        self.place, self.copies, self.order = place, copies, order
        self.sources, self.landed, self.started = [first] + list(held), landed, [[], [], []]

    def pick(self, phase, spot):
        left = [axis for axis in "zyx" if axis in self.order[phase:]]
        return tuple(spot if axis == self.order[phase] else slice(None) for axis in left)

    def send(self, phase, k):
        axis = self.order[phase]
        src, lanes = self.sources[phase]
        spots = self.pick(phase, ring(self.place.at[axis], k))
        src = src.at[spots + (slice(None), lanes)]
        self.started[phase].append(
            self.copies.go(src, self.landed[phase].at[k - 1], self.place.peer(axis, k))
        )

    def start(self, phase):
        for k in (1, 2, 3):
            self.send(phase, k)

    def total(self, phase):
        for copy in self.started[phase]:
            copy.wait_recv()
        src, lanes = self.sources[phase]
        spots = self.pick(phase, self.place.at[self.order[phase]])
        value = src[spots + (slice(None), lanes)].astype(F32)
        for k in range(3):
            value = value + self.landed[phase][k].astype(F32)
        if phase < 2:
            nxt, width = self.sources[phase + 1]
            nxt[...] = value.astype(BF)
        return value


def reduce_scratch(width):
    return [
        pltpu.VMEM((4, 4, 16, width), BF), pltpu.VMEM((4, 16, width), BF),
        pltpu.VMEM((3, 4, 4, 16, width), BF), pltpu.VMEM((3, 4, 16, width), BF), pltpu.VMEM((3, 16, width), BF),
    ]


def folded(value):
    return jnp.concatenate([value[:, : D // 2], value[:, D // 2 :]], axis=0)


def unfolded(value):
    return jnp.concatenate([value[:8], value[8:]], axis=1)


def fold_rows(value):
    half = D // 2
    return jnp.concatenate(
        [value[:, at : at + half].reshape(32, 8, half) for at in (0, half)], axis=1
    )


def unfold_into(ref, plane, value):
    half = D // 2
    rows = slice(plane * 256, plane * 256 + 256)
    ref[rows, :half] = value[:, :8, :].reshape(256, half).astype(BF)
    ref[rows, half:] = value[:, 8:, :].reshape(256, half).astype(BF)


def lane_pick():
    col = lax.broadcasted_iota(jnp.int32, (128, D), 1)
    return (lax.rem(col, 8) == lax.broadcasted_iota(jnp.int32, (128, D), 0)).astype(BF)


def own_columns():
    col = lax.broadcasted_iota(jnp.int32, (128, D), 1)
    low = lax.broadcasted_iota(jnp.int32, (128, D), 0) * 8
    return (col >= low) & (col < low + 8)


def by_device(row):
    high, low = halves(jnp.where(own_columns(), row, 0.0))
    pick = lane_pick()
    return nt(high, pick) + nt(low, pick)


def pick_row(values, row):
    at = lax.broadcasted_iota(jnp.int32, values.shape, values.ndim - 2)
    return jnp.sum(jnp.where(at == row, values, 0.0), axis=-2)


def gather_part(
    place, x_ref, wq_ref, wk_ref, wv_ref, wo_ref, small_ref, place_ref, dy_ref,
    normed_ref, land_ref, dy_land, wq_out, wk_out, wv_out, wr_out, gain_out, tab_out,
    box, out_ref, dy_hold, send_sem, recv_sem, sems,
):
    z, y, x, c = place.z, place.y, place.x, place.c
    for at, w_ref in ((0, wq_ref), (HALF, wk_ref), (2 * HALF, wv_ref), (OUT, wo_ref)):
        box[z, y, x, c, :, at : at + HALF] = folded(w_ref[...].astype(F32)).astype(BF)
    box[z, y, x, c, :, SMALL:OUT] = small_ref[...]
    greet(plane_peers() + place.peers("x") + [place.twin])
    copies = Copies(send_sem, recv_sem)
    trade = Exchange(out_ref, land_ref, sems[0], sems[1])
    early = Exchange(dy_hold, dy_land, sems[2], sems[3])
    both = [Gather(place, box, copies, lanes, order) for lanes, order in GATHER_PARTS]
    late = [Gather(place, box, copies, lanes, order) for lanes, order in LATE_PARTS]
    for part in both:
        part.start(0)
    for part in both + late:
        part.forward_own()
    for part in late:
        part.start(0)
    tokens = x_ref[...].astype(F32)
    unit = tokens * lax.rsqrt(jnp.mean(tokens * tokens, axis=-1, keepdims=True) + EPS)
    for part in both:
        part.arrive(0)
        part.start(1)
    for part in both:
        part.forward_all(0)
    for part in both:
        part.arrive(1)
        part.start_relay(2)
    for part in both:
        part.forward_all(1)
    dy_hold[...] = spread(nn(place_ref[...], dy_ref[...]))
    for part in both:
        part.arrive_relay(2)
    for part in late:
        part.arrive(0, forward=True)
        part.start(1)
    for part in both:
        part.finish()

    for k, w_out in enumerate((wq_out, wk_out, wv_out)):
        unfold(box, k * HALF, w_out)
    small = box[:, :, :, :, :, SMALL:OUT].reshape(128, 16, 128).astype(F32)
    lane = lax.broadcasted_iota(jnp.int32, (D, 128), 1)
    wr_out[...] = jnp.where(lane < EXPERTS, small[:, :8, :].reshape(D, 128), 0.0).astype(BF)
    pick, mine = lane_pick(), own_columns()
    gains = [
        jnp.sum(jnp.where(mine, nn(pick_row(small[:, 8:, :], row).astype(BF), pick), 0.0), axis=0, keepdims=True)
        for row in range(2)
    ]
    gain_out[...] = jnp.concatenate(gains + [jnp.zeros((6, D), F32)], axis=0)
    near = box[z, y, :, :, :, SMALL:OUT].reshape(8, 16, 128).astype(F32)
    tab_out[...] = pick_row(near, 10)

    normed = (unit * gains[0]).astype(BF)
    normed_ref[...] = normed
    for k in (1, 2, 3, 0):
        part = ring(z, k)
        for which, w_ref in enumerate((wq_out, wk_out, wv_out)):
            res = nn(normed, w_ref[:, pl.ds(pl.multiple_of(part * 256, 256), 256)])
            for pair in range(2):
                head = part * 4 + pair * 2
                cols = slice(pair * 128, pair * 128 + 128)
                first, second = pack_pair(res[:TS, cols], res[TS:, cols])
                out_ref[head, which * TS : (which + 1) * TS, :] = first
                out_ref[head + 1, which * TS : (which + 1) * TS, :] = second
        if k == 1:
            for part_late in late:
                part_late.arrive(1, forward=True)
                part_late.start(2)
        for j in (1, 2, 3, 0):
            if k or j:
                trade.copy(part * 4 + ring(y, j)).start()
            else:
                trade.keep()
    early.start()
    return copies, trade, early, late


def unfold(box, at, w_out):
    for plane in range(4):
        value = box[plane, :, :, :, :, at : at + HALF].reshape(32, 16, HALF)
        unfold_into(w_out, plane, value.astype(F32))


def attn_setup(len_ref, recv_ref, kext, qext):
    rows = lax.broadcasted_iota(jnp.int32, (SEQ, 128), 0)
    lanes = lax.broadcasted_iota(jnp.int32, (SEQ, 128), 1)
    end1 = [len_ref[m, 0] for m in range(2)]
    end2 = [len_ref[m, 0] + len_ref[m, 1] for m in range(2)]
    kfeat = jnp.where(lanes == 4, 1.0, 0.0)
    for m in range(2):
        kfeat = jnp.where((lanes == 2 * m) & (rows < end1[m]), 1.0, kfeat)
        kfeat = jnp.where((lanes == 2 * m + 1) & (rows < end2[m]), 1.0, kfeat)
    kext[:, 128:] = kfeat.astype(BF)
    for i in range(EXPERTS):
        kext[i * TS : (i + 1) * TS, :128] = recv_ref[i, TS : 2 * TS, :]
    left = lane_half((TS, 128))
    row_in = lax.broadcasted_iota(jnp.int32, (TS, 128), 0)
    lane_in = lax.broadcasted_iota(jnp.int32, (TS, 128), 1)
    for i in range(EXPERTS):
        q2 = recv_ref[i, 0:TS, :].astype(F32) * (HD**-0.5)
        pos = row_in + i * TS
        for m in range(2):
            keep = left if m == 0 else jnp.logical_not(left)
            qext[i, m * TS : (m + 1) * TS, :128] = jnp.where(keep, q2, 0.0).astype(BF)
            feat = jnp.where((lane_in == 2 * m) & (pos >= end1[m]), MASKED, 0.0)
            feat = jnp.where((lane_in == 2 * m + 1) & (pos >= end2[m]), MASKED, feat)
            qext[i, m * TS : (m + 1) * TS, 128:] = feat.astype(BF)

def bias_setup(tab_ref, bias):
    row_in = lax.broadcasted_iota(jnp.int32, (TS, 128), 0)
    lane_in = lax.broadcasted_iota(jnp.int32, (TS, 128), 1)
    for block in range(12):
        dist = 1024 - block * TS + lane_in - row_in
        if block in (7, 8):
            value = jnp.broadcast_to(tab_ref[0:1, 0:1], (TS, 128))
            for bucket, edge in enumerate(EDGES):
                b = bucket + 1
                value = jnp.where(dist >= edge, tab_ref[b // 4 : b // 4 + 1, b % 4 : b % 4 + 1], value)
        else:
            value = jnp.broadcast_to(tab_ref[7:8, 3:4], (TS, 128))
        value = jnp.where((dist >= 0) & (dist < WINDOW), value, MASKED)
        bias[block * TS : (block + 1) * TS, :128] = value
        bias[block * TS : (block + 1) * TS, 128:] = value


def eye(size):
    return (
        lax.broadcasted_iota(jnp.int32, (size, size), 0)
        == lax.broadcasted_iota(jnp.int32, (size, size), 1)
    ).astype(BF)


def strips(strip, after):
    def run(low, count):
        def body(at, carry):
            i = low + at
            strip(i + 8, 9, i)
            strip(i, count, 0)
            after(i)
            return carry

        lax.fori_loop(0, 4, body, 0)

    run(0, 4)
    run(4, 8)


def span(block, count):
    return pl.ds(pl.multiple_of(block * TS, TS), count * TS)


def attn_fwd_part(len_ref, recv_ref, land_ref, lse_ref, kext, qext, bias, vt, out_ref, sems):
    trade = Exchange(out_ref, land_ref, sems[0], sems[1])
    attn_setup(len_ref, recv_ref, kext, qext)
    unit = eye(TS)
    for i in range(EXPERTS):
        vt[:, i * TS : (i + 1) * TS] = nt(unit, recv_ref[i, 2 * TS : 3 * TS, :]).astype(BF)

    def strip(i, count, first):
        s = nt(kext[span(first, count), :], qext[i]) + bias[span(first - i + 8, count), :]
        top = jnp.max(s, axis=0, keepdims=True)
        p = jnp.exp(s - top)
        total = jnp.sum(p, axis=0, keepdims=True)
        res = nn(vt[:, span(first, count)], p.astype(BF)) / total
        both = jnp.concatenate([res[:HD, :TS], res[HD:, TS:]], axis=0)
        out_ref[i] = both.T.astype(BF)
        lse_ref[i] = jnp.broadcast_to(top + jnp.log(total), (8, TOK))

    def after(i):
        trade.push(i + 8)
        trade.push(i)

    strips(strip, after)
    return trade


def head_kernel(
    len_ref, x_ref, wq_ref, wk_ref, wv_ref, wo_ref, small_ref, place_ref, dy_ref,
    normed_ref, heads_ref, dy_land, wq_out, wk_out, wv_out, wo_out, wr_out, gain_out, tab_out, att_land, lse_ref,
    box, head_hold, dy_hold, kext, qext, bias, vt, att_hold, send_sem, recv_sem, *sems,
):
    copies, trade, early, late = gather_part(
        Place(), x_ref, wq_ref, wk_ref, wv_ref, wo_ref, small_ref, place_ref, dy_ref,
        normed_ref, heads_ref, dy_land, wq_out, wk_out, wv_out, wr_out, gain_out, tab_out,
        box, head_hold, dy_hold, send_sem, recv_sem, sems[0:4],
    )
    bias_setup(tab_out, bias)
    trade.arrive()
    for part in late:
        part.arrive(2, forward=True)
    back = attn_fwd_part(len_ref, heads_ref, att_land, lse_ref, kext, qext, bias, vt, att_hold, sems[4:6])
    for part in late:
        part.finish()
    unfold(box, OUT, wo_out)
    for sent in (back, early):
        sent.arrive()
    for sent in (trade, back, early):
        sent.drain()
    copies.drain()


def attn_bwd_part(
    len_ref, tab_ref, recv_ref, dout_ref, lse_ref, land_ref, tab_out_ref,
    kext, qext, bias, ktext, dk, dv, near, far, out_ref, sems, ready, meanwhile,
):
    trade_q = Exchange(out_ref, land_ref, sems[0], sems[1], pl.ds(0, TS))
    trade_kv = Exchange(out_ref, land_ref, sems[2], sems[3], pl.ds(TS, 2 * TS))
    attn_setup(len_ref, recv_ref, kext, qext)
    bias_setup(tab_ref, bias)
    unit = eye(256)
    for i in range(EXPERTS):
        ktext[:, i * TS : (i + 1) * TS] = nt(unit, kext[i * TS : (i + 1) * TS, :])[:144].astype(BF)
    dk[...] = jnp.zeros_like(dk)
    dv[...] = jnp.zeros_like(dv)
    near[...] = jnp.zeros_like(near)
    far[...] = jnp.zeros_like(far)
    left = lane_half((TS, 128))

    def strip(i, count, first):
        q = qext[i]
        s = nt(kext[span(first, count), :], q) + bias[span(first - i + 8, count), :]
        p = jnp.exp(s - lse_ref[i][0:1])
        do2 = dout_ref[i]
        zero = jnp.zeros_like(do2)
        do = jnp.concatenate([jnp.where(left, do2, zero), jnp.where(left, zero, do2)], axis=0)
        if count == 9:
            v = recv_ref[pl.ds(first, count), 2 * TS : 3 * TS, :].reshape(count * TS, 128)
        else:
            v = recv_ref[0:count, 2 * TS : 3 * TS, :].reshape(count * TS, 128)
        dp = nt(v, do)
        inner = jnp.sum(p * dp, axis=0, keepdims=True)
        ds = (p * (dp - inner)).astype(BF)
        dv[span(first, count), :] += nn(p.astype(BF), do)
        dk[span(first, count), :] += nn(ds, q[:, :128])
        dqt = nn(ktext[:, span(first, count)], ds)
        both = jnp.concatenate([dqt[:HD, :TS], dqt[HD : 2 * HD, TS:]], axis=0) * (HD**-0.5)
        out_ref[i, 0:TS, :] = both.T.astype(BF)
        far[...] += dqt[128:136]
        if count == 9:
            near[...] += ds[7 * TS :].astype(F32)
        else:
            for block in range(count):
                value = ds[block * TS : (block + 1) * TS].astype(F32)
                near[TS:] += value * (i == block).astype(F32)
                near[:TS] += value * (i == block + 1).astype(F32)

    def finish(i):
        out_ref[i, TS : 2 * TS, :] = dk[span(i, 1), :].astype(BF)
        out_ref[i, 2 * TS :, :] = dv[span(i, 1), :].astype(BF)
        trade_kv.push(i)

    ready()

    odd = lax.rem(trade_kv.me, 2)

    def first_half(low, count):
        def body(at, carry):
            i = low + 2 * at
            strip(i, count, 0)
            strip(i + 1, count, 0)
            trade_q.push(i)
            trade_q.push(i + 1)
            return carry

        lax.fori_loop(0, 2, body, 0)

    first_half(0, 4)
    first_half(4, 8)

    def second_half(at, carry):
        blocks = [odd * (8 + step) + (1 - odd) * (15 - step) for step in (2 * at, 2 * at + 1)]
        for i in blocks:
            strip(i, 9, i - 8)
        for i in blocks:
            trade_q.push(i)
            finish(i - 8 * odd)
        return carry

    lax.fori_loop(0, 4, second_half, 0)

    def rest(step, carry):
        finish(lax.rem(step + lax.div(trade_kv.me, 2), 8) + 8 * odd)
        return carry

    lax.fori_loop(0, 8, rest, 0)
    grads = near[:, :TS] + near[:, TS:]
    dist = (
        TS
        + lax.broadcasted_iota(jnp.int32, (TOK, TS), 1)
        - lax.broadcasted_iota(jnp.int32, (TOK, TS), 0)
    )
    total = jnp.sum(far[4:5, :])
    lane = lax.broadcasted_iota(jnp.int32, (8, 128), 1)
    lane = jnp.where(lane < 4, lane + 4 * lax.broadcasted_iota(jnp.int32, (8, 128), 0), NB)
    res = jnp.zeros((8, 128), F32)
    lows = (0,) + EDGES
    seen = 0.0
    for b in range(NB - 1):
        part = jnp.sum(jnp.where((dist >= lows[b]) & (dist < lows[b + 1]), grads, 0.0))
        seen = seen + part
        res = jnp.where(lane == b, part, res)
    res = jnp.where(lane == NB - 1, total - seen, res)
    tab_out_ref[...] = res
    meanwhile()
    for trade in (trade_q, trade_kv):
        trade.arrive()
    return trade_q, trade_kv


def row_expert():
    row = lax.broadcasted_iota(jnp.int32, (BUF, 128), 0)
    lane = lax.broadcasted_iota(jnp.int32, (BUF, 128), 1) * (2 * CAP)
    return (row >= lane) & (row < lane + 2 * CAP)


def unpack_heads(recv_ref, lo, emit):
    for pair in range(H // 2):
        one = recv_ref[2 * pair, lo : lo + TS, :].astype(F32)
        two = recv_ref[2 * pair + 1, lo : lo + TS, :].astype(F32)
        first, second = pack_pair(one, two)
        emit(pair, first, second)


def slot_share(place, share_e, own):
    high, low = halves(share_e)
    return jnp.sum(jnp.where(own, nn(place, high) + nn(place, low), 0.0), axis=1, keepdims=True)


CHUNKS = ((0, 768), (768, 768), (1536, 768), (2304, 512))


def pieces(at, size):
    found, row = [], at
    while row < at + size:
        end = min(at + size, (row // SHARD + 1) * SHARD)
        found.append((row // SHARD, row % SHARD, row - at, end - row))
        row = end
    return found


STAGED = 3 * sum(len(pieces(at, size)) for at, size in CHUNKS)


def moe_kernel(
    recv_ref, x_ref, wo_ref, gain_ref, wr_ref, mask_ref, place_ref, dy_ref, w_ref,
    att_ref, hidden_ref, mixed_ref, share_ref, back_out, back_row, grads_ref,
    w_buf, hold_a, hold_b, land_a, hold_s, land_s, rows, slots, act, first, second, acc, stage,
    w_sem, stage_sem, *sems,
):
    loads = [
        [
            pltpu.make_async_copy(
                w_ref.at[s, pl.ds(k * SHARD, SHARD)],
                w_buf.at[k, pl.ds(s * SHARD, SHARD)],
                w_sem.at[k * FSDP + s],
            )
            for s in range(FSDP)
        ]
        for k in range(3)
    ]
    for k in (2, 0, 1):
        for copy in loads[k]:
            copy.start()
    greet(plane_peers())
    to_rows = Exchange(hold_a, land_a, sems[0], sems[1])
    to_shares = Exchange(hold_s, land_s, sems[2], sems[3])
    from_out = Exchange(hold_a, back_out, sems[4], sems[5])
    from_row = Exchange(hold_b, back_row, sems[6], sems[7])

    def emit(pair, one, two):
        att_ref[0:TS, pair * 128 : pair * 128 + 128] = one
        att_ref[TS:, pair * 128 : pair * 128 + 128] = two

    unpack_heads(recv_ref, 0, emit)
    hidden = x_ref[...].astype(F32) + nn(att_ref[...], wo_ref[...])
    hidden_ref[...] = hidden
    factor = lax.rsqrt(jnp.mean(hidden * hidden, axis=-1, keepdims=True) + EPS)
    mixed = (hidden * factor * gain_ref[1:2, :]).astype(BF)
    mixed_ref[...] = mixed
    place = place_ref[...]
    hold_a[...] = spread(nn(place, mixed))
    to_rows.start()
    picked = mask_ref[...] > 0
    logits = jnp.where(picked, nn(mixed, wr_ref[...]), MASKED)
    weight = jnp.exp(logits - jnp.max(logits, axis=1, keepdims=True))
    share = weight / jnp.sum(weight, axis=1, keepdims=True)
    share_ref[...] = share
    high, low = halves(slot_share(place, share, row_expert()))
    lane = lax.broadcasted_iota(jnp.int32, (BUF, 128), 1)
    value = jnp.where(lane == 0, high.astype(F32), 0.0) + jnp.where(lane == 1, low.astype(F32), 0.0)
    value = value.reshape(EXPERTS, 2 * CAP, 128)
    hold_s[...] = jnp.concatenate([value, jnp.zeros((EXPERTS, 8, 128), F32)], axis=1).astype(BF)
    to_shares.start()

    unspread(slots, dy_ref)
    for copy in loads[2]:
        copy.wait()
    for at, size in CHUNKS:
        first[:, at : at + size] = nt(slots[...], w_buf[2, at : at + size, :]).astype(BF)
    for k in range(2):
        for copy in loads[k]:
            copy.wait()
    to_rows.arrive()
    unspread(rows, land_a)
    for at, size in CHUNKS:
        cols = slice(at, at + size)
        gate = nt(rows[...], w_buf[0, cols, :])
        up = nt(rows[...], w_buf[1, cols, :])
        square = gate * gate
        tanh = jnp.tanh(GELU_C * gate * (1.0 + 0.044715 * square))
        half_up = 0.5 * (1.0 + tanh)
        gelu = gate * half_up
        slope = half_up + 0.5 * gate * (1.0 - tanh * tanh) * (
            GELU_C * (1.0 + 3 * 0.044715 * square)
        )
        act_grad = first[:, cols].astype(F32)
        act[:, cols] = (gelu * up).astype(BF)
        first[:, cols] = (act_grad * up * slope).astype(BF)
        second[:, cols] = (act_grad * gelu).astype(BF)
    for half in range(2):
        cols = slice(half * HALF, half * HALF + HALF)
        acc[:, cols] = nn(act[...], w_buf[2, :, cols])
    to_rows.drain()
    hold_a[...] = spread(acc[...])
    from_out.start()
    for half in range(2):
        cols = slice(half * HALF, half * HALF + HALF)
        acc[:, cols] = nn(first[...], w_buf[0, :, cols]) + nn(second[...], w_buf[1, :, cols])
    hold_b[...] = spread(acc[...])
    from_row.start()

    to_shares.arrive()
    value = land_s[...].astype(F32)[:, : 2 * CAP, :].reshape(BUF, 128)
    scale = jnp.sum(value, axis=1, keepdims=True)
    rows[...] = (rows[...].astype(F32) * scale).astype(BF)
    slots[...] = (slots[...].astype(F32) * scale).astype(BF)
    pending = [[], [], []]
    count = turn = 0
    for which, (left, right) in ((2, (act, slots)), (0, (first, rows)), (1, (second, rows))):
        for at, size in CHUNKS:
            value = tn(left[:, at : at + size], right[...]).astype(BF)
            for copy in pending[turn]:
                copy.wait()
            stage[turn, :size, :] = value
            pending[turn] = []
            for shard, row, local, amount in pieces(at, size):
                copy = pltpu.make_async_copy(
                    stage.at[turn, pl.ds(local, amount)],
                    grads_ref.at[shard, pl.ds(which * SHARD + row, amount)],
                    stage_sem.at[count],
                )
                copy.start()
                pending[turn].append(copy)
                count += 1
            turn = (turn + 1) % 3
    for group in pending:
        for copy in group:
            copy.wait()
    from_out.arrive()
    from_row.arrive()
    from_out.drain()
    from_row.drain()
    to_shares.drain()


def back_part(
    out_ref, row_ref, place_ref, place_t_ref, dy_ref, hidden_ref, mixed_ref, share_ref, wr_ref, gain_ref, wo_ref,
    result_ref, hgrad_ref, branch_ref, land_ref, router_ref, gain_out_ref,
    send_ref, outs, rows, send_sem, recv_sem,
):
    z, y, _, _ = coords()
    trade = Exchange(send_ref, land_ref, send_sem, recv_sem)
    unspread(outs, out_ref)
    unspread(rows, row_ref)
    place = place_ref[...]
    place_t = place_t_ref[...]
    own = row_expert()
    dy = dy_ref[...]
    returned = outs[...]
    dots = jnp.sum(nn(place, dy) * returned.astype(F32), axis=1, keepdims=True)
    high, low = halves(jnp.where(own, dots, 0.0))
    share = share_ref[...]
    share_grad = nn(place_t, high) + nn(place_t, low)
    inner = jnp.sum(share * share_grad, axis=1, keepdims=True)
    lg_high, lg_low = halves(share * (share_grad - inner))
    wr = wr_ref[...]
    scale_high, scale_low = halves(
        place_t.astype(F32) * slot_share(place, share, own).T
    )
    mixed_grad = (nn(scale_high, rows[...]) + nn(scale_low, rows[...])) + (
        nt(lg_high, wr) + nt(lg_low, wr)
    )
    hidden = hidden_ref[...]
    factor = lax.rsqrt(jnp.mean(hidden * hidden, axis=-1, keepdims=True) + EPS)
    unit = hidden * factor
    gain_out_ref[...] = jnp.broadcast_to(jnp.sum(mixed_grad * unit, axis=0, keepdims=True), (8, D))
    scaled = mixed_grad * gain_ref[1:2, :]
    hgrad = dy.astype(F32) + factor * (
        scaled - unit * jnp.mean(scaled * unit, axis=-1, keepdims=True)
    )
    hgrad_ref[...] = hgrad
    branch = hgrad.astype(BF)
    branch_ref[...] = branch
    for k in (1, 2, 3, 0):
        part = ring(z, k)
        res = nt(branch, wo_ref[pl.ds(pl.multiple_of(part * 256, 256), 256), :])
        for pair in range(2):
            head = part * 4 + pair * 2
            cols = slice(pair * 128, pair * 128 + 128)
            one, two = pack_pair(res[:TS, cols], res[TS:, cols])
            send_ref[head] = one
            send_ref[head + 1] = two
        for j in (1, 2, 3, 0):
            if k or j:
                trade.copy(part * 4 + ring(y, j)).start()
            else:
                trade.keep()
    mixed = mixed_ref[...]
    router_ref[...] = tn(mixed, lg_high) + tn(mixed, lg_low)
    moe = nn(scale_high, returned) + nn(scale_low, returned)
    result_ref[...] = (hidden + moe).astype(BF)
    return trade


def final_part(
    place, copies, recv_ref, normed_ref, x_ref, gains_ref, hgrad_ref, wq_ref, wk_ref, wv_ref,
    router_ref, moe_gain_ref, table_ref, igrad_ref, sum_ref,
    flat_q, flat_k, flat_v, box, from_twin, rest,
):
    z, y, c = place.z, place.y, place.c
    parts = [
        Reduce(
            place, copies, order, (from_twin, lanes),
            [(bufs[0], pl.ds(0, lanes.size)), (bufs[1], pl.ds(0, lanes.size))], bufs[2:],
        )
        for (lanes, order), bufs in zip(REDUCE_PARTS, (rest[0:5], rest[5:10], rest[10:15], rest[15:20]))
    ]
    flats = (flat_q, flat_k, flat_v)
    for which, flat in enumerate(flats):

        def emit(pair, first, second):
            flat[0:TS, pair * 128 : pair * 128 + 128] = first
            flat[TS:, pair * 128 : pair * 128 + 128] = second

        unpack_heads(recv_ref, which * TS, emit)

    planes = [ring(z, k) for k in (1, 2, 3, 0)]
    to_twin = []

    def pair_sum(k):
        plane = planes[k]
        to_twin[k].wait_recv()
        both = box[plane, :, :, c, :, MAIN].astype(F32) + from_twin[plane, :, :, :, MAIN].astype(F32)
        from_twin[plane, :, :, :, MAIN] = both.astype(BF)
        if k < 3:
            parts[0].send(0, k + 1)

    for k, plane in enumerate(planes):
        for which, flat in enumerate(flats):
            plane_grads(box, plane, which, normed_ref, flat)
        to_twin.append(
            copies.go(
                box.at[plane, :, :, 1 - c, :, MAIN], from_twin.at[plane, :, :, :, MAIN], place.twin
            )
        )
        if k:
            pair_sum(k - 1)
    pair_sum(3)
    parts[1].start(0)
    parts[2].start(0)

    total = nt(flat_q[...], wq_ref[...]) + nt(flat_k[...], wk_ref[...]) + nt(flat_v[...], wv_ref[...])
    tokens = x_ref[...].astype(F32)
    factor = lax.rsqrt(jnp.mean(tokens * tokens, axis=-1, keepdims=True) + EPS)
    unit = tokens * factor

    at = lax.broadcasted_iota(jnp.int32, (128, 8, 128), 1)
    gains = [by_device(row) for row in (jnp.sum(total * unit, axis=0, keepdims=True), moe_gain_ref[0:1, :])]
    lower = jnp.where(at == 0, gains[0][:, None, :], 0.0) + jnp.where(at == 1, gains[1][:, None, :], 0.0)
    extra = jnp.concatenate([router_ref[...].reshape(128, 8, 128), lower], axis=1)
    box[:, :, :, :, :, REST] = extra.astype(BF).reshape(4, 4, 4, 2, 16, 128)
    at = lax.broadcasted_iota(jnp.int32, (8, 16, 128), 1)
    here = box[z, y, :, :, :, REST].reshape(8, 16, 128).astype(F32)
    here = here + jnp.where(at == 10, table_ref[...][:, None, :], 0.0)
    box[z, y, :, :, :, REST] = here.astype(BF).reshape(4, 2, 16, 128)
    rest_copy = copies.go(
        box.at[:, :, :, 1 - c, :, REST], from_twin.at[:, :, :, :, REST], place.twin
    )
    rest_copy.wait_recv()
    both = box[:, :, :, c, :, REST].astype(F32) + from_twin[:, :, :, :, REST].astype(F32)
    from_twin[:, :, :, :, REST] = both.astype(BF)
    parts[3].start(0)
    scaled = total * gains_ref[0:1, :]
    igrad_ref[...] = (
        hgrad_ref[...]
        + factor * (scaled - unit * jnp.mean(scaled * unit, axis=-1, keepdims=True))
    ).astype(BF)
    for phase in range(2):
        for part in parts:
            part.total(phase)
            part.start(phase + 1)
    value = jnp.concatenate([part.total(2) for part in parts], axis=1)
    for which in range(4):
        sum_ref[which * 8 : which * 8 + 8, :] = unfolded(value[:, which * HALF : (which + 1) * HALF])
    sum_ref[32:48, 0:128] = value[:, 4 * HALF :]


def plane_grads(box, plane, which, left, right):
    cols = pl.ds(pl.multiple_of(plane * 256, 256), 256)
    value = fold_rows(tn(left[:, cols], right[...])).astype(BF)
    box[plane, :, :, :, :, which * HALF : (which + 1) * HALF] = value.reshape(4, 4, 2, 16, HALF)


def tail_kernel(
    len_ref, tab_ref, out_ref, row_ref, place_ref, place_t_ref, dy_ref, hidden_ref, mixed_ref, share_ref,
    wr_ref, gains_ref, wo_ref, heads_ref, lse_ref, normed_ref, x_ref, wq_ref, wk_ref, wv_ref, att_ref,
    result_ref, igrad_ref, sum_ref,
    hgrad, branch, head_grads, router, moe_gain, head_send, outs, rows,
    kext, qext, bias, ktext, dk, dv, near, far, grads_send, token_grads, table,
    flat_q, flat_k, flat_v, box, from_twin, *rest,
):
    place = Place()
    greet(plane_peers() + place.peers("x") + [place.twin])
    copies = Copies(rest[20], rest[21])
    sems = rest[22:]
    trade = back_part(
        out_ref, row_ref, place_ref, place_t_ref, dy_ref, hidden_ref, mixed_ref, share_ref, wr_ref, gains_ref,
        wo_ref, result_ref, hgrad, branch, head_grads, router, moe_gain, head_send, outs, rows, sems[0], sems[1],
    )

    def out_grads():
        for plane in range(4):
            plane_grads(box, plane, 3, att_ref, branch)

    trades = attn_bwd_part(
        len_ref, tab_ref, heads_ref, head_grads, lse_ref, token_grads, table,
        kext, qext, bias, ktext, dk, dv, near, far, grads_send, sems[2:6], trade.arrive, out_grads,
    )
    final_part(
        place, copies, token_grads, normed_ref, x_ref, gains_ref, hgrad, wq_ref, wk_ref, wv_ref,
        router, moe_gain, table, igrad_ref, sum_ref, flat_q, flat_k, flat_v, box, from_twin, rest,
    )
    for sent in (trade,) + trades:
        sent.drain()
    copies.drain()


def emit_kernel(expert_ref, sum_ref, gate, up, down, gq, gk, gv, go, router, gain_attn, gain_moe, table):
    for k, ref in enumerate((gate, up, down)):
        ref[...] = expert_ref[k].astype(F32)
    for k, ref in enumerate((gq, gk, gv, go)):
        ref[...] = sum_ref[k * 8 : k * 8 + 8, :]
    router[...] = sum_ref[32:40, :EXPERTS]
    gain_attn[...] = sum_ref[40:41, :8]
    gain_moe[...] = sum_ref[41:42, :8]
    table[...] = sum_ref[42:43, :4]


def placement(routes, order):
    micro = routes.shape[0]
    slots = routes.reshape(micro, 2 * TS)
    rank_of = order.reshape(micro, 2 * TS)
    same = slots[:, :, None] == slots[:, None, :]
    earlier = rank_of[:, None, :] < rank_of[:, :, None]
    rank = jnp.sum((same & earlier).astype(jnp.int32), axis=2)
    base = slots * (2 * CAP) + jnp.arange(micro, dtype=jnp.int32)[:, None] * CAP
    target = jnp.where(rank < CAP, base + rank, BUF).reshape(micro * TS, 2)
    rows = jnp.arange(BUF, dtype=jnp.int32)
    place = (rows[:, None] == target[None, :, 0]) | (rows[:, None] == target[None, :, 1])
    place_t = (rows[None, :] == target[:, 0:1]) | (rows[None, :] == target[:, 1:2])
    return place.astype(BF), place_t.astype(BF)


def on_device(
    tokens, cotangent, doc_lengths, routes, order, gain_attn, w_query, w_key, w_value, w_out,
    rel_table, gain_moe, w_router, w_gate, w_up, w_down,
):
    expert_shard = jnp.concatenate([w_gate[0].T, w_up[0].T, w_down[0]], axis=0)
    expert_w = lax.all_gather(expert_shard, "fsdp", axis=0, tiled=False)

    def padded(value):
        return jnp.pad(value, ((0, 0), (0, 128 - value.shape[1])))

    small = jnp.concatenate(
        [padded(v) for v in (w_router, gain_attn[None], gain_moe[None], rel_table[None])]
        + [jnp.zeros((5, 128), BF)],
        axis=0,
    )
    place, place_t = placement(routes[:, 0], order[:, 0, 0])
    lanes = jnp.arange(128, dtype=jnp.int32)
    route_rows = routes.reshape(TOK, 2)
    picked = (
        (route_rows[:, 0:1] == lanes) | (route_rows[:, 1:2] == lanes)
    ).astype(F32)
    x = tokens.reshape(TOK, D)
    dy = cotangent.reshape(TOK, D)
    lengths = doc_lengths[:, 0]

    chunk = (EXPERTS, 4 * CAP, HALF)
    chunk = (EXPERTS, 4 * CAP, HALF)
    smem = pl.BlockSpec(memory_space=pltpu.SMEM)
    vmem = pl.BlockSpec(memory_space=pltpu.VMEM)
    attn_scratch = [
        pltpu.VMEM((SEQ, 256), BF), pltpu.VMEM((EXPERTS, TOK, 256), BF), pltpu.VMEM((12 * TS, TOK), F32),
    ]
    matrix = shape((D, D), BF)
    normed, heads, dy_rows, wq, wk, wv, wo, wr, gains, table, att_back, lse = call(
        head_kernel,
        (
            shape((TOK, D), BF), shape((H, 3 * TS, 128), BF), shape(chunk, BF), matrix, matrix, matrix, matrix,
            shape((D, 128), BF), shape((8, D), F32), shape((8, 128), F32),
            shape((EXPERTS, TS, 128), BF), shape((EXPERTS, 8, TOK), F32),
        ),
        lengths, x, w_query, w_key, w_value, w_out, small, place, dy,
        in_specs=[smem] + [vmem] * 8,
        scratch=[
            pltpu.VMEM((4, 4, 4, 2, 16, WIDE), BF), pltpu.VMEM((H, 3 * TS, 128), BF), pltpu.VMEM(chunk, BF),
        ]
        + attn_scratch
        + [pltpu.VMEM((128, SEQ), BF), pltpu.VMEM((EXPERTS, TS, 128), BF)]
        + [pltpu.SemaphoreType.DMA((78,))] * 2
        + [pltpu.SemaphoreType.DMA((EXPERTS,))] * 6,
        collective_id=1,
    )
    anywhere = pl.BlockSpec(memory_space=pl.ANY)
    att, hidden, mixed, share, outs, row_grads, expert_grads = call(
        moe_kernel,
        (
            shape((TOK, D), BF), shape((TOK, D), F32), shape((TOK, D), BF), shape((TOK, 128), F32),
            shape(chunk, BF), shape(chunk, BF), shape((FSDP, 3 * SHARD, D), BF),
        ),
        att_back, x, wo, gains, wr, picked, place, dy_rows, expert_w,
        in_specs=[vmem] * 8 + [anywhere],
        out_specs=(vmem,) * 6 + (anywhere,),
        scratch=[
            pltpu.VMEM((3, FF, D), BF),
            pltpu.VMEM(chunk, BF), pltpu.VMEM(chunk, BF), pltpu.VMEM(chunk, BF),
            pltpu.VMEM((EXPERTS, 48, 128), BF), pltpu.VMEM((EXPERTS, 48, 128), BF),
            pltpu.VMEM((BUF, D), BF), pltpu.VMEM((BUF, D), BF),
            pltpu.VMEM((BUF, FF), BF), pltpu.VMEM((BUF, FF), BF), pltpu.VMEM((BUF, FF), BF),
            pltpu.VMEM((BUF, D), F32),
            pltpu.VMEM((3, 768, D), BF),
            pltpu.SemaphoreType.DMA((3 * FSDP,)), pltpu.SemaphoreType.DMA((STAGED,)),
        ]
        + [pltpu.SemaphoreType.DMA((EXPERTS,))] * 8,
        collective_id=3,
    )
    expert_sum = lax.psum_scatter(
        expert_grads.reshape(FSDP * 3 * SHARD, D), "fsdp", scatter_dimension=0, tiled=True
    )
    result, input_grad, sums = call(
        tail_kernel,
        (shape((TOK, D), BF), shape((TOK, D), BF), shape((48, D), F32)),
        lengths, table, outs, row_grads, place, place_t, dy, hidden, mixed, share, wr, gains, wo,
        heads, lse, normed, x, wq, wk, wv, att,
        in_specs=[smem] + [vmem] * 20,
        scratch=[
            pltpu.VMEM((TOK, D), F32), pltpu.VMEM((TOK, D), BF), pltpu.VMEM((H, TS, 128), BF),
            pltpu.VMEM((D, 128), F32), pltpu.VMEM((8, D), F32), pltpu.VMEM((H, TS, 128), BF),
            pltpu.VMEM((BUF, D), BF), pltpu.VMEM((BUF, D), BF),
        ]
        + attn_scratch
        + [
            pltpu.VMEM((144, SEQ), BF), pltpu.VMEM((SEQ, 128), F32), pltpu.VMEM((SEQ, 128), F32),
            pltpu.VMEM((2 * TS, TOK), F32), pltpu.VMEM((8, TOK), F32),
            pltpu.VMEM((EXPERTS, 3 * TS, 128), BF), pltpu.VMEM((EXPERTS, 3 * TS, 128), BF),
            pltpu.VMEM((8, 128), F32),
            pltpu.VMEM((TOK, D), BF), pltpu.VMEM((TOK, D), BF), pltpu.VMEM((TOK, D), BF),
            pltpu.VMEM((4, 4, 4, 2, 16, WIDE), BF),
            pltpu.VMEM((4, 4, 4, 16, WIDE), BF),
        ]
        + [buf for lanes, _ in REDUCE_PARTS for buf in reduce_scratch(lanes.size)]
        + [pltpu.SemaphoreType.DMA((41,))] * 2
        + [pltpu.SemaphoreType.DMA((EXPERTS,))] * 6,
        collective_id=2,
    )
    block = shape((SHARD, D), F32)
    rows = shape((8, D), F32)
    small_shapes = (rows, rows, rows, rows) + tuple(
        shape(dims, F32) for dims in ((8, EXPERTS), (1, 8), (1, 8), (1, 4))
    )
    part = SHARD // 2
    gate, up, down, gq, gk, gv, go, router, gain_a, gain_m, table_sum = pl.pallas_call(
        emit_kernel,
        grid=(2,),
        out_shape=(block, block, block) + small_shapes,
        in_specs=[pl.BlockSpec((3, part, D), lambda i: (0, i, 0)), pl.BlockSpec((48, D), lambda i: (0, 0))],
        out_specs=(pl.BlockSpec((part, D), lambda i: (i, 0)),) * 3
        + tuple(pl.BlockSpec(small_shape.shape, lambda i: (0, 0)) for small_shape in small_shapes),
        compiler_params=pltpu.CompilerParams(vmem_limit_bytes=VMEM_LIMIT),
    )(expert_sum.reshape(3, SHARD, D), sums)
    return (
        result.reshape(tokens.shape), input_grad.reshape(tokens.shape), gain_a[0], gq, gk, gv, go,
        table_sum[0], gain_m[0], router, gate.T[None], up.T[None], down[None],
    )


def solution(mesh):
    row = P(None, "fsdp", "expert", None)
    flat = P(("expert", "fsdp"))
    matrix = P(("expert", "fsdp"), None)
    columns = P("expert", None, "fsdp")
    deep = P("expert", "fsdp", None)
    return jax.shard_map(
        on_device,
        mesh=mesh,
        in_specs=(
            row, row, P(None, "fsdp", None), row, row, flat, matrix, matrix, matrix, matrix,
            flat, flat, matrix, columns, columns, deep,
        ),
        out_specs=(
            row, row, flat, matrix, matrix, matrix, matrix, flat, flat, matrix, columns, columns, deep,
        ),
        check_vma=False,
    )
```
